128 devices in a mesh: fx: 8 (over x, core), fy: 16 (over y, z).
Axes of the slice: x: 4, y: 4, z: 4, core: 2. Of those that a mesh axis runs over, the one named last changes fastest.
Arguments:
- ll_blocks: bfloat16 [8192, 8192], P(('fx', 'fy')), may hold values from -6 to 6
- dest_dev: int32 [8192, 2], P(('fx', 'fy')), may hold values from 0 to 127, as said below
- dest_pos: int32 [8192, 2], P(('fx', 'fy')), may hold values from 0 to 63, as said below
- fwd_id: int32 [8192, 2], P(('fx', 'fy')), may hold values from 0 to 63
- back_id: int32 [8192, 2], P(('fx', 'fy')), may hold values from 0 to 63
- fwd_table: bfloat16 [64, 128, 128], replicated, may hold values from -0.5 to 0.5
- back_table: bfloat16 [64, 128, 128], replicated, may hold values from -0.5 to 0.5
- kernel_one: bfloat16 [3, 3, 64, 64], replicated, may hold values from -0.25 to 0.25
- bias_one: float32 [64], replicated, may hold values from -3 to 3
- kernel_two: bfloat16 [3, 3, 64, 64], replicated, may hold values from -0.25 to 0.25
- bias_two: float32 [64], replicated, may hold values from -3 to 3
Outputs:
- ll_out: bfloat16 [8192, 8192], P(('fx', 'fy'))
The draws below stay inside these ranges and needn't reach their ends.
Inputs may be any that keep to these rules, and one draw needn't show every extreme that they name: `dest_dev`: among the rows of one device no device is named more than 2 times, and that many is reached; each device is named in route 0 by exactly 64 rows; a row's two routes may name the same device. `dest_pos`: the route-0 rows that name a device name each of its 64 blocks exactly once.
All inputs are finite; a program needn't handle non-finite values.
Results may differ from the reference program's by a relative error of at most 0.015.
Values may be sent and summed in bfloat16 or wider, within the bound.
No kernel may reach another device: no remote copies, remote signals or barrier semaphores. Data moves between devices by JAX's collectives and lax.ppermute only.
A program may use at most 128 MiB of HBM per device.

```python
import math
import jax
import jax.numpy as jnp
from jax import lax

C = 64
SEG = 128
NW = 64
TOP = 2
TR = 64
TC = 128
HBLK_DEV = 64
BLK_DEV = 64
EXTRA = 1
NBLK = 8192
NROWS = 512
NCOLS = 2048
N_FX = 8
N_FY = 16


def routing(key):
    devices = N_FX * N_FY
    order_key, local_key, busy_key, pick_key, spot_key = jax.random.split(key, 5)
    owners = jax.random.permutation(order_key, devices).astype(jnp.int32)
    within = jax.random.permutation(local_key, BLK_DEV).astype(jnp.int32)
    busy_count = (BLK_DEV + EXTRA - 1) // EXTRA
    busy = jax.random.permutation(busy_key, devices).astype(jnp.int32)[:busy_count]
    picks = jax.random.permutation(pick_key, BLK_DEV).astype(jnp.int32) // EXTRA
    second = busy[picks]
    sender = jnp.arange(devices, dtype=jnp.int32)[:, None]
    first_dev = owners[(sender + within[None, :]) % devices]
    second_dev = owners[jnp.broadcast_to(second[None, :], (devices, BLK_DEV))]
    first_pos = jnp.broadcast_to(within[None, :], (devices, BLK_DEV))
    second_pos = jax.random.randint(spot_key, (devices, BLK_DEV), 0, HBLK_DEV).astype(jnp.int32)
    dev_all = jnp.stack([first_dev, second_dev], axis=-1).reshape(NBLK, TOP)
    pos_all = jnp.stack([first_pos, second_pos], axis=-1).reshape(NBLK, TOP)
    return (dev_all.astype(jnp.int32), pos_all.astype(jnp.int32))


def draw_dest_dev(key, part):
    return routing(key)[0]


def draw_dest_pos(key, part):
    return routing(key)[1]


def with_ends(values, own_key, smallest, top_value):
    longest = values.shape.index(max(values.shape))
    spots = []
    for shift in (0, 1):
        where = [jax.random.randint(jax.random.fold_in(own_key, axis), (), 0, length) for axis, length in enumerate(values.shape)]
        where[longest] = (where[longest] + shift) % values.shape[longest]
        spots.append(tuple(where))
    return values.at[spots[0]].set(smallest).at[spots[1]].set(top_value)


def steps_of(rng, dims, shards, low, largest):
    gain = 1.0
    for dim, shards_of in shards:
        draws = jax.random.uniform(jax.random.fold_in(jax.random.fold_in(rng, 6), dim), (shards_of,), jnp.float32, low / len(shards), largest / len(shards))
        gain = gain * jnp.repeat(jnp.exp(draws), dims[dim] // shards_of).reshape((-1,) + (1,) * (len(dims) - 1 - dim))
    return gain


def bell_draw(own_key, dims, scale, limit, shards=(), kind=jnp.bfloat16):
    level = steps_of(own_key, dims, shards, -0.22, 0.18) if shards else 1.0
    array = jax.random.normal(own_key, dims, jnp.float32) * scale * level
    return jnp.minimum(jnp.maximum(array, -limit), limit).astype(kind)


def setup_inputs(seed: int = 0) -> dict:
    arg_keys = jax.random.split(jax.random.key(seed), 12)
    return {
        "ll_blocks": bell_draw(arg_keys[0], (NBLK, C * SEG), 1.0, 6.0, ((0, 128),)),
        "dest_dev": draw_dest_dev(jax.random.fold_in(arg_keys[11], 71), 0),
        "dest_pos": draw_dest_pos(jax.random.fold_in(arg_keys[11], 71), 0),
        "fwd_id": with_ends(jax.random.randint(arg_keys[3], (NBLK, TOP), 0, NW), jax.random.fold_in(arg_keys[3], 1), 0, NW - 1).astype(jnp.int32),
        "back_id": with_ends(jax.random.randint(arg_keys[4], (NBLK, TOP), 0, NW), jax.random.fold_in(arg_keys[4], 1), 0, NW - 1).astype(jnp.int32),
        "fwd_table": bell_draw(arg_keys[5], (NW, SEG, SEG), SEG ** -0.5, 0.5),
        "back_table": bell_draw(arg_keys[6], (NW, SEG, SEG), SEG ** -0.5, 0.5),
        "kernel_one": bell_draw(arg_keys[7], (3, 3, C, C), (9 * C) ** -0.5, 0.25),
        "bias_one": bell_draw(arg_keys[8], (C,), 0.5, 3.0, (), jnp.float32),
        "kernel_two": bell_draw(arg_keys[9], (3, 3, C, C), (9 * C) ** -0.5, 0.25),
        "bias_two": bell_draw(arg_keys[10], (C,), 0.5, 3.0, (), jnp.float32),
    }


def apply_blocks(table, ids, blocks):
    count = blocks.shape[0]
    weights = table[ids].astype(jnp.float32)
    shaped = blocks.reshape(count, C, SEG).astype(jnp.float32)
    product = jnp.einsum("gij,gcj->gci", weights, shaped)
    return product.astype(jnp.bfloat16).reshape(count, C * SEG)


def convolve(field, kernel, bias):
    rows = jnp.concatenate([field[-1:], field, field[:1]], axis=0)
    padded = jnp.pad(rows, ((0, 0), (1, 1), (0, 0)))
    out = lax.conv_general_dilated(padded[None], kernel, (1, 1), "VALID", dimension_numbers=("NHWC", "HWIO", "NHWC"), preferred_element_type=jnp.float32)[0]
    return out + bias.astype(jnp.float32)


def reference(ll_blocks, dest_dev, dest_pos, fwd_id, back_id, fwd_table, back_table, kernel_one, bias_one, kernel_two, bias_two):
    devices = N_FX * N_FY
    total = ll_blocks.shape[0]
    routes_all = total * TOP
    group = math.gcd(routes_all, 512)
    source = jnp.repeat(jnp.arange(total, dtype=jnp.int32), TOP)
    target = (dest_dev * HBLK_DEV + dest_pos).reshape(-1).astype(jnp.int32)
    fwd_flat = fwd_id.reshape(-1)
    back_flat = back_id.reshape(-1)
    starts = jnp.arange(0, routes_all, group, dtype=jnp.int32)

    def forward(carry, start):
        rows = lax.dynamic_slice_in_dim(source, start, group)
        ids = lax.dynamic_slice_in_dim(fwd_flat, start, group)
        where = lax.dynamic_slice_in_dim(target, start, group)
        contrib = apply_blocks(fwd_table, ids, ll_blocks[rows]).astype(jnp.float32)
        return carry.at[where].add(contrib), None

    accum, _ = lax.scan(forward, jnp.zeros((devices * HBLK_DEV, C * SEG), jnp.float32), starts)
    field = accum.astype(jnp.bfloat16).reshape(N_FX, N_FY, TR, C, TC).transpose(0, 2, 1, 4, 3).reshape(NROWS, NCOLS, C)
    hidden = jax.nn.gelu(convolve(field, kernel_one, bias_one)).astype(jnp.bfloat16)
    state = (convolve(hidden, kernel_two, bias_two) + field.astype(jnp.float32)).astype(jnp.bfloat16)
    tiles = state.reshape(N_FX, TR, N_FY, TC, C).transpose(0, 2, 1, 4, 3).reshape(devices * HBLK_DEV, C * SEG)

    def backward(carry, start):
        rows = lax.dynamic_slice_in_dim(source, start, group)
        ids = lax.dynamic_slice_in_dim(back_flat, start, group)
        where = lax.dynamic_slice_in_dim(target, start, group)
        partial_value = apply_blocks(back_table, ids, tiles[where]).astype(jnp.float32)
        return carry.at[rows].add(partial_value), None

    result, _ = lax.scan(backward, jnp.zeros((total, C * SEG), jnp.float32), starts)
    return result.astype(jnp.bfloat16)
```

```python
import jax
import jax.numpy as jnp
from jax import lax
from jax.experimental import pallas as pl
from jax.experimental.pallas import tpu as pltpu
from jax.sharding import PartitionSpec as P

CAP = 2
AXES = ("fx", "fy")
F32 = jnp.float32
BF16 = jnp.bfloat16
VMEM_LIMIT = 48 * 1024 * 1024

META = 8
NT = (((1,), (1,)), ((), ()))


def code_of(dev, pos, fwd, back):
    return ((dev * 64 + pos) * 64 + fwd) * 64 + back


def code_dev(code):
    return lax.shift_right_logical(code, 18)


def code_pos(code):
    return lax.shift_right_logical(code, 12) & 63


def code_fwd(code):
    return lax.shift_right_logical(code, 6) & 63


def code_back(code):
    return code & 63


def smem():
    return pl.BlockSpec(memory_space=pltpu.SMEM)


def vmem():
    return pl.BlockSpec(memory_space=pltpu.VMEM)


def forward_kernel(code_ref, x_ref, table_ref, send_ref, slot_ref, rows_ref, count_ref, pos_ref):
    blocks, width = x_ref.shape
    seg = table_ref.shape[1]
    chans = width // seg
    devices = count_ref.shape[0]

    def clear(d, carry):
        count_ref[d] = 0
        pos_ref[CAP * d] = -1
        pos_ref[CAP * d + 1] = -1
        return carry

    lax.fori_loop(0, devices, clear, 0, unroll=4)
    for c in range(chans):
        rows_ref[c * blocks : (c + 1) * blocks, :] = x_ref[:, c * seg : (c + 1) * seg].astype(F32)

    def one_block(b, carry):
        codes = [code_ref[b, t] for t in range(2)]
        x = rows_ref[pl.ds(b, chans, stride=blocks), :].astype(BF16)
        weights = jnp.concatenate([table_ref[code_fwd(code)] for code in codes], axis=0)
        product = lax.dot_general(x, weights, NT, preferred_element_type=F32)
        for t, code in enumerate(codes):
            dev = code_dev(code)
            rank = count_ref[dev]
            count_ref[dev] = rank + 1
            slot_ref[b, t] = dev * CAP + rank
            pos_ref[dev * CAP + rank] = code_pos(code)
            at = pl.multiple_of(rank * chans, chans)
            send_ref[dev, pl.ds(at, chans), :] = product[:, t * seg : (t + 1) * seg].astype(BF16)
        return carry

    lax.fori_loop(0, blocks, one_block, 0, unroll=4)
    half = lax.broadcasted_iota(jnp.int32, (META, seg), 0) < META // 2

    def positions(d, carry):
        both = jnp.where(half, pos_ref[CAP * d], pos_ref[CAP * d + 1])
        send_ref[d, CAP * chans :, :] = both.astype(F32).astype(BF16)
        return carry

    lax.fori_loop(0, devices, positions, 0, unroll=4)


def forward_remap(codes, ll_blocks, fwd_table, devices):
    blocks, width = ll_blocks.shape
    seg = fwd_table.shape[1]
    chans = width // seg
    return pl.pallas_call(
        forward_kernel,
        out_shape=(
            jax.ShapeDtypeStruct((devices, CAP * chans + META, seg), BF16),
            jax.ShapeDtypeStruct((blocks, 2), jnp.int32),
        ),
        in_specs=[smem(), vmem(), vmem()],
        out_specs=(vmem(), smem()),
        scratch_shapes=[
            pltpu.VMEM((chans * blocks, seg), F32),
            pltpu.SMEM((devices,), jnp.int32),
            pltpu.SMEM((devices * CAP,), jnp.int32),
        ],
        compiler_params=pltpu.CompilerParams(vmem_limit_bytes=VMEM_LIMIT),
        cost_estimate=pl.CostEstimate(
            flops=4 * blocks * width * seg, bytes_accessed=8 << 20, transcendentals=0
        ),
    )(codes, ll_blocks, fwd_table)


def field_kernel(pos_ref, got_ref, field_ref, edge_left_ref, edge_right_ref, sum_ref, edge_ref):
    step = pl.program_id(0)
    part = got_ref.shape[0]
    pairs, cols, lanes = field_ref.shape
    chans = lanes // 2
    spare = 2 * pairs

    @pl.when(step == 0)
    def _():
        def clear(r, carry):
            sum_ref[r] = jnp.zeros(sum_ref.shape[1:], F32)
            return carry

        lax.fori_loop(0, spare, clear, 0, unroll=4)

    def add(n, carry):
        for rank in range(CAP):
            pos = pos_ref[step * part + n, rank]
            row = jnp.where(pos < 0, spare, pos)
            block = got_ref[n, rank * chans : (rank + 1) * chans, :]
            sum_ref[row] = sum_ref[row] + block.astype(F32)
        return carry

    lax.fori_loop(0, part, add, 0, unroll=4)

    @pl.when(step == pl.num_programs(0) - 1)
    def _():
        def one_pair(g, carry):
            both = sum_ref[pl.ds(2 * g, 2)].reshape(2 * chans, cols)
            turned = both.T
            field_ref[g] = turned.astype(BF16)
            for n, k in enumerate((0, 1, cols - 2, cols - 1)):
                edge_ref[pl.ds(n * pairs + g, 1), :] = turned[k : k + 1, :]
            return carry

        lax.fori_loop(0, pairs, one_pair, 0, unroll=2)
        edge_left_ref[...] = edge_ref[0 : 2 * pairs, :].astype(BF16)
        edge_right_ref[...] = edge_ref[2 * pairs : 4 * pairs, :].astype(BF16)


def sum_field(positions, got, hblocks):
    devices, depth, cols = got.shape
    chans = (depth - META) // CAP
    pairs = hblocks // 2
    parts = 8
    part = devices // parts
    return pl.pallas_call(
        field_kernel,
        grid=(parts,),
        out_shape=(
            jax.ShapeDtypeStruct((pairs, cols, 2 * chans), BF16),
            jax.ShapeDtypeStruct((2 * pairs, 2 * chans), BF16),
            jax.ShapeDtypeStruct((2 * pairs, 2 * chans), BF16),
        ),
        in_specs=[smem(), pl.BlockSpec((part, depth, cols), lambda s: (s, 0, 0))],
        out_specs=(vmem(), vmem(), vmem()),
        scratch_shapes=[
            pltpu.VMEM((hblocks + 1, chans, cols), F32),
            pltpu.VMEM((4 * pairs, 2 * chans), F32),
        ],
        compiler_params=pltpu.CompilerParams(vmem_limit_bytes=VMEM_LIMIT),
    )(positions, got)


def gelu(x):
    return 0.5 * x * (1.0 + jnp.tanh(0.7978845608028654 * (x + 0.044715 * (x * x * x))))


def conv_kernel(
    pos_ref,
    place_ref,
    field_ref,
    above_ref,
    below_ref,
    left_ref,
    right_ref,
    k1_ref,
    b1_ref,
    k2_ref,
    b2_ref,
    send_ref,
    ext_ref,
    hid_ref,
    side_ref,
    halo_ref,
    state_ref,
):
    pairs, cols, lanes = field_ref.shape
    chans = lanes // 2
    slots = send_ref.shape[0]
    groups = pairs + 1
    ext_ref[0] = above_ref[0:cols, :]
    ext_ref[pl.ds(1, pairs)] = field_ref[...]
    ext_ref[pairs + 1] = below_ref[0:cols, :]
    above = above_ref[cols:, :].astype(F32)
    below = below_ref[cols:, :].astype(F32)
    left = left_ref[...].astype(F32)
    right = right_ref[...].astype(F32)
    for n, (source, at) in enumerate(((left, 0), (left, 1), (right, 0), (right, 1))):
        k = (0, 1, 4, 5)[n]
        side_ref[k, 0:1, :] = above[n : n + 1, :]
        side_ref[k, 1 : pairs + 1, :] = source[at * pairs : (at + 1) * pairs, :]
        side_ref[k, pairs + 1 : pairs + 2, :] = below[n : n + 1, :]

    def inner_side(g, carry):
        block = ext_ref[g]
        side_ref[2, pl.ds(g, 1), :] = block[0:16, :].astype(F32)[0:1, :]
        side_ref[3, pl.ds(g, 1), :] = block[cols - 16 : cols, :].astype(F32)[15:16, :]
        return carry

    lax.fori_loop(0, pairs + 2, inner_side, 0, unroll=2)

    def paired(k):
        return jnp.concatenate(
            [side_ref[k, 0:groups, :], side_ref[k, 1 : groups + 1, :]], axis=1
        ).astype(BF16)

    def taps(x, weights_ref, d):
        return jnp.dot(
            x, weights_ref[:, d * lanes : (d + 1) * lanes], preferred_element_type=F32
        )

    b1 = b1_ref[...]
    b2 = b2_ref[...]
    c = [paired(k) for k in range(6)]
    halo_ref[0, 0:groups, :] = taps(c[1], k1_ref, 0)
    halo_ref[1, 0:groups, :] = taps(c[4], k1_ref, 2)
    before = taps(c[0], k1_ref, 0) + taps(c[1], k1_ref, 1) + taps(c[2], k1_ref, 2) + b1
    after = taps(c[3], k1_ref, 0) + taps(c[4], k1_ref, 1) + taps(c[5], k1_ref, 2) + b1
    before = jnp.where(place_ref[0] > 0, gelu(before), 0.0)
    after = jnp.where(place_ref[1] > 0, gelu(after), 0.0)
    for n, (column, d) in enumerate(((before, 0), (after, 2))):
        side_ref[n, 0:groups, :] = column
        both = jnp.concatenate(
            [side_ref[n, 0:pairs, :], side_ref[n, 1 : pairs + 1, :]], axis=1
        ).astype(BF16)
        halo_ref[2 + n, 0:pairs, :] = taps(both, k2_ref, d)

    column = lax.broadcasted_iota(jnp.int32, (cols, lanes), 0)

    def convolve(source_ref, g, weights_ref, bias, h):
        rows = jnp.concatenate([source_ref[g], source_ref[g + 1]], axis=1)
        product = jnp.dot(rows, weights_ref[...], preferred_element_type=F32)
        ahead = pltpu.roll(product[:, 0:lanes], 1, axis=0)
        behind = pltpu.roll(product[:, 2 * lanes :], cols - 1, axis=0)
        ahead = jnp.where(column == 0, halo_ref[h, pl.ds(g, 1), :], ahead)
        behind = jnp.where(column == cols - 1, halo_ref[h + 1, pl.ds(g, 1), :], behind)
        return product[:, lanes : 2 * lanes] + ahead + behind + bias

    def first(g, carry):
        hid_ref[g] = gelu(convolve(ext_ref, g, k1_ref, b1, 0)).astype(BF16)
        return carry

    lax.fori_loop(0, groups, first, 0, unroll=3)

    def second(g, carry):
        state = convolve(hid_ref, g, k2_ref, b2, 2) + ext_ref[g + 1].astype(F32)
        state_ref[pl.ds(2 * g, 2)] = state.T.astype(BF16).reshape(2, chans, cols)
        return carry

    lax.fori_loop(0, pairs, second, 0, unroll=2)

    def pick(n, carry):
        pos = jnp.maximum(pos_ref[n // CAP, n % CAP], 0)
        send_ref[n] = state_ref[pos]
        return carry

    lax.fori_loop(0, slots, pick, 0, unroll=4)


def convolutions(positions, place, field, above, below, left, right, k1, b1, k2, b2):
    pairs, cols, lanes = field.shape
    chans = lanes // 2
    slots = positions.shape[0] * CAP
    return pl.pallas_call(
        conv_kernel,
        out_shape=jax.ShapeDtypeStruct((slots, chans, cols), BF16),
        in_specs=[smem(), smem()] + [vmem()] * 9,
        out_specs=vmem(),
        scratch_shapes=[
            pltpu.VMEM((pairs + 2, cols, lanes), BF16),
            pltpu.VMEM((pairs + 1, cols, lanes), BF16),
            pltpu.VMEM((6, pairs + 8, lanes), F32),
            pltpu.VMEM((4, pairs + 8, lanes), F32),
            pltpu.VMEM((2 * pairs, chans, cols), BF16),
        ],
        compiler_params=pltpu.CompilerParams(vmem_limit_bytes=VMEM_LIMIT),
    )(positions, place, field, above, below, left, right, k1, b1, k2, b2)


def backward_kernel(slot_ref, code_ref, got_ref, table_ref, out_ref, rows_ref):
    blocks, width = out_ref.shape
    seg = table_ref.shape[1]
    chans = width // seg

    def one_block(b, carry):
        state = jnp.concatenate([got_ref[slot_ref[b, 0]], got_ref[slot_ref[b, 1]]], axis=1)
        weights = jnp.concatenate(
            [table_ref[code_back(code_ref[b, t])] for t in range(2)], axis=1
        )
        rows_ref[pl.ds(b, chans, stride=blocks), :] = lax.dot_general(
            state, weights, NT, preferred_element_type=F32
        )
        return carry

    lax.fori_loop(0, blocks, one_block, 0, unroll=4)
    for c in range(chans):
        out_ref[:, c * seg : (c + 1) * seg] = rows_ref[c * blocks : (c + 1) * blocks, :].astype(BF16)


def backward_remap(slots, codes, got, back_table):
    blocks = slots.shape[0]
    _, chans, seg = got.shape
    return pl.pallas_call(
        backward_kernel,
        out_shape=jax.ShapeDtypeStruct((blocks, chans * seg), BF16),
        in_specs=[smem(), smem(), vmem(), vmem()],
        out_specs=vmem(),
        scratch_shapes=[pltpu.VMEM((chans * blocks, seg), F32)],
        compiler_params=pltpu.CompilerParams(vmem_limit_bytes=VMEM_LIMIT),
    )(slots, codes, got, back_table)


def row_pair_weights(kernel):
    none = jnp.zeros((1,) + kernel.shape[1:], kernel.dtype)
    upper = jnp.concatenate([kernel, none], axis=0)
    lower = jnp.concatenate([none, kernel], axis=0)
    both = jnp.stack([upper, lower], axis=3)
    both = both.transpose(0, 2, 1, 3, 4)
    chans = kernel.shape[2]
    return both.reshape(4 * chans, 3 * 2 * kernel.shape[3])


def exchange(buffer):
    return lax.all_to_all(buffer, AXES, split_axis=0, concat_axis=0, tiled=True)


def local(
    ll_blocks,
    dest_dev,
    dest_pos,
    fwd_id,
    back_id,
    fwd_table,
    back_table,
    kernel_one,
    bias_one,
    kernel_two,
    bias_two,
):
    n_fx = lax.axis_size("fx")
    n_fy = lax.axis_size("fy")
    devices = n_fx * n_fy
    hblocks = 64
    pairs = hblocks // 2
    codes = code_of(dest_dev, dest_pos, fwd_id, back_id)
    send, slots = forward_remap(codes, ll_blocks, fwd_table, devices)
    got = exchange(send)
    positions = got[:, got.shape[1] - META :: META // 2, 0].astype(jnp.int32)
    field, edge_left, edge_right = sum_field(positions, got, hblocks)

    right_going = [(j, j + 1) for j in range(n_fy - 1)]
    left_going = [(j + 1, j) for j in range(n_fy - 1)]
    down_going = [(i, (i + 1) % n_fx) for i in range(n_fx)]
    up_going = [((i + 1) % n_fx, i) for i in range(n_fx)]
    left = lax.ppermute(edge_right, "fy", right_going)
    right = lax.ppermute(edge_left, "fy", left_going)

    def row_message(g):
        corners = [side[at * pairs + g][None] for side in (left, right) for at in (0, 1)]
        rest = jnp.zeros((12, field.shape[2]), BF16)
        return jnp.concatenate([field[g]] + corners + [rest], axis=0)

    above = lax.ppermute(row_message(pairs - 1), "fx", down_going)
    below = lax.ppermute(row_message(0), "fx", up_going)
    j = lax.axis_index("fy")
    place = jnp.stack([(j > 0).astype(jnp.int32), (j < n_fy - 1).astype(jnp.int32)])
    send_back = convolutions(
        positions,
        place,
        field,
        above,
        below,
        left,
        right,
        row_pair_weights(kernel_one),
        jnp.tile(bias_one, 2)[None],
        row_pair_weights(kernel_two),
        jnp.tile(bias_two, 2)[None],
    )
    slot_shape = send_back.shape
    got_back = exchange(send_back.reshape(devices, -1, slot_shape[2])).reshape(slot_shape)
    return backward_remap(slots, codes, got_back, back_table)


def solution(mesh):
    blocked = P(AXES, None)
    in_specs = (blocked,) * 5 + (P(),) * 6
    return jax.shard_map(
        local, mesh=mesh, in_specs=in_specs, out_specs=P(AXES, None), check_vma=False
    )
```

```python
import functools

import jax
import jax.numpy as jnp
from jax import lax
from jax.experimental import pallas as pl
from jax.experimental.pallas import tpu as pltpu
from jax.sharding import PartitionSpec as P

CAP = 2
META = 8
AXES = ("fx", "fy")
F32 = jnp.float32
BF16 = jnp.bfloat16
VMEM_LIMIT = 48 * 1024 * 1024
NT = (((1,), (1,)), ((), ()))


def code_of(dev, pos, fwd, back):
    return ((dev * 64 + pos) * 64 + fwd) * 64 + back


def code_dev(code):
    return lax.shift_right_logical(code, 18)


def code_pos(code):
    return lax.shift_right_logical(code, 12) & 63


def code_fwd(code):
    return lax.shift_right_logical(code, 6) & 63


def code_back(code):
    return code & 63


def smem():
    return pl.BlockSpec(memory_space=pltpu.SMEM)


def vmem():
    return pl.BlockSpec(memory_space=pltpu.VMEM)


def hbm():
    return pl.BlockSpec(memory_space=pl.ANY)


def params():
    return pltpu.CompilerParams(vmem_limit_bytes=VMEM_LIMIT)


def lane_iota(shape):
    return lax.broadcasted_iota(jnp.int32, shape, len(shape) - 1)


def forward_kernel(
    n_fy,
    code_ref,
    x_hbm,
    table_hbm,
    send_ref,
    slot_ref,
    x_ref,
    table_ref,
    rows_ref,
    edge_ref,
    stage_ref,
    meta_ref,
    packed_ref,
    count_ref,
    x_sem,
    table_sem,
    out_sem,
    meta_sem,
):
    blocks, width = x_ref.shape
    tables, seg, _ = table_ref.shape
    chans = width // seg
    devices = count_ref.shape[0]
    parts = x_sem.shape[0]
    wide = width // parts
    pieces = table_sem.shape[0]
    deep = tables // pieces
    x_copies = [
        pltpu.make_async_copy(
            x_hbm.at[:, pl.ds(q * wide, wide)], x_ref.at[:, pl.ds(q * wide, wide)], x_sem.at[q]
        )
        for q in range(parts)
    ]
    table_copies = [
        pltpu.make_async_copy(
            table_hbm.at[pl.ds(q * deep, deep)], table_ref.at[pl.ds(q * deep, deep)], table_sem.at[q]
        )
        for q in range(pieces)
    ]
    for copy in x_copies + table_copies:
        copy.start()

    def clear(d, carry):
        count_ref[d] = 0
        return carry

    lax.fori_loop(0, devices, clear, 0, unroll=8)
    meta_ref[...] = jnp.zeros_like(meta_ref)
    for q, copy in enumerate(x_copies):
        copy.wait()
        for c in range(q * wide // seg, (q + 1) * wide // seg):
            rows_ref[c * blocks : (c + 1) * blocks, :] = x_ref[:, c * seg : (c + 1) * seg].astype(F32)
    for q, copy in enumerate(table_copies):
        copy.wait()

        def edges(n, carry):
            edge_ref[n, 0:2, :] = table_ref[n, seg - 16 : seg, :].astype(F32)[14:16, :]
            edge_ref[n, 2:4, :] = table_ref[n, 0:16, :].astype(F32)[0:2, :]
            return carry

        lax.fori_loop(q * deep, (q + 1) * deep, edges, 0, unroll=4)
    lane = lane_iota((1, seg))

    def one_block(b, carry):
        codes = [code_ref[b, t] for t in range(2)]
        x = rows_ref[pl.ds(b, chans, stride=blocks), :].astype(BF16)
        weights = jnp.concatenate([table_ref[code_fwd(code)] for code in codes], axis=0)
        product = lax.dot_general(x, weights, NT, preferred_element_type=F32)
        tips = jnp.concatenate([edge_ref[code_fwd(code)] for code in codes], axis=0).astype(BF16)
        ends = lax.dot_general(tips, x, NT, preferred_element_type=F32)
        ends = jnp.concatenate([ends, ends], axis=1)
        for t, code in enumerate(codes):
            dev = code_dev(code)
            pos = (code_pos(code) + 1).astype(F32)
            rank = count_ref[dev]
            count_ref[dev] = rank + 1
            slot_ref[b, t] = dev * CAP + rank
            route = 2 * b + t
            stage_ref[route] = product[:, t * seg : (t + 1) * seg].astype(BF16)
            at = pl.multiple_of(rank * chans, chans)
            pltpu.make_async_copy(
                stage_ref.at[route], send_ref.at[dev, pl.ds(at, chans), :], out_sem
            ).start()
            meta_ref[dev, pl.ds(4 + rank, 1), :] = jnp.full((1, seg), pos, F32)
            col = lax.rem(dev, n_fy)
            mine = (lane >= chans) == (rank == 1)
            for side in range(2):
                inside = (col < n_fy - 1) if side == 0 else (col > 0)
                near = jnp.where(inside, dev + 1 - 2 * side, devices)
                first = t * 4 + side * 2
                meta_ref[near, pl.ds(2 * side + rank, 1), :] = jnp.where(
                    lane < chans, ends[first : first + 1, :], ends[first + 1 : first + 2, :]
                )
                old = meta_ref[near, 6 + side : 7 + side, :]
                meta_ref[near, 6 + side : 7 + side, :] = jnp.where(mine, pos, old)
        return carry

    lax.fori_loop(0, blocks, one_block, 0, unroll=8)
    packed_ref[...] = meta_ref[0:devices].astype(BF16)
    meta_copy = pltpu.make_async_copy(
        packed_ref, send_ref.at[:, pl.ds(CAP * chans, META), :], meta_sem
    )
    meta_copy.start()
    pltpu.make_async_copy(stage_ref, send_ref.at[:, pl.ds(0, chans), :], out_sem).wait()
    meta_copy.wait()


def forward_remap(codes, ll_blocks, fwd_table, devices, n_fy):
    blocks, width = ll_blocks.shape
    tables, seg, _ = fwd_table.shape
    chans = width // seg
    return pl.pallas_call(
        functools.partial(forward_kernel, n_fy),
        out_shape=(
            jax.ShapeDtypeStruct((devices, CAP * chans + META, seg), BF16),
            jax.ShapeDtypeStruct((blocks, 2), jnp.int32),
        ),
        in_specs=[smem(), hbm(), hbm()],
        out_specs=(hbm(), smem()),
        scratch_shapes=[
            pltpu.VMEM((blocks, width), BF16),
            pltpu.VMEM((tables, seg, seg), BF16),
            pltpu.VMEM((chans * blocks, seg), F32),
            pltpu.VMEM((tables, 4, seg), F32),
            pltpu.VMEM((2 * blocks, chans, seg), BF16),
            pltpu.VMEM((devices + 1, META, seg), F32),
            pltpu.VMEM((devices, META, seg), BF16),
            pltpu.SMEM((devices,), jnp.int32),
            pltpu.SemaphoreType.DMA((4,)),
            pltpu.SemaphoreType.DMA((8,)),
            pltpu.SemaphoreType.DMA,
            pltpu.SemaphoreType.DMA,
        ],
        compiler_params=params(),
    )(codes, ll_blocks, fwd_table)


def sum_kernel(
    got_hbm,
    field_ref,
    up_ref,
    down_ref,
    side_ref,
    pos_ref,
    got_ref,
    meta_ref,
    rows_ref,
    sum_ref,
    spot_ref,
    meta_sem,
    got_sem,
    spot_sem,
):
    devices, _, cols = got_ref.shape
    hblocks, chans, _ = field_ref.shape
    pairs = hblocks // 2
    lanes = 2 * chans
    parts = got_sem.shape[0]
    part = devices // parts
    meta_copy = pltpu.make_async_copy(
        got_hbm.at[:, pl.ds(CAP * chans, META), :], meta_ref, meta_sem
    )
    meta_copy.start()
    copies = [
        pltpu.make_async_copy(
            got_hbm.at[pl.ds(q * part, part), pl.ds(0, CAP * chans), :],
            got_ref.at[pl.ds(q * part, part)],
            got_sem.at[q],
        )
        for q in range(parts)
    ]
    for copy in copies:
        copy.start()

    def clear(r, carry):
        for rank in range(CAP):
            sum_ref[rank, r] = jnp.zeros((chans, cols), F32)
        return carry

    lax.fori_loop(0, hblocks, clear, 0, unroll=4)
    meta_copy.wait()
    rows_ref[...] = meta_ref[...].reshape(devices * META, lanes).astype(F32)

    def meta_row(n):
        return rows_ref[pl.ds(n, devices, stride=META), :]

    lane = lane_iota((devices, lanes))
    table = jnp.where(lane % 2 == 0, meta_row(4), meta_row(5))
    beside = [meta_row(6), meta_row(7)]
    for side in range(2):
        turned_half = pltpu.roll(beside[side], chans, axis=1)
        for rank in range(CAP):
            here = lane == 2 + 2 * side + rank
            table = jnp.where(here, beside[side] if rank == 0 else turned_half, table)
    spots = table.T[0:8, :].astype(jnp.int32) - 1
    pos_ref[...] = spots
    spot_copy = pltpu.make_async_copy(pos_ref, spot_ref, spot_sem)
    spot_copy.start()
    block = lax.broadcasted_iota(jnp.int32, (pairs, devices), 0)
    low = lane_iota((pairs, lanes)) < chans
    for side in range(2):
        sums = []
        for parity in range(2):
            total = jnp.zeros((pairs, lanes), F32)
            for rank in range(CAP):
                n = 2 + 2 * side + rank
                hit = (spots[n : n + 1, :] == 2 * block + parity).astype(F32).astype(BF16)
                total += jnp.dot(
                    hit, meta_row(2 * side + rank).astype(BF16), preferred_element_type=F32
                )
            sums.append(total)
        even, odd = sums
        side_ref[2 * side] = jnp.where(low, even, pltpu.roll(odd, chans, axis=1))
        side_ref[2 * side + 1] = jnp.where(low, pltpu.roll(even, chans, axis=1), odd)
    spot_copy.wait()
    for q, copy in enumerate(copies):
        copy.wait()

        def add(d, carry):
            for rank in range(CAP):
                pos = spot_ref[rank, d]
                row = jnp.where(pos < 0, hblocks, pos)
                block = got_ref[d, rank * chans : (rank + 1) * chans, :]
                sum_ref[rank, row] = sum_ref[rank, row] + block.astype(F32)
            return carry

        lax.fori_loop(q * part, (q + 1) * part, add, 0, unroll=4)

    def total_of(r):
        return sum_ref[0, r] + sum_ref[1, r]

    corners = jnp.zeros((up_ref.shape[0] - cols, lanes), F32)
    corner_row = lax.broadcasted_iota(jnp.int32, corners.shape, 0)
    for ref, g in ((up_ref, 0), (down_ref, pairs - 1)):
        ref[0:cols, :] = jnp.concatenate([total_of(2 * g), total_of(2 * g + 1)], axis=0).T.astype(BF16)
        rest = corners
        for n in range(4):
            rest = jnp.where(corner_row == n, side_ref[n, g : g + 1, :], rest)
        ref[cols:, :] = rest.astype(BF16)

    def finish(r, carry):
        field_ref[r] = total_of(r).astype(BF16)
        return carry

    lax.fori_loop(0, hblocks, finish, 0, unroll=4)


def sum_field(got, hblocks):
    devices, depth, cols = got.shape
    chans = (depth - META) // CAP
    pairs = hblocks // 2
    message = jax.ShapeDtypeStruct((cols + 16, 2 * chans), BF16)
    return pl.pallas_call(
        sum_kernel,
        out_shape=(
            jax.ShapeDtypeStruct((hblocks, chans, cols), BF16),
            message,
            message,
            jax.ShapeDtypeStruct((4, pairs, 2 * chans), F32),
            jax.ShapeDtypeStruct((8, devices), jnp.int32),
        ),
        in_specs=[hbm()],
        out_specs=(vmem(),) * 5,
        scratch_shapes=[
            pltpu.VMEM((devices, CAP * chans, cols), BF16),
            pltpu.VMEM((devices, META, cols), BF16),
            pltpu.VMEM((devices * META, cols), F32),
            pltpu.VMEM((CAP, hblocks + 1, chans, cols), F32),
            pltpu.SMEM((8, devices), jnp.int32),
            pltpu.SemaphoreType.DMA,
            pltpu.SemaphoreType.DMA((8,)),
            pltpu.SemaphoreType.DMA,
        ],
        compiler_params=params(),
    )(got)


def gelu(x):
    return 0.5 * x * (1.0 + jnp.tanh(0.7978845608028654 * (x + 0.044715 * (x * x * x))))


def taps(x, weights_ref, d):
    lanes = x.shape[1] // 2
    return jnp.dot(x, weights_ref[:, d * lanes : (d + 1) * lanes], preferred_element_type=F32)


def row_pair_conv(upper, lower, weights_ref, bias, before, after):
    cols, lanes = upper.shape
    rows = jnp.concatenate([upper, lower], axis=1)
    product = jnp.dot(rows, weights_ref[...], preferred_element_type=F32)
    column = lax.broadcasted_iota(jnp.int32, (cols, lanes), 0)
    ahead = pltpu.roll(product[:, 0:lanes], 1, axis=0)
    behind = pltpu.roll(product[:, 2 * lanes :], cols - 1, axis=0)
    ahead = jnp.where(column == 0, before, ahead)
    behind = jnp.where(column == cols - 1, after, behind)
    return product[:, lanes : 2 * lanes] + ahead + behind + bias


def round_to_bf16(x):
    return x.astype(BF16).astype(F32)


def inner_kernel(field_ref, side_ref, k1_ref, b1_ref, turned_ref, hid_ref, halo_ref):
    hblocks, chans, cols = field_ref.shape
    pairs = hblocks // 2

    def turn(g, carry):
        turned_ref[g] = field_ref[pl.ds(2 * g, 2)].reshape(2 * chans, cols).T
        return carry

    lax.fori_loop(0, pairs, turn, 0, unroll=4)
    b1 = b1_ref[...]
    for n, (k, d) in enumerate(((1, 0), (2, 2))):
        both = jnp.concatenate([side_ref[k, 0 : pairs - 1, :], side_ref[k, 1:pairs, :]], axis=1)
        halo_ref[n, 1:pairs, :] = taps(both.astype(BF16), k1_ref, d)

    def first(g, carry):
        out = row_pair_conv(
            turned_ref[g - 1],
            turned_ref[g],
            k1_ref,
            b1,
            halo_ref[0, pl.ds(g, 1), :],
            halo_ref[1, pl.ds(g, 1), :],
        )
        hid_ref[g] = gelu(out).astype(BF16)
        return carry

    lax.fori_loop(1, pairs, first, 0, unroll=4)


def inner_hidden(field, sides, k1, b1):
    hblocks, chans, cols = field.shape
    pairs = hblocks // 2
    shape = jax.ShapeDtypeStruct((pairs, cols, 2 * chans), BF16)
    return pl.pallas_call(
        inner_kernel,
        out_shape=(shape, shape),
        in_specs=[vmem()] * 4,
        out_specs=(vmem(), vmem()),
        scratch_shapes=[pltpu.VMEM((2, pairs + 8, 2 * chans), F32)],
        compiler_params=params(),
        cost_estimate=pl.CostEstimate(
            flops=2 * 8192 * 9 * 64 * 64, bytes_accessed=4 << 20, transcendentals=1 << 19
        ),
    )(field, sides, k1, b1)


def outer_kernel(
    pos_ref,
    place_ref,
    field_ref,
    hid_ref,
    sides_ref,
    above_ref,
    below_ref,
    k1_ref,
    b1_ref,
    k2_ref,
    b2_ref,
    send_ref,
    side_ref,
    halo_ref,
    state_ref,
    stage_ref,
    out_sem,
):
    pairs, cols, lanes = field_ref.shape
    chans = lanes // 2
    devices = pos_ref.shape[1]
    groups = pairs + 1
    above = above_ref[cols:, :].astype(F32)
    below = below_ref[cols:, :].astype(F32)
    for n, k in enumerate((0, 1, 4, 5)):
        side_ref[k, 0:1, :] = above[n : n + 1, :]
        side_ref[k, 1 : pairs + 1, :] = sides_ref[n]
        side_ref[k, pairs + 1 : pairs + 2, :] = below[n : n + 1, :]

    def ends(block):
        return (
            block[0:16, :].astype(F32)[0:1, :],
            block[cols - 16 : cols, :].astype(F32)[15:16, :],
        )

    for k, (high, low) in enumerate(zip(ends(above_ref[0:cols, :]), ends(below_ref[0:cols, :]))):
        side_ref[2 + k, 0:1, :] = high
        side_ref[2 + k, pairs + 1 : pairs + 2, :] = low

    def inner_side(g, carry):
        for k, end in enumerate(ends(field_ref[g])):
            side_ref[2 + k, pl.ds(g + 1, 1), :] = end
        return carry

    lax.fori_loop(0, pairs, inner_side, 0, unroll=4)

    def paired(k):
        return jnp.concatenate(
            [side_ref[k, 0:groups, :], side_ref[k, 1 : groups + 1, :]], axis=1
        ).astype(BF16)

    b1 = b1_ref[...]
    b2 = b2_ref[...]
    c = [paired(k) for k in range(6)]
    left = taps(c[1], k1_ref, 0)
    right = taps(c[4], k1_ref, 2)
    before = taps(c[0], k1_ref, 0) + taps(c[1], k1_ref, 1) + taps(c[2], k1_ref, 2) + b1
    after = taps(c[3], k1_ref, 0) + taps(c[4], k1_ref, 1) + taps(c[5], k1_ref, 2) + b1
    before = jnp.where(place_ref[0] > 0, gelu(before), 0.0)
    after = jnp.where(place_ref[1] > 0, gelu(after), 0.0)
    for n, (column, d) in enumerate(((before, 0), (after, 2))):
        side_ref[n, 0:groups, :] = column
        both = jnp.concatenate([side_ref[n, 0:pairs, :], side_ref[n, 1 : pairs + 1, :]], axis=1)
        halo_ref[n, 0:pairs, :] = taps(both.astype(BF16), k2_ref, d)

    def hidden(upper, lower, g):
        out = row_pair_conv(upper, lower, k1_ref, b1, left[g : g + 1, :], right[g : g + 1, :])
        return gelu(out).astype(BF16)

    def second(g, upper, lower):
        out = row_pair_conv(
            upper, lower, k2_ref, b2, halo_ref[0, pl.ds(g, 1), :], halo_ref[1, pl.ds(g, 1), :]
        )
        state = out + field_ref[g].astype(F32)
        state_ref[pl.ds(2 * g, 2)] = state.T.astype(BF16).reshape(2, chans, cols)

    second(0, hidden(above_ref[0:cols, :], field_ref[0], 0), hid_ref[1])
    second(pairs - 1, hid_ref[pairs - 1], hidden(field_ref[pairs - 1], below_ref[0:cols, :], pairs))

    def inner(g, carry):
        second(g, hid_ref[g], hid_ref[g + 1])
        return carry

    lax.fori_loop(1, pairs - 1, inner, 0, unroll=5)
    parts = out_sem.shape[0]
    part = devices // parts
    copies = []
    for q in range(parts):

        def pick(d, carry):
            for rank in range(CAP):
                pos = jnp.maximum(pos_ref[rank, d], 0)
                stage_ref[d, rank * chans : (rank + 1) * chans, :] = state_ref[pos]
            return carry

        lax.fori_loop(q * part, (q + 1) * part, pick, 0, unroll=4)
        piece = pl.ds(q * part, part)
        copies.append(pltpu.make_async_copy(stage_ref.at[piece], send_ref.at[piece], out_sem.at[q]))
        copies[-1].start()
    for copy in copies:
        copy.wait()


def outer_state(positions, place, field, hidden, sides, above, below, k1, b1, k2, b2):
    pairs, cols, lanes = field.shape
    chans = lanes // 2
    devices = positions.shape[1]
    return pl.pallas_call(
        outer_kernel,
        out_shape=jax.ShapeDtypeStruct((devices, CAP * chans, cols), BF16),
        in_specs=[smem(), smem()] + [vmem()] * 9,
        out_specs=hbm(),
        scratch_shapes=[
            pltpu.VMEM((6, pairs + 8, lanes), F32),
            pltpu.VMEM((2, pairs + 8, lanes), F32),
            pltpu.VMEM((2 * pairs, chans, cols), BF16),
            pltpu.VMEM((devices, CAP * chans, cols), BF16),
            pltpu.SemaphoreType.DMA((8,)),
        ],
        compiler_params=params(),
    )(positions, place, field, hidden, sides, above, below, k1, b1, k2, b2)


def backward_kernel(slot_ref, code_ref, got_hbm, table_ref, out_ref, got_ref, rows_ref, got_sem):
    blocks, width = out_ref.shape
    seg = table_ref.shape[1]
    chans = width // seg
    parts = got_sem.shape[0]
    part = blocks // parts

    def fetch(q):
        def one(b, carry):
            for t in range(2):
                slot = slot_ref[b, t]
                at = pl.multiple_of(lax.rem(slot, CAP) * chans, chans)
                pltpu.make_async_copy(
                    got_hbm.at[lax.div(slot, CAP), pl.ds(at, chans), :],
                    got_ref.at[q, 2 * (b - q * part) + t],
                    got_sem.at[q],
                ).start()
            return carry

        lax.fori_loop(q * part, (q + 1) * part, one, 0, unroll=4)

    def arrived(q):
        pltpu.make_async_copy(
            got_hbm.at[pl.ds(0, 2 * part), pl.ds(0, chans), :], got_ref.at[q], got_sem.at[q]
        ).wait()

    for q in range(parts):
        fetch(q)
    for q in range(parts):
        arrived(q)

        def one_block(n, carry):
            b = q * part + n
            state = jnp.concatenate([got_ref[q, 2 * n], got_ref[q, 2 * n + 1]], axis=1)
            weights = jnp.concatenate(
                [table_ref[code_back(code_ref[b, t])] for t in range(2)], axis=1
            )
            rows_ref[pl.ds(b, chans, stride=blocks), :] = lax.dot_general(
                state, weights, NT, preferred_element_type=F32
            )
            return carry

        lax.fori_loop(0, part, one_block, 0, unroll=16)
    for c in range(chans):
        out_ref[:, c * seg : (c + 1) * seg] = rows_ref[c * blocks : (c + 1) * blocks, :].astype(BF16)


def backward_remap(slots, codes, got, back_table):
    blocks = slots.shape[0]
    chans = got.shape[1] // CAP
    seg = got.shape[2]
    parts = 4
    return pl.pallas_call(
        backward_kernel,
        out_shape=jax.ShapeDtypeStruct((blocks, chans * seg), BF16),
        in_specs=[smem(), smem(), hbm(), vmem()],
        out_specs=vmem(),
        scratch_shapes=[
            pltpu.VMEM((parts, 2 * blocks // parts, chans, seg), BF16),
            pltpu.VMEM((chans * blocks, seg), F32),
            pltpu.SemaphoreType.DMA((parts,)),
        ],
        compiler_params=params(),
    )(slots, codes, got, back_table)


def row_pair_weights(kernel):
    none = jnp.zeros((1,) + kernel.shape[1:], kernel.dtype)
    upper = jnp.concatenate([kernel, none], axis=0)
    lower = jnp.concatenate([none, kernel], axis=0)
    both = jnp.stack([upper, lower], axis=3)
    both = both.transpose(0, 2, 1, 3, 4)
    chans = kernel.shape[2]
    return both.reshape(4 * chans, 3 * 2 * kernel.shape[3])


def exchange(buffer):
    return lax.all_to_all(buffer, AXES, split_axis=0, concat_axis=0, tiled=True)


def local(
    ll_blocks,
    dest_dev,
    dest_pos,
    fwd_id,
    back_id,
    fwd_table,
    back_table,
    kernel_one,
    bias_one,
    kernel_two,
    bias_two,
):
    n_fx = lax.axis_size("fx")
    n_fy = lax.axis_size("fy")
    hblocks = 64
    codes = code_of(dest_dev, dest_pos, fwd_id, back_id)
    send, slots = forward_remap(codes, ll_blocks, fwd_table, n_fx * n_fy, n_fy)
    field, up, down, sides, positions = sum_field(exchange(send), hblocks)
    above = lax.ppermute(down, "fx", [(i, (i + 1) % n_fx) for i in range(n_fx)])
    below = lax.ppermute(up, "fx", [((i + 1) % n_fx, i) for i in range(n_fx)])
    k1 = row_pair_weights(kernel_one)
    b1 = jnp.tile(bias_one, 2)[None]
    turned, hidden = inner_hidden(field, sides, k1, b1)
    j = lax.axis_index("fy")
    place = jnp.stack([(j > 0).astype(jnp.int32), (j < n_fy - 1).astype(jnp.int32)])
    k2 = row_pair_weights(kernel_two)
    b2 = jnp.tile(bias_two, 2)[None]
    send_back = outer_state(
        positions, place, turned, hidden, sides, above, below, k1, b1, k2, b2
    )
    return backward_remap(slots, codes, exchange(send_back), back_table)


def solution(mesh):
    blocked = P(AXES, None)
    in_specs = (blocked,) * 5 + (P(),) * 6
    return jax.shard_map(
        local, mesh=mesh, in_specs=in_specs, out_specs=P(AXES, None), check_vma=False
    )
```

```python
import functools

import jax
import jax.numpy as jnp
from jax import lax
from jax.experimental import pallas as pl
from jax.experimental.pallas import tpu as pltpu
from jax.sharding import PartitionSpec as P

CAP = 2
META = 8
AXES = ("fx", "fy")
F32 = jnp.float32
BF16 = jnp.bfloat16
VMEM_LIMIT = 40 * 1024 * 1024
FULL_VMEM = 60 * 1024 * 1024
NT = (((1,), (1,)), ((), ()))


def smem():
    return pl.BlockSpec(memory_space=pltpu.SMEM)


def vmem():
    return pl.BlockSpec(memory_space=pltpu.VMEM)


def hbm():
    return pl.BlockSpec(memory_space=pl.ANY)


def params(limit=VMEM_LIMIT):
    return pltpu.CompilerParams(vmem_limit_bytes=limit)


def log2(count):
    assert count & (count - 1) == 0
    return count.bit_length() - 1


def lane_iota(shape):
    return lax.broadcasted_iota(jnp.int32, shape, len(shape) - 1)


def forward_kernel(
    n_fy,
    dev_hbm,
    pos_hbm,
    fwd_hbm,
    back_hbm,
    x_hbm,
    table_hbm,
    send_ref,
    return_hbm,
    dev_ref,
    pos_ref,
    fwd_ref,
    back_ref,
    return_ref,
    x_ref,
    table_ref,
    rows_ref,
    edge_ref,
    stage_ref,
    meta_ref,
    packed_ref,
    count_ref,
    code_sem,
    x_sem,
    table_sem,
    out_sem,
    meta_sem,
    return_sem,
):
    blocks, width = x_ref.shape
    tables, seg, _ = table_ref.shape
    chans = width // seg
    devices = count_ref.shape[0]
    assert n_fy == 1 << log2(n_fy)
    parts = x_sem.shape[0]
    wide = width // parts
    pieces = table_sem.shape[0]
    deep = tables // pieces
    x_copies = [
        pltpu.make_async_copy(
            x_hbm.at[:, pl.ds(q * wide, wide)], x_ref.at[:, pl.ds(q * wide, wide)], x_sem.at[q]
        )
        for q in range(parts)
    ]
    table_copies = [
        pltpu.make_async_copy(
            table_hbm.at[pl.ds(q * deep, deep)], table_ref.at[pl.ds(q * deep, deep)], table_sem.at[q]
        )
        for q in range(pieces)
    ]
    code_copies = [
        pltpu.make_async_copy(source, target, code_sem.at[n])
        for n, (source, target) in enumerate(
            ((dev_hbm, dev_ref), (pos_hbm, pos_ref), (fwd_hbm, fwd_ref), (back_hbm, back_ref))
        )
    ]
    for copy in code_copies + x_copies + table_copies:
        copy.start()

    def clear(d, carry):
        count_ref[d] = 0
        return carry

    lax.fori_loop(0, devices, clear, 0, unroll=8)
    meta_ref[...] = jnp.zeros_like(meta_ref)
    for q, copy in enumerate(x_copies):
        copy.wait()
        for c in range(q * wide // seg, (q + 1) * wide // seg):
            rows_ref[c * blocks : (c + 1) * blocks, :] = x_ref[:, c * seg : (c + 1) * seg].astype(F32)
    for q, copy in enumerate(table_copies):
        copy.wait()

        def edges(n, carry):
            edge_ref[n, 0:2, :] = table_ref[n, seg - 16 : seg, :].astype(F32)[14:16, :]
            edge_ref[n, 2:4, :] = table_ref[n, 0:16, :].astype(F32)[0:2, :]
            return carry

        lax.fori_loop(q * deep, (q + 1) * deep, edges, 0, unroll=4)
    for copy in code_copies:
        copy.wait()
    lane = lane_iota((1, seg))

    def one_block(b, carry):
        tables_of = [fwd_ref[t, b] for t in range(2)]
        x = rows_ref[pl.ds(b, chans, stride=blocks), :].astype(BF16)
        weights = jnp.concatenate([table_ref[n] for n in tables_of], axis=0)
        product = lax.dot_general(x, weights, NT, preferred_element_type=F32)
        tips = jnp.concatenate([edge_ref[n] for n in tables_of], axis=0).astype(BF16)
        ends = lax.dot_general(tips, x, NT, preferred_element_type=F32)
        ends = jnp.concatenate([ends, ends], axis=1)
        for t in range(2):
            dev = dev_ref[t, b]
            pos = (pos_ref[t, b] + 1).astype(F32)
            rank = count_ref[dev]
            count_ref[dev] = rank + 1
            return_ref[t, b] = ((dev * CAP + rank) << log2(tables)) + back_ref[t, b]
            route = 2 * b + t
            stage_ref[route] = product[:, t * seg : (t + 1) * seg].astype(BF16)
            at = pl.multiple_of(rank * chans, chans)
            pltpu.make_async_copy(
                stage_ref.at[route], send_ref.at[dev, pl.ds(at, chans), :], out_sem
            ).start()
            meta_ref[dev, pl.ds(4 + rank, 1), :] = jnp.full((1, seg), pos, F32)
            col = dev & (n_fy - 1)
            mine = (lane >= chans) == (rank == 1)
            for side in range(2):
                inside = (col < n_fy - 1) if side == 0 else (col > 0)
                near = jnp.where(inside, dev + 1 - 2 * side, devices)
                first = t * 4 + side * 2
                meta_ref[near, pl.ds(2 * side + rank, 1), :] = jnp.where(
                    lane < chans, ends[first : first + 1, :], ends[first + 1 : first + 2, :]
                )
                old = meta_ref[near, 6 + side : 7 + side, :]
                meta_ref[near, 6 + side : 7 + side, :] = jnp.where(mine, pos, old)
        return carry

    lax.fori_loop(0, blocks, one_block, 0, unroll=True)
    packed_ref[...] = meta_ref[0:devices].astype(BF16)
    meta_copy = pltpu.make_async_copy(
        packed_ref, send_ref.at[:, pl.ds(CAP * chans, META), :], meta_sem
    )
    meta_copy.start()
    return_copy = pltpu.make_async_copy(return_ref, return_hbm, return_sem)
    return_copy.start()
    pltpu.make_async_copy(stage_ref, send_ref.at[:, pl.ds(0, chans), :], out_sem).wait()
    meta_copy.wait()
    return_copy.wait()


def forward_remap(dest_dev, dest_pos, fwd_id, back_id, ll_blocks, fwd_table, devices, n_fy):
    blocks, width = ll_blocks.shape
    tables, seg, _ = fwd_table.shape
    chans = width // seg
    return pl.pallas_call(
        functools.partial(forward_kernel, n_fy),
        out_shape=(
            jax.ShapeDtypeStruct((devices, CAP * chans + META, seg), BF16),
            jax.ShapeDtypeStruct((2, blocks), jnp.int32),
        ),
        in_specs=[hbm()] * 6,
        out_specs=(hbm(), hbm()),
        scratch_shapes=[
            pltpu.SMEM((2, blocks), jnp.int32),
            pltpu.SMEM((2, blocks), jnp.int32),
            pltpu.SMEM((2, blocks), jnp.int32),
            pltpu.SMEM((2, blocks), jnp.int32),
            pltpu.SMEM((2, blocks), jnp.int32),
            pltpu.VMEM((blocks, width), BF16),
            pltpu.VMEM((tables, seg, seg), BF16),
            pltpu.VMEM((chans * blocks, seg), F32),
            pltpu.VMEM((tables, 4, seg), F32),
            pltpu.VMEM((2 * blocks, chans, seg), BF16),
            pltpu.VMEM((devices + 1, META, seg), F32),
            pltpu.VMEM((devices, META, seg), BF16),
            pltpu.SMEM((devices,), jnp.int32),
            pltpu.SemaphoreType.DMA((4,)),
            pltpu.SemaphoreType.DMA((4,)),
            pltpu.SemaphoreType.DMA((8,)),
            pltpu.SemaphoreType.DMA,
            pltpu.SemaphoreType.DMA,
            pltpu.SemaphoreType.DMA,
        ],
        compiler_params=params(FULL_VMEM),
    )(dest_dev.T, dest_pos.T, fwd_id.T, back_id.T, ll_blocks, fwd_table)


def sum_kernel(
    got_hbm,
    field_ref,
    up_ref,
    down_ref,
    side_ref,
    pos_ref,
    got_ref,
    meta_ref,
    rows_ref,
    sum_ref,
    spot_ref,
    meta_sem,
    got_sem,
    spot_sem,
):
    devices, _, cols = got_ref.shape
    hblocks, chans, _ = field_ref.shape
    pairs = hblocks // 2
    lanes = 2 * chans
    parts = got_sem.shape[0]
    part = devices // parts
    meta_copy = pltpu.make_async_copy(
        got_hbm.at[:, pl.ds(CAP * chans, META), :], meta_ref, meta_sem
    )
    meta_copy.start()
    copies = [
        pltpu.make_async_copy(
            got_hbm.at[pl.ds(q * part, part), pl.ds(0, CAP * chans), :],
            got_ref.at[pl.ds(q * part, part)],
            got_sem.at[q],
        )
        for q in range(parts)
    ]
    for copy in copies:
        copy.start()

    def clear(r, carry):
        for rank in range(CAP):
            sum_ref[rank, r] = jnp.zeros((chans, cols), F32)
        return carry

    lax.fori_loop(0, hblocks, clear, 0, unroll=4)
    meta_copy.wait()
    rows_ref[...] = meta_ref[...].reshape(devices * META, lanes).astype(F32)

    def meta_row(n):
        return rows_ref[pl.ds(n, devices, stride=META), :]

    lane = lane_iota((devices, lanes))
    table = jnp.where(lane % 2 == 0, meta_row(4), meta_row(5))
    beside = [meta_row(6), meta_row(7)]
    for side in range(2):
        turned_half = pltpu.roll(beside[side], chans, axis=1)
        for rank in range(CAP):
            here = lane == 2 + 2 * side + rank
            table = jnp.where(here, beside[side] if rank == 0 else turned_half, table)
    spots = table.T[0:8, :].astype(jnp.int32) - 1
    pos_ref[...] = spots
    spot_copy = pltpu.make_async_copy(pos_ref, spot_ref, spot_sem)
    spot_copy.start()
    block = lax.broadcasted_iota(jnp.int32, (pairs, devices), 0)
    low = lane_iota((pairs, lanes)) < chans
    for side in range(2):
        sums = []
        for parity in range(2):
            total = jnp.zeros((pairs, lanes), F32)
            for rank in range(CAP):
                n = 2 + 2 * side + rank
                hit = (spots[n : n + 1, :] == 2 * block + parity).astype(F32).astype(BF16)
                total += jnp.dot(
                    hit, meta_row(2 * side + rank).astype(BF16), preferred_element_type=F32
                )
            sums.append(total)
        even, odd = sums
        side_ref[2 * side] = jnp.where(low, even, pltpu.roll(odd, chans, axis=1))
        side_ref[2 * side + 1] = jnp.where(low, pltpu.roll(even, chans, axis=1), odd)
    spot_copy.wait()
    for q, copy in enumerate(copies):
        copy.wait()

        def add(d, carry):
            for rank in range(CAP):
                pos = spot_ref[rank, d]
                row = jnp.where(pos < 0, hblocks, pos)
                block = got_ref[d, rank * chans : (rank + 1) * chans, :]
                sum_ref[rank, row] = sum_ref[rank, row] + block.astype(F32)
            return carry

        lax.fori_loop(q * part, (q + 1) * part, add, 0, unroll=4)

    def total_of(r):
        return sum_ref[0, r] + sum_ref[1, r]

    corners = jnp.zeros((up_ref.shape[0] - cols, lanes), F32)
    corner_row = lax.broadcasted_iota(jnp.int32, corners.shape, 0)
    for ref, g in ((up_ref, 0), (down_ref, pairs - 1)):
        ref[0:cols, :] = jnp.concatenate([total_of(2 * g), total_of(2 * g + 1)], axis=0).T.astype(BF16)
        rest = corners
        for n in range(4):
            rest = jnp.where(corner_row == n, side_ref[n, g : g + 1, :], rest)
        ref[cols:, :] = rest.astype(BF16)

    def finish(r, carry):
        field_ref[r] = total_of(r).astype(BF16)
        return carry

    lax.fori_loop(0, hblocks, finish, 0, unroll=4)


def sum_field(got, hblocks):
    devices, depth, cols = got.shape
    chans = (depth - META) // CAP
    pairs = hblocks // 2
    message = jax.ShapeDtypeStruct((cols + 16, 2 * chans), BF16)
    return pl.pallas_call(
        sum_kernel,
        out_shape=(
            jax.ShapeDtypeStruct((hblocks, chans, cols), BF16),
            message,
            message,
            jax.ShapeDtypeStruct((4, pairs, 2 * chans), F32),
            jax.ShapeDtypeStruct((8, devices), jnp.int32),
        ),
        in_specs=[hbm()],
        out_specs=(vmem(),) * 5,
        scratch_shapes=[
            pltpu.VMEM((devices, CAP * chans, cols), BF16),
            pltpu.VMEM((devices, META, cols), BF16),
            pltpu.VMEM((devices * META, cols), F32),
            pltpu.VMEM((CAP, hblocks + 1, chans, cols), F32),
            pltpu.SMEM((8, devices), jnp.int32),
            pltpu.SemaphoreType.DMA,
            pltpu.SemaphoreType.DMA((8,)),
            pltpu.SemaphoreType.DMA,
        ],
        compiler_params=params(),
    )(got)


def gelu(x):
    return 0.5 * x * (1.0 + jnp.tanh(0.7978845608028654 * (x + 0.044715 * (x * x * x))))


def taps(x, weights_ref, d):
    lanes = x.shape[1] // 2
    return jnp.dot(x, weights_ref[:, d * lanes : (d + 1) * lanes], preferred_element_type=F32)


def row_pair_conv(upper, lower, weights_ref, bias, before, after):
    cols, lanes = upper.shape
    rows = jnp.concatenate([upper, lower], axis=1)
    product = jnp.dot(rows, weights_ref[...], preferred_element_type=F32)
    column = lax.broadcasted_iota(jnp.int32, (cols, lanes), 0)
    ahead = pltpu.roll(product[:, 0:lanes], 1, axis=0)
    behind = pltpu.roll(product[:, 2 * lanes :], cols - 1, axis=0)
    ahead = jnp.where(column == 0, before, ahead)
    behind = jnp.where(column == cols - 1, after, behind)
    return product[:, lanes : 2 * lanes] + ahead + behind + bias


def round_to_bf16(x):
    return x.astype(BF16).astype(F32)


def inner_kernel(field_ref, side_ref, k1_ref, b1_ref, turned_ref, hid_ref, halo_ref):
    hblocks, chans, cols = field_ref.shape
    pairs = hblocks // 2

    def turn(g, carry):
        turned_ref[g] = field_ref[pl.ds(2 * g, 2)].reshape(2 * chans, cols).T
        return carry

    lax.fori_loop(0, pairs, turn, 0, unroll=4)
    b1 = b1_ref[...]
    for n, (k, d) in enumerate(((1, 0), (2, 2))):
        both = jnp.concatenate([side_ref[k, 0 : pairs - 1, :], side_ref[k, 1:pairs, :]], axis=1)
        halo_ref[n, 1:pairs, :] = taps(both.astype(BF16), k1_ref, d)

    def first(g, carry):
        out = row_pair_conv(
            turned_ref[g - 1],
            turned_ref[g],
            k1_ref,
            b1,
            halo_ref[0, pl.ds(g, 1), :],
            halo_ref[1, pl.ds(g, 1), :],
        )
        hid_ref[g] = gelu(out).astype(BF16)
        return carry

    lax.fori_loop(1, pairs, first, 0, unroll=True)


def inner_hidden(field, sides, k1, b1):
    hblocks, chans, cols = field.shape
    pairs = hblocks // 2
    shape = jax.ShapeDtypeStruct((pairs, cols, 2 * chans), BF16)
    return pl.pallas_call(
        inner_kernel,
        out_shape=(shape, shape),
        in_specs=[vmem()] * 4,
        out_specs=(vmem(), vmem()),
        scratch_shapes=[pltpu.VMEM((2, pairs + 8, 2 * chans), F32)],
        compiler_params=params(),
        cost_estimate=pl.CostEstimate(
            flops=2 * 8192 * 9 * 64 * 64, bytes_accessed=4 << 20, transcendentals=1 << 19
        ),
    )(field, sides, k1, b1)


def outer_kernel(
    pos_hbm,
    place_ref,
    field_ref,
    hid_ref,
    sides_ref,
    above_ref,
    below_ref,
    k1_ref,
    b1_ref,
    k2_ref,
    b2_ref,
    send_ref,
    side_ref,
    halo_ref,
    state_ref,
    stage_ref,
    pos_ref,
    out_sem,
    pos_sem,
):
    pos_copy = pltpu.make_async_copy(pos_hbm, pos_ref, pos_sem)
    pos_copy.start()
    pairs, cols, lanes = field_ref.shape
    chans = lanes // 2
    devices = pos_ref.shape[1]
    groups = pairs + 1
    above = above_ref[cols:, :].astype(F32)
    below = below_ref[cols:, :].astype(F32)
    for n, k in enumerate((0, 1, 4, 5)):
        side_ref[k, 0:1, :] = above[n : n + 1, :]
        side_ref[k, 1 : pairs + 1, :] = sides_ref[n]
        side_ref[k, pairs + 1 : pairs + 2, :] = below[n : n + 1, :]

    def ends(block):
        return (
            block[0:16, :].astype(F32)[0:1, :],
            block[cols - 16 : cols, :].astype(F32)[15:16, :],
        )

    for k, (high, low) in enumerate(zip(ends(above_ref[0:cols, :]), ends(below_ref[0:cols, :]))):
        side_ref[2 + k, 0:1, :] = high
        side_ref[2 + k, pairs + 1 : pairs + 2, :] = low

    def inner_side(g, carry):
        for k, end in enumerate(ends(field_ref[g])):
            side_ref[2 + k, pl.ds(g + 1, 1), :] = end
        return carry

    lax.fori_loop(0, pairs, inner_side, 0, unroll=4)

    def paired(k):
        return jnp.concatenate(
            [side_ref[k, 0:groups, :], side_ref[k, 1 : groups + 1, :]], axis=1
        ).astype(BF16)

    b1 = b1_ref[...]
    b2 = b2_ref[...]
    c = [paired(k) for k in range(6)]
    left = taps(c[1], k1_ref, 0)
    right = taps(c[4], k1_ref, 2)
    before = taps(c[0], k1_ref, 0) + taps(c[1], k1_ref, 1) + taps(c[2], k1_ref, 2) + b1
    after = taps(c[3], k1_ref, 0) + taps(c[4], k1_ref, 1) + taps(c[5], k1_ref, 2) + b1
    before = jnp.where(place_ref[0:1, :] > 0, gelu(before), 0.0)
    after = jnp.where(place_ref[1:2, :] > 0, gelu(after), 0.0)
    for n, (column, d) in enumerate(((before, 0), (after, 2))):
        side_ref[n, 0:groups, :] = column
        both = jnp.concatenate([side_ref[n, 0:pairs, :], side_ref[n, 1 : pairs + 1, :]], axis=1)
        halo_ref[n, 0:pairs, :] = taps(both.astype(BF16), k2_ref, d)

    def hidden(upper, lower, g):
        out = row_pair_conv(upper, lower, k1_ref, b1, left[g : g + 1, :], right[g : g + 1, :])
        return gelu(out).astype(BF16)

    def second(g, upper, lower):
        out = row_pair_conv(
            upper, lower, k2_ref, b2, halo_ref[0, pl.ds(g, 1), :], halo_ref[1, pl.ds(g, 1), :]
        )
        state = out + field_ref[g].astype(F32)
        state_ref[pl.ds(2 * g, 2)] = state.T.astype(BF16).reshape(2, chans, cols)

    second(0, hidden(above_ref[0:cols, :], field_ref[0], 0), hid_ref[1])
    second(pairs - 1, hid_ref[pairs - 1], hidden(field_ref[pairs - 1], below_ref[0:cols, :], pairs))

    def inner(g, carry):
        second(g, hid_ref[g], hid_ref[g + 1])
        return carry

    lax.fori_loop(1, pairs - 1, inner, 0, unroll=True)
    parts = out_sem.shape[0]
    part = devices // parts
    copies = []
    pos_copy.wait()
    for q in range(parts):

        def pick(d, carry):
            for rank in range(CAP):
                pos = jnp.maximum(pos_ref[rank, d], 0)
                stage_ref[d, rank * chans : (rank + 1) * chans, :] = state_ref[pos]
            return carry

        lax.fori_loop(q * part, (q + 1) * part, pick, 0, unroll=4)
        piece = pl.ds(q * part, part)
        copies.append(pltpu.make_async_copy(stage_ref.at[piece], send_ref.at[piece], out_sem.at[q]))
        copies[-1].start()
    for copy in copies:
        copy.wait()


def outer_state(positions, place, field, hidden, sides, above, below, k1, b1, k2, b2):
    pairs, cols, lanes = field.shape
    chans = lanes // 2
    devices = positions.shape[1]
    return pl.pallas_call(
        outer_kernel,
        out_shape=jax.ShapeDtypeStruct((devices, CAP * chans, cols), BF16),
        in_specs=[vmem()] * 11,
        out_specs=hbm(),
        scratch_shapes=[
            pltpu.VMEM((6, pairs + 8, lanes), F32),
            pltpu.VMEM((2, pairs + 8, lanes), F32),
            pltpu.VMEM((2 * pairs, chans, cols), BF16),
            pltpu.VMEM((devices, CAP * chans, cols), BF16),
            pltpu.SMEM(positions.shape, jnp.int32),
            pltpu.SemaphoreType.DMA((8,)),
            pltpu.SemaphoreType.DMA,
        ],
        compiler_params=params(),
    )(positions, place, field, hidden, sides, above, below, k1, b1, k2, b2)


def backward_kernel(
    return_hbm,
    got_hbm,
    table_ref,
    out_hbm,
    return_ref,
    got_ref,
    rows_ref,
    out_ref,
    return_sem,
    got_sem,
    out_sem,
):
    blocks, width = out_hbm.shape
    tables, seg, _ = table_ref.shape
    chans = width // seg
    devices = got_ref.shape[0]
    loads = got_sem.shape[0]
    load = devices // loads
    parts = out_sem.shape[0]
    part = blocks // parts
    copies = [pltpu.make_async_copy(return_hbm, return_ref, return_sem)]
    for q in range(loads):
        piece = pl.ds(q * load, load)
        copies.append(
            pltpu.make_async_copy(got_hbm.at[piece], got_ref.at[piece], got_sem.at[q])
        )
    for copy in copies:
        copy.start()
    for copy in copies:
        copy.wait()

    out_copies = []

    def finish(q):
        piece = pl.ds(q * part, part)
        for c in range(chans):
            out_ref[piece, c * seg : (c + 1) * seg] = rows_ref[
                q, c * part : (c + 1) * part, :
            ].astype(BF16)
        out_copies.append(
            pltpu.make_async_copy(out_ref.at[piece], out_hbm.at[piece], out_sem.at[q])
        )
        out_copies[-1].start()

    for q in range(parts):
        if q > 0:
            finish(q - 1)
        for n in range(part):
            states, weights = [], []
            for t in range(2):
                code = return_ref[t, q * part + n]
                slot = code >> log2(tables)
                at = pl.multiple_of((slot & 1) * chans, chans)
                states.append(got_ref[slot >> 1, pl.ds(at, chans), :])
                weights.append(table_ref[code & (tables - 1)])
            rows_ref[q, pl.ds(n, chans, stride=part), :] = lax.dot_general(
                jnp.concatenate(states, axis=1),
                jnp.concatenate(weights, axis=1),
                NT,
                preferred_element_type=F32,
            )
    finish(parts - 1)
    for copy in out_copies:
        copy.wait()


def backward_remap(returns, got, back_table):
    blocks = returns.shape[1]
    chans = got.shape[1] // CAP
    seg = got.shape[2]
    parts = 4
    return pl.pallas_call(
        backward_kernel,
        out_shape=jax.ShapeDtypeStruct((blocks, chans * seg), BF16),
        in_specs=[hbm(), hbm(), vmem()],
        out_specs=hbm(),
        scratch_shapes=[
            pltpu.SMEM(returns.shape, jnp.int32),
            pltpu.VMEM(got.shape, BF16),
            pltpu.VMEM((parts, chans * blocks // parts, seg), F32),
            pltpu.VMEM((blocks, chans * seg), BF16),
            pltpu.SemaphoreType.DMA,
            pltpu.SemaphoreType.DMA((8,)),
            pltpu.SemaphoreType.DMA((parts,)),
        ],
        compiler_params=params(),
    )(returns, got, back_table)


def row_pair_weights(kernel):
    none = jnp.zeros((1,) + kernel.shape[1:], kernel.dtype)
    upper = jnp.concatenate([kernel, none], axis=0)
    lower = jnp.concatenate([none, kernel], axis=0)
    both = jnp.stack([upper, lower], axis=3)
    both = both.transpose(0, 2, 1, 3, 4)
    chans = kernel.shape[2]
    return both.reshape(4 * chans, 3 * 2 * kernel.shape[3])


def exchange(buffer):
    return lax.all_to_all(buffer, AXES, split_axis=0, concat_axis=0, tiled=True)


def local(
    ll_blocks,
    dest_dev,
    dest_pos,
    fwd_id,
    back_id,
    fwd_table,
    back_table,
    kernel_one,
    bias_one,
    kernel_two,
    bias_two,
):
    n_fx = lax.axis_size("fx")
    n_fy = lax.axis_size("fy")
    hblocks = 64
    send, returns = forward_remap(
        dest_dev, dest_pos, fwd_id, back_id, ll_blocks, fwd_table, n_fx * n_fy, n_fy
    )
    field, up, down, sides, positions = sum_field(exchange(send), hblocks)
    above = lax.ppermute(down, "fx", [(i, (i + 1) % n_fx) for i in range(n_fx)])
    below = lax.ppermute(up, "fx", [((i + 1) % n_fx, i) for i in range(n_fx)])
    k1 = row_pair_weights(kernel_one)
    b1 = jnp.tile(bias_one, 2)[None]
    turned, hidden = inner_hidden(field, sides, k1, b1)
    j = lax.axis_index("fy")
    place = jnp.stack([j > 0, j < n_fy - 1]).astype(jnp.int32)[:, None]
    place = jnp.broadcast_to(place, (2, 128))
    k2 = row_pair_weights(kernel_two)
    b2 = jnp.tile(bias_two, 2)[None]
    send_back = outer_state(
        positions, place, turned, hidden, sides, above, below, k1, b1, k2, b2
    )
    return backward_remap(returns, exchange(send_back), back_table)


def solution(mesh):
    blocked = P(AXES, None)
    in_specs = (blocked,) * 5 + (P(),) * 6
    return jax.shard_map(
        local, mesh=mesh, in_specs=in_specs, out_specs=P(AXES, None), check_vma=False
    )
```

```python
import functools

import jax
import jax.numpy as jnp
from jax import lax
from jax.experimental import pallas as pl
from jax.experimental.pallas import tpu as pltpu
from jax.sharding import PartitionSpec as P

CAP = 2
META = 8
AXES = ("fx", "fy")
F32 = jnp.float32
BF16 = jnp.bfloat16
VMEM_LIMIT = 40 * 1024 * 1024
NT = (((1,), (1,)), ((), ()))


def smem():
    return pl.BlockSpec(memory_space=pltpu.SMEM)


def vmem():
    return pl.BlockSpec(memory_space=pltpu.VMEM)


def hbm():
    return pl.BlockSpec(memory_space=pl.ANY)


def params():
    return pltpu.CompilerParams(vmem_limit_bytes=VMEM_LIMIT)


def in_hbm(x):
    return pltpu.with_memory_space_constraint(x, pltpu.HBM)


def log2(count):
    assert count & (count - 1) == 0
    return count.bit_length() - 1


def lane_iota(shape):
    return lax.broadcasted_iota(jnp.int32, shape, len(shape) - 1)


def row_pair_weights(taps_ref, weights_ref):
    _, columns, chans, _ = taps_ref.shape
    none = jnp.zeros((chans, chans), BF16)
    for q in range(4):
        for d in range(columns):
            upper = taps_ref[q, d] if q < 3 else none
            lower = taps_ref[q - 1, d] if q > 0 else none
            weights_ref[q * chans : (q + 1) * chans, 2 * d * chans : 2 * (d + 1) * chans] = (
                jnp.concatenate([upper, lower], axis=1)
            )


def forward_kernel(
    n_fy,
    dev_hbm,
    pos_hbm,
    fwd_hbm,
    back_hbm,
    x_hbm,
    table_hbm,
    k1_hbm,
    k2_hbm,
    send_ref,
    return_hbm,
    w1_ref,
    w2_ref,
    dev_ref,
    pos_ref,
    fwd_ref,
    back_ref,
    return_ref,
    x_ref,
    table_ref,
    taps_ref,
    rows_ref,
    edge_ref,
    meta_ref,
    count_ref,
    code_sem,
    x_sem,
    table_sem,
    taps_sem,
    return_sem,
):
    blocks, width = x_ref.shape
    tables, seg, _ = table_ref.shape
    chans = width // seg
    devices = count_ref.shape[0]
    assert n_fy == 1 << log2(n_fy)
    parts = x_sem.shape[0]
    wide = width // parts
    pieces = table_sem.shape[0]
    deep = tables // pieces
    x_copies = [
        pltpu.make_async_copy(
            x_hbm.at[:, pl.ds(q * wide, wide)], x_ref.at[:, pl.ds(q * wide, wide)], x_sem.at[q]
        )
        for q in range(parts)
    ]
    table_copies = [
        pltpu.make_async_copy(
            table_hbm.at[pl.ds(q * deep, deep)], table_ref.at[pl.ds(q * deep, deep)], table_sem.at[q]
        )
        for q in range(pieces)
    ]
    code_copies = [
        pltpu.make_async_copy(source, target, code_sem.at[n])
        for n, (source, target) in enumerate(
            ((dev_hbm, dev_ref), (pos_hbm, pos_ref), (fwd_hbm, fwd_ref), (back_hbm, back_ref))
        )
    ]
    taps_copies = [
        pltpu.make_async_copy(source, taps_ref.at[n], taps_sem.at[n])
        for n, source in enumerate((k1_hbm, k2_hbm))
    ]
    for copy in code_copies + x_copies + taps_copies + table_copies:
        copy.start()

    def clear(d, carry):
        count_ref[d] = 0
        return carry

    lax.fori_loop(0, devices, clear, 0, unroll=8)
    meta_ref[...] = jnp.zeros_like(meta_ref)
    for q, copy in enumerate(x_copies):
        copy.wait()
        for c in range(q * wide // seg, (q + 1) * wide // seg):
            rows_ref[c * blocks : (c + 1) * blocks, :] = x_ref[:, c * seg : (c + 1) * seg].astype(F32)
    for n, (copy, weights_ref) in enumerate(zip(taps_copies, (w1_ref, w2_ref))):
        copy.wait()
        row_pair_weights(taps_ref.at[n], weights_ref)
    for q, copy in enumerate(table_copies):
        copy.wait()

        def edges(n, carry):
            edge_ref[n, 0:2, :] = table_ref[n, seg - 16 : seg, :].astype(F32)[14:16, :]
            edge_ref[n, 2:4, :] = table_ref[n, 0:16, :].astype(F32)[0:2, :]
            return carry

        lax.fori_loop(q * deep, (q + 1) * deep, edges, 0, unroll=4)
    for copy in code_copies:
        copy.wait()
    lane = lane_iota((1, seg))

    def one_block(b, carry):
        tables_of = [fwd_ref[t, b] for t in range(2)]
        x = rows_ref[pl.ds(b, chans, stride=blocks), :].astype(BF16)
        weights = jnp.concatenate([table_ref[n] for n in tables_of], axis=0)
        product = lax.dot_general(x, weights, NT, preferred_element_type=F32)
        tips = jnp.concatenate([edge_ref[n] for n in tables_of], axis=0).astype(BF16)
        ends = lax.dot_general(tips, x, NT, preferred_element_type=F32)
        ends = jnp.concatenate([ends, ends], axis=1)
        for t in range(2):
            dev = dev_ref[t, b]
            pos = (pos_ref[t, b] + 1).astype(F32)
            rank = count_ref[dev]
            count_ref[dev] = rank + 1
            return_ref[t, b] = ((dev * CAP + rank) << log2(tables)) + back_ref[t, b]
            at = pl.multiple_of(rank * chans, chans)
            send_ref[dev, pl.ds(at, chans), :] = product[:, t * seg : (t + 1) * seg].astype(BF16)
            meta_ref[dev, pl.ds(4 + rank, 1), :] = jnp.full((1, seg), pos, F32)
            col = dev & (n_fy - 1)
            mine = (lane >= chans) == (rank == 1)
            for side in range(2):
                inside = (col < n_fy - 1) if side == 0 else (col > 0)
                near = jnp.where(inside, dev + 1 - 2 * side, devices)
                first = t * 4 + side * 2
                meta_ref[near, pl.ds(2 * side + rank, 1), :] = jnp.where(
                    lane < chans, ends[first : first + 1, :], ends[first + 1 : first + 2, :]
                )
                old = meta_ref[near, 6 + side : 7 + side, :]
                meta_ref[near, 6 + side : 7 + side, :] = jnp.where(mine, pos, old)
        return carry

    lax.fori_loop(0, blocks, one_block, 0, unroll=True)
    send_ref[:, CAP * chans :, :] = meta_ref[0:devices].astype(BF16)
    return_copy = pltpu.make_async_copy(return_ref, return_hbm, return_sem)
    return_copy.start()
    return_copy.wait()


def forward_remap(
    dest_dev, dest_pos, fwd_id, back_id, ll_blocks, fwd_table, k1, k2, devices, n_fy
):
    blocks, width = ll_blocks.shape
    tables, seg, _ = fwd_table.shape
    chans = width // seg
    return pl.pallas_call(
        functools.partial(forward_kernel, n_fy),
        out_shape=(
            jax.ShapeDtypeStruct((devices, CAP * chans + META, seg), BF16),
            jax.ShapeDtypeStruct((2, blocks), jnp.int32),
            jax.ShapeDtypeStruct((4 * chans, 6 * chans), BF16),
            jax.ShapeDtypeStruct((4 * chans, 6 * chans), BF16),
        ),
        in_specs=[hbm()] * 8,
        out_specs=(vmem(), hbm(), vmem(), vmem()),
        scratch_shapes=[
            pltpu.SMEM((2, blocks), jnp.int32),
            pltpu.SMEM((2, blocks), jnp.int32),
            pltpu.SMEM((2, blocks), jnp.int32),
            pltpu.SMEM((2, blocks), jnp.int32),
            pltpu.SMEM((2, blocks), jnp.int32),
            pltpu.VMEM((blocks, width), BF16),
            pltpu.VMEM((tables, seg, seg), BF16),
            pltpu.VMEM((2,) + k1.shape, BF16),
            pltpu.VMEM((chans * blocks, seg), F32),
            pltpu.VMEM((tables, 4, seg), F32),
            pltpu.VMEM((devices + 1, META, seg), F32),
            pltpu.SMEM((devices,), jnp.int32),
            pltpu.SemaphoreType.DMA((4,)),
            pltpu.SemaphoreType.DMA((4,)),
            pltpu.SemaphoreType.DMA((8,)),
            pltpu.SemaphoreType.DMA((2,)),
            pltpu.SemaphoreType.DMA,
        ],
        compiler_params=params(),
    )(
        *(in_hbm(route.T) for route in (dest_dev, dest_pos, fwd_id, back_id)),
        *(in_hbm(x) for x in (ll_blocks, fwd_table, k1, k2)),
    )


def sum_kernel(
    got_ref,
    field_ref,
    up_ref,
    down_ref,
    side_ref,
    pos_ref,
    rows_ref,
    sum_ref,
    spot_ref,
    spot_sem,
):
    devices, _, cols = got_ref.shape
    hblocks, chans, _ = field_ref.shape
    pairs = hblocks // 2
    lanes = 2 * chans
    rows_ref[...] = got_ref[:, CAP * chans :, :].reshape(devices * META, lanes).astype(F32)

    def meta_row(n):
        return rows_ref[pl.ds(n, devices, stride=META), :]

    lane = lane_iota((devices, lanes))
    table = jnp.where(lane % 2 == 0, meta_row(4), meta_row(5))
    beside = [meta_row(6), meta_row(7)]
    for side in range(2):
        turned_half = pltpu.roll(beside[side], chans, axis=1)
        for rank in range(CAP):
            here = lane == 2 + 2 * side + rank
            table = jnp.where(here, beside[side] if rank == 0 else turned_half, table)
    spots = table.T[0:8, :].astype(jnp.int32) - 1
    pos_ref[...] = spots
    spot_copy = pltpu.make_async_copy(pos_ref, spot_ref, spot_sem)
    spot_copy.start()

    def clear(r, carry):
        for rank in range(CAP):
            sum_ref[rank, r] = jnp.zeros((chans, cols), F32)
        return carry

    lax.fori_loop(0, hblocks, clear, 0, unroll=4)
    block = lax.broadcasted_iota(jnp.int32, (pairs, devices), 0)
    low = lane_iota((pairs, lanes)) < chans
    for side in range(2):
        sums = []
        for parity in range(2):
            total = jnp.zeros((pairs, lanes), F32)
            for rank in range(CAP):
                n = 2 + 2 * side + rank
                hit = (spots[n : n + 1, :] == 2 * block + parity).astype(F32).astype(BF16)
                total += jnp.dot(
                    hit, meta_row(2 * side + rank).astype(BF16), preferred_element_type=F32
                )
            sums.append(total)
        even, odd = sums
        side_ref[2 * side] = jnp.where(low, even, pltpu.roll(odd, chans, axis=1))
        side_ref[2 * side + 1] = jnp.where(low, pltpu.roll(even, chans, axis=1), odd)
    spot_copy.wait()

    def add(d, carry):
        for rank in range(CAP):
            pos = spot_ref[rank, d]
            row = jnp.where(pos < 0, hblocks, pos)
            block = got_ref[d, rank * chans : (rank + 1) * chans, :]
            sum_ref[rank, row] = sum_ref[rank, row] + block.astype(F32)
        return carry

    lax.fori_loop(0, devices, add, 0, unroll=16)

    def total_of(r):
        return sum_ref[0, r] + sum_ref[1, r]

    corners = jnp.zeros((up_ref.shape[0] - cols, lanes), F32)
    corner_row = lax.broadcasted_iota(jnp.int32, corners.shape, 0)
    for ref, g in ((up_ref, 0), (down_ref, pairs - 1)):
        ref[0:cols, :] = jnp.concatenate([total_of(2 * g), total_of(2 * g + 1)], axis=0).T.astype(BF16)
        rest = corners
        for n in range(4):
            rest = jnp.where(corner_row == n, side_ref[n, g : g + 1, :], rest)
        ref[cols:, :] = rest.astype(BF16)

    def finish(r, carry):
        field_ref[r] = total_of(r).astype(BF16)
        return carry

    lax.fori_loop(0, hblocks, finish, 0, unroll=4)


def sum_field(got, hblocks):
    devices, depth, cols = got.shape
    chans = (depth - META) // CAP
    pairs = hblocks // 2
    message = jax.ShapeDtypeStruct((cols + 16, 2 * chans), BF16)
    return pl.pallas_call(
        sum_kernel,
        out_shape=(
            jax.ShapeDtypeStruct((hblocks, chans, cols), BF16),
            message,
            message,
            jax.ShapeDtypeStruct((4, pairs, 2 * chans), F32),
            jax.ShapeDtypeStruct((8, devices), jnp.int32),
        ),
        in_specs=[vmem()],
        out_specs=(vmem(),) * 5,
        scratch_shapes=[
            pltpu.VMEM((devices * META, cols), F32),
            pltpu.VMEM((CAP, hblocks + 1, chans, cols), F32),
            pltpu.SMEM((8, devices), jnp.int32),
            pltpu.SemaphoreType.DMA,
        ],
        compiler_params=params(),
    )(got)


def gelu(x):
    return 0.5 * x * (1.0 + jnp.tanh(0.7978845608028654 * (x + 0.044715 * (x * x * x))))


def taps(x, weights_ref, d):
    lanes = x.shape[1] // 2
    return jnp.dot(x, weights_ref[:, d * lanes : (d + 1) * lanes], preferred_element_type=F32)


def row_pair_conv(upper, lower, weights_ref, bias, before, after):
    cols, lanes = upper.shape
    rows = jnp.concatenate([upper, lower], axis=1)
    product = jnp.dot(rows, weights_ref[...], preferred_element_type=F32)
    column = lax.broadcasted_iota(jnp.int32, (cols, lanes), 0)
    ahead = pltpu.roll(product[:, 0:lanes], 1, axis=0)
    behind = pltpu.roll(product[:, 2 * lanes :], cols - 1, axis=0)
    ahead = jnp.where(column == 0, before, ahead)
    behind = jnp.where(column == cols - 1, after, behind)
    return product[:, lanes : 2 * lanes] + ahead + behind + bias


def twice(bias_ref):
    return jnp.concatenate([bias_ref[...], bias_ref[...]], axis=1)


def inner_kernel(field_ref, side_ref, k1_ref, b1_ref, turned_ref, hid_ref, halo_ref):
    hblocks, chans, cols = field_ref.shape
    pairs = hblocks // 2

    def turn(g, carry):
        turned_ref[g] = field_ref[pl.ds(2 * g, 2)].reshape(2 * chans, cols).T
        return carry

    lax.fori_loop(0, pairs, turn, 0, unroll=4)
    b1 = twice(b1_ref)
    for n, (k, d) in enumerate(((1, 0), (2, 2))):
        both = jnp.concatenate([side_ref[k, 0 : pairs - 1, :], side_ref[k, 1:pairs, :]], axis=1)
        halo_ref[n, 1:pairs, :] = taps(both.astype(BF16), k1_ref, d)

    def first(g, carry):
        out = row_pair_conv(
            turned_ref[g - 1],
            turned_ref[g],
            k1_ref,
            b1,
            halo_ref[0, pl.ds(g, 1), :],
            halo_ref[1, pl.ds(g, 1), :],
        )
        hid_ref[g] = gelu(out).astype(BF16)
        return carry

    lax.fori_loop(1, pairs, first, 0, unroll=True)


def inner_hidden(field, sides, k1, b1):
    hblocks, chans, cols = field.shape
    pairs = hblocks // 2
    shape = jax.ShapeDtypeStruct((pairs, cols, 2 * chans), BF16)
    return pl.pallas_call(
        inner_kernel,
        out_shape=(shape, shape),
        in_specs=[vmem()] * 4,
        out_specs=(vmem(), vmem()),
        scratch_shapes=[pltpu.VMEM((2, pairs + 8, 2 * chans), F32)],
        compiler_params=params(),
        cost_estimate=pl.CostEstimate(
            flops=2 * 8192 * 9 * 64 * 64, bytes_accessed=4 << 20, transcendentals=1 << 19
        ),
    )(field, sides, k1, b1)


def outer_kernel(
    pos_hbm,
    place_ref,
    field_ref,
    hid_ref,
    sides_ref,
    above_ref,
    below_ref,
    k1_ref,
    b1_ref,
    k2_ref,
    b2_ref,
    send_ref,
    side_ref,
    halo_ref,
    state_ref,
    pos_ref,
    pos_sem,
):
    pos_copy = pltpu.make_async_copy(pos_hbm, pos_ref, pos_sem)
    pos_copy.start()
    pairs, cols, lanes = field_ref.shape
    chans = lanes // 2
    devices = pos_ref.shape[1]
    groups = pairs + 1
    above = above_ref[cols:, :].astype(F32)
    below = below_ref[cols:, :].astype(F32)
    for n, k in enumerate((0, 1, 4, 5)):
        side_ref[k, 0:1, :] = above[n : n + 1, :]
        side_ref[k, 1 : pairs + 1, :] = sides_ref[n]
        side_ref[k, pairs + 1 : pairs + 2, :] = below[n : n + 1, :]

    def ends(block):
        return (
            block[0:16, :].astype(F32)[0:1, :],
            block[cols - 16 : cols, :].astype(F32)[15:16, :],
        )

    for k, (high, low) in enumerate(zip(ends(above_ref[0:cols, :]), ends(below_ref[0:cols, :]))):
        side_ref[2 + k, 0:1, :] = high
        side_ref[2 + k, pairs + 1 : pairs + 2, :] = low

    def inner_side(g, carry):
        for k, end in enumerate(ends(field_ref[g])):
            side_ref[2 + k, pl.ds(g + 1, 1), :] = end
        return carry

    lax.fori_loop(0, pairs, inner_side, 0, unroll=4)

    def paired(k):
        return jnp.concatenate(
            [side_ref[k, 0:groups, :], side_ref[k, 1 : groups + 1, :]], axis=1
        ).astype(BF16)

    b1 = twice(b1_ref)
    b2 = twice(b2_ref)
    c = [paired(k) for k in range(6)]
    left = taps(c[1], k1_ref, 0)
    right = taps(c[4], k1_ref, 2)
    before = taps(c[0], k1_ref, 0) + taps(c[1], k1_ref, 1) + taps(c[2], k1_ref, 2) + b1
    after = taps(c[3], k1_ref, 0) + taps(c[4], k1_ref, 1) + taps(c[5], k1_ref, 2) + b1
    before = jnp.where(place_ref[0:1, :] > 0, gelu(before), 0.0)
    after = jnp.where(place_ref[1:2, :] > 0, gelu(after), 0.0)
    for n, (column, d) in enumerate(((before, 0), (after, 2))):
        side_ref[n, 0:groups, :] = column
        both = jnp.concatenate([side_ref[n, 0:pairs, :], side_ref[n, 1 : pairs + 1, :]], axis=1)
        halo_ref[n, 0:pairs, :] = taps(both.astype(BF16), k2_ref, d)

    def hidden(upper, lower, g):
        out = row_pair_conv(upper, lower, k1_ref, b1, left[g : g + 1, :], right[g : g + 1, :])
        return gelu(out).astype(BF16)

    def second(g, upper, lower):
        out = row_pair_conv(
            upper, lower, k2_ref, b2, halo_ref[0, pl.ds(g, 1), :], halo_ref[1, pl.ds(g, 1), :]
        )
        state = out + field_ref[g].astype(F32)
        state_ref[pl.ds(2 * g, 2)] = state.T.astype(BF16).reshape(2, chans, cols)

    second(0, hidden(above_ref[0:cols, :], field_ref[0], 0), hid_ref[1])
    second(pairs - 1, hid_ref[pairs - 1], hidden(field_ref[pairs - 1], below_ref[0:cols, :], pairs))

    def inner(g, carry):
        second(g, hid_ref[g], hid_ref[g + 1])
        return carry

    lax.fori_loop(1, pairs - 1, inner, 0, unroll=True)
    pos_copy.wait()

    def pick(d, carry):
        for rank in range(CAP):
            pos = jnp.maximum(pos_ref[rank, d], 0)
            send_ref[d, rank * chans : (rank + 1) * chans, :] = state_ref[pos]
        return carry

    lax.fori_loop(0, devices, pick, 0, unroll=16)


def outer_state(positions, place, field, hidden, sides, above, below, k1, b1, k2, b2):
    pairs, cols, lanes = field.shape
    chans = lanes // 2
    devices = positions.shape[1]
    return pl.pallas_call(
        outer_kernel,
        out_shape=jax.ShapeDtypeStruct((devices, CAP * chans, cols), BF16),
        in_specs=[vmem()] * 11,
        out_specs=vmem(),
        scratch_shapes=[
            pltpu.VMEM((6, pairs + 8, lanes), F32),
            pltpu.VMEM((2, pairs + 8, lanes), F32),
            pltpu.VMEM((2 * pairs, chans, cols), BF16),
            pltpu.SMEM(positions.shape, jnp.int32),
            pltpu.SemaphoreType.DMA,
        ],
        compiler_params=params(),
    )(positions, place, field, hidden, sides, above, below, k1, b1, k2, b2)


def backward_kernel(
    return_hbm,
    got_ref,
    table_ref,
    out_hbm,
    return_ref,
    rows_ref,
    out_ref,
    return_sem,
    out_sem,
):
    blocks, width = out_hbm.shape
    tables, seg, _ = table_ref.shape
    chans = width // seg
    parts = out_sem.shape[0]
    part = blocks // parts
    return_copy = pltpu.make_async_copy(return_hbm, return_ref, return_sem)
    return_copy.start()
    return_copy.wait()
    out_copies = []

    def finish(q):
        piece = pl.ds(q * part, part)
        for c in range(chans):
            out_ref[piece, c * seg : (c + 1) * seg] = rows_ref[
                q, c * part : (c + 1) * part, :
            ].astype(BF16)
        out_copies.append(
            pltpu.make_async_copy(out_ref.at[piece], out_hbm.at[piece], out_sem.at[q])
        )
        out_copies[-1].start()

    for q in range(parts):
        if q > 0:
            finish(q - 1)
        for n in range(part):
            states, weights = [], []
            for t in range(2):
                code = return_ref[t, q * part + n]
                slot = code >> log2(tables)
                at = pl.multiple_of((slot & 1) * chans, chans)
                states.append(got_ref[slot >> 1, pl.ds(at, chans), :])
                weights.append(table_ref[code & (tables - 1)])
            rows_ref[q, pl.ds(n, chans, stride=part), :] = lax.dot_general(
                jnp.concatenate(states, axis=1),
                jnp.concatenate(weights, axis=1),
                NT,
                preferred_element_type=F32,
            )
    finish(parts - 1)
    for copy in out_copies:
        copy.wait()


def backward_remap(returns, got, back_table):
    blocks = returns.shape[1]
    chans = got.shape[1] // CAP
    seg = got.shape[2]
    parts = 4
    return pl.pallas_call(
        backward_kernel,
        out_shape=jax.ShapeDtypeStruct((blocks, chans * seg), BF16),
        in_specs=[hbm(), vmem(), vmem()],
        out_specs=hbm(),
        scratch_shapes=[
            pltpu.SMEM(returns.shape, jnp.int32),
            pltpu.VMEM((parts, chans * blocks // parts, seg), F32),
            pltpu.VMEM((blocks, chans * seg), BF16),
            pltpu.SemaphoreType.DMA,
            pltpu.SemaphoreType.DMA((parts,)),
        ],
        compiler_params=params(),
    )(returns, got, back_table)


def exchange(buffer):
    return lax.all_to_all(buffer, AXES, split_axis=0, concat_axis=0, tiled=True)


def local(
    ll_blocks,
    dest_dev,
    dest_pos,
    fwd_id,
    back_id,
    fwd_table,
    back_table,
    kernel_one,
    bias_one,
    kernel_two,
    bias_two,
):
    n_fx = lax.axis_size("fx")
    n_fy = lax.axis_size("fy")
    hblocks = 64
    j = lax.axis_index("fy")
    place = jnp.stack([j > 0, j < n_fy - 1]).astype(jnp.int32)[:, None]
    place = jnp.broadcast_to(place, (2, 128))
    send, returns, w1, w2 = forward_remap(
        dest_dev,
        dest_pos,
        fwd_id,
        back_id,
        ll_blocks,
        fwd_table,
        kernel_one,
        kernel_two,
        n_fx * n_fy,
        n_fy,
    )
    send, place = lax.optimization_barrier((send, place))
    b1, b2 = bias_one[None], bias_two[None]
    field, up, down, sides, positions = sum_field(exchange(send), hblocks)
    above = lax.ppermute(down, "fx", [(i, (i + 1) % n_fx) for i in range(n_fx)])
    below = lax.ppermute(up, "fx", [((i + 1) % n_fx, i) for i in range(n_fx)])
    turned, hidden = inner_hidden(field, sides, w1, b1)
    send_back = outer_state(
        positions, place, turned, hidden, sides, above, below, w1, b1, w2, b2
    )
    return backward_remap(returns, exchange(send_back), back_table)


def solution(mesh):
    blocked = P(AXES, None)
    in_specs = (blocked,) * 5 + (P(),) * 6
    return jax.shard_map(
        local, mesh=mesh, in_specs=in_specs, out_specs=P(AXES, None), check_vma=False
    )
```

```python
import functools

import jax
import jax.numpy as jnp
from jax import lax
from jax.experimental import pallas as pl
from jax.experimental.pallas import tpu as pltpu
from jax.sharding import PartitionSpec as P

CAP = 2
PAD = 8
META = 8
AXES = ("fx", "fy")
F32 = jnp.float32
BF16 = jnp.bfloat16
VMEM_LIMIT = 40 * 1024 * 1024
NT = (((1,), (1,)), ((), ()))


def smem():
    return pl.BlockSpec(memory_space=pltpu.SMEM)


def vmem():
    return pl.BlockSpec(memory_space=pltpu.VMEM)


def hbm():
    return pl.BlockSpec(memory_space=pl.ANY)


def params():
    return pltpu.CompilerParams(vmem_limit_bytes=VMEM_LIMIT)


def in_hbm(x):
    return pltpu.with_memory_space_constraint(x, pltpu.HBM)


def log2(count):
    assert count & (count - 1) == 0
    return count.bit_length() - 1


def lane_iota(shape):
    return lax.broadcasted_iota(jnp.int32, shape, len(shape) - 1)


def row_pair_weights(taps_ref, weights_ref):
    _, columns, chans, _ = taps_ref.shape
    none = jnp.zeros((chans, chans), BF16)
    for q in range(4):
        for d in range(columns):
            upper = taps_ref[q, d] if q < 3 else none
            lower = taps_ref[q - 1, d] if q > 0 else none
            weights_ref[q * chans : (q + 1) * chans, 2 * d * chans : 2 * (d + 1) * chans] = (
                jnp.concatenate([upper, lower], axis=1)
            )


def forward_kernel(
    n_fy,
    dev_hbm,
    pos_hbm,
    fwd_hbm,
    back_hbm,
    x_hbm,
    table_hbm,
    k1_hbm,
    k2_hbm,
    send_ref,
    return_hbm,
    w1_ref,
    w2_ref,
    dev_ref,
    pos_ref,
    fwd_ref,
    back_ref,
    return_ref,
    x_ref,
    table_ref,
    taps_ref,
    rows_ref,
    edge_ref,
    meta_ref,
    count_ref,
    code_sem,
    x_sem,
    table_sem,
    taps_sem,
    return_sem,
):
    blocks, width = x_ref.shape
    tables, seg, _ = table_ref.shape
    chans = width // seg
    devices = count_ref.shape[0]
    assert n_fy == 1 << log2(n_fy)
    parts = x_sem.shape[0]
    wide = width // parts
    step = rows_ref.shape[0] // chans
    pieces = table_sem.shape[0]
    deep = tables // pieces
    x_copies = [
        pltpu.make_async_copy(
            x_hbm.at[:, pl.ds(q * wide, wide)], x_ref.at[:, pl.ds(q * wide, wide)], x_sem.at[q]
        )
        for q in range(parts)
    ]
    table_copies = [
        pltpu.make_async_copy(
            table_hbm.at[pl.ds(q * deep, deep)], table_ref.at[pl.ds(q * deep, deep)], table_sem.at[q]
        )
        for q in range(pieces)
    ]
    code_copies = [
        pltpu.make_async_copy(source, target, code_sem.at[n])
        for n, (source, target) in enumerate(
            ((dev_hbm, dev_ref), (pos_hbm, pos_ref), (fwd_hbm, fwd_ref), (back_hbm, back_ref))
        )
    ]
    taps_copies = [
        pltpu.make_async_copy(source, taps_ref.at[n], taps_sem.at[n])
        for n, source in enumerate((k1_hbm, k2_hbm))
    ]
    for copy in code_copies + x_copies + taps_copies + table_copies:
        copy.start()

    def clear(d, carry):
        count_ref[d] = 0
        return carry

    lax.fori_loop(0, devices, clear, 0, unroll=8)
    meta_ref[...] = jnp.zeros_like(meta_ref)
    for copy in code_copies:
        copy.wait()

    def plan(b, carry):
        for t in range(2):
            dev = dev_ref[t, b]
            rank = count_ref[dev]
            count_ref[dev] = rank + 1
            return_ref[t, b] = ((dev * CAP + rank) << log2(tables)) + back_ref[t, b]
            pos = (pos_ref[t, b] + 1).astype(F32)
            meta_ref[pl.ds(dev * META + 4 + rank, 1), :] = jnp.full((1, seg), pos, F32)
        return carry

    lax.fori_loop(0, blocks, plan, 0, unroll=8)
    return_copy = pltpu.make_async_copy(return_ref, return_hbm, return_sem)
    return_copy.start()
    both = jnp.where(
        lane_iota((devices, seg)) < chans,
        meta_ref[pl.ds(4, devices, stride=META), :],
        meta_ref[pl.ds(5, devices, stride=META), :],
    )
    col = lax.broadcasted_iota(jnp.int32, both.shape, 0) & (n_fy - 1)
    meta_ref[pl.ds(6, devices, stride=META), :] = jnp.where(
        col > 0, pltpu.roll(both, 1, axis=0), 0.0
    )
    meta_ref[pl.ds(7, devices, stride=META), :] = jnp.where(
        col < n_fy - 1, pltpu.roll(both, devices - 1, axis=0), 0.0
    )
    for q, copy in enumerate(x_copies):
        copy.wait()
        for c in range(q * wide // seg, (q + 1) * wide // seg):
            rows_ref[c * step : c * step + blocks, :] = x_ref[:, c * seg : (c + 1) * seg].astype(F32)
    for n, (copy, weights_ref) in enumerate(zip(taps_copies, (w1_ref, w2_ref))):
        copy.wait()
        row_pair_weights(taps_ref.at[n], weights_ref)
    for q, copy in enumerate(table_copies):
        copy.wait()

        def edges(n, carry):
            edge_ref[n, 0:2, :] = table_ref[n, seg - 16 : seg, :].astype(F32)[14:16, :]
            edge_ref[n, 2:4, :] = table_ref[n, 0:16, :].astype(F32)[0:2, :]
            return carry

        lax.fori_loop(q * deep, (q + 1) * deep, edges, 0, unroll=4)
    lane = lane_iota((1, seg))

    def one_block(b, carry):
        tables_of = [fwd_ref[t, b] for t in range(2)]
        x = rows_ref[pl.ds(b, chans, stride=step), :].astype(BF16)
        weights = jnp.concatenate([table_ref[n] for n in tables_of], axis=0)
        product = lax.dot_general(x, weights, NT, preferred_element_type=F32)
        tips = jnp.concatenate([edge_ref[n] for n in tables_of], axis=0).astype(BF16)
        ends = lax.dot_general(tips, x, NT, preferred_element_type=F32)
        ends = jnp.concatenate([ends, ends], axis=1)
        for t in range(2):
            slot = return_ref[t, b] >> log2(tables)
            dev, rank = slot >> 1, slot & 1
            at = pl.multiple_of(rank * chans, chans)
            send_ref[dev, pl.ds(at, chans), :] = product[:, t * seg : (t + 1) * seg].astype(BF16)
            col = dev & (n_fy - 1)
            for side in range(2):
                inside = (col < n_fy - 1) if side == 0 else (col > 0)
                near = jnp.where(inside, dev + 1 - 2 * side, devices)
                first = t * 4 + side * 2
                meta_ref[pl.ds(near * META + 2 * side + rank, 1), :] = jnp.where(
                    lane < chans, ends[first : first + 1, :], ends[first + 1 : first + 2, :]
                )
        return carry

    lax.fori_loop(0, blocks, one_block, 0, unroll=True)
    send_ref[:, CAP * chans :, :] = (
        meta_ref[0 : devices * META, :].astype(BF16).reshape(devices, META, seg)
    )
    return_copy.wait()


def forward_remap(
    dest_dev, dest_pos, fwd_id, back_id, ll_blocks, fwd_table, k1, k2, devices, n_fy
):
    blocks, width = ll_blocks.shape
    tables, seg, _ = fwd_table.shape
    chans = width // seg
    return pl.pallas_call(
        functools.partial(forward_kernel, n_fy),
        out_shape=(
            jax.ShapeDtypeStruct((devices, CAP * chans + META, seg), BF16),
            jax.ShapeDtypeStruct((2, blocks), jnp.int32),
            jax.ShapeDtypeStruct((4 * chans, 6 * chans), BF16),
            jax.ShapeDtypeStruct((4 * chans, 6 * chans), BF16),
        ),
        in_specs=[hbm()] * 8,
        out_specs=(vmem(), hbm(), vmem(), vmem()),
        scratch_shapes=[
            pltpu.SMEM((2, blocks), jnp.int32),
            pltpu.SMEM((2, blocks), jnp.int32),
            pltpu.SMEM((2, blocks), jnp.int32),
            pltpu.SMEM((2, blocks), jnp.int32),
            pltpu.SMEM((2, blocks), jnp.int32),
            pltpu.VMEM((blocks, width), BF16),
            pltpu.VMEM((tables, seg, seg), BF16),
            pltpu.VMEM((2,) + k1.shape, BF16),
            pltpu.VMEM((chans * (blocks + PAD), seg), F32),
            pltpu.VMEM((tables, 4, seg), F32),
            pltpu.VMEM(((devices + 1) * META, seg), F32),
            pltpu.SMEM((devices,), jnp.int32),
            pltpu.SemaphoreType.DMA((4,)),
            pltpu.SemaphoreType.DMA((4,)),
            pltpu.SemaphoreType.DMA((8,)),
            pltpu.SemaphoreType.DMA((2,)),
            pltpu.SemaphoreType.DMA,
        ],
        compiler_params=params(),
    )(
        *(in_hbm(route.T) for route in (dest_dev, dest_pos, fwd_id, back_id)),
        *(in_hbm(x) for x in (ll_blocks, fwd_table, k1, k2)),
    )


def sum_kernel(
    got_ref,
    field_ref,
    up_ref,
    down_ref,
    side_ref,
    pos_ref,
    rows_ref,
    sum_ref,
    spot_ref,
    spot_sem,
):
    devices, _, cols = got_ref.shape
    hblocks, chans, _ = field_ref.shape
    pairs = hblocks // 2
    lanes = 2 * chans
    rows_ref[...] = got_ref[:, CAP * chans :, :].reshape(devices * META, lanes).astype(F32)

    def meta_row(n):
        return rows_ref[pl.ds(n, devices, stride=META), :]

    lane = lane_iota((devices, lanes))
    table = jnp.where(lane % 2 == 0, meta_row(4), meta_row(5))
    beside = [meta_row(6), meta_row(7)]
    for side in range(2):
        turned_half = pltpu.roll(beside[side], chans, axis=1)
        for rank in range(CAP):
            here = lane == 2 + 2 * side + rank
            table = jnp.where(here, beside[side] if rank == 0 else turned_half, table)
    spots = table.T[0:8, :].astype(jnp.int32) - 1
    pos_ref[...] = spots
    spot_copy = pltpu.make_async_copy(pos_ref, spot_ref, spot_sem)
    spot_copy.start()

    def clear(r, carry):
        for rank in range(CAP):
            sum_ref[rank, r] = jnp.zeros((chans, cols), F32)
        return carry

    lax.fori_loop(0, hblocks, clear, 0, unroll=4)
    block = lax.broadcasted_iota(jnp.int32, (pairs, devices), 0)
    low = lane_iota((pairs, lanes)) < chans
    for side in range(2):
        sums = []
        for parity in range(2):
            total = jnp.zeros((pairs, lanes), F32)
            for rank in range(CAP):
                n = 2 + 2 * side + rank
                hit = (spots[n : n + 1, :] == 2 * block + parity).astype(F32).astype(BF16)
                total += jnp.dot(
                    hit, meta_row(2 * side + rank).astype(BF16), preferred_element_type=F32
                )
            sums.append(total)
        even, odd = sums
        side_ref[2 * side] = jnp.where(low, even, pltpu.roll(odd, chans, axis=1))
        side_ref[2 * side + 1] = jnp.where(low, pltpu.roll(even, chans, axis=1), odd)
    spot_copy.wait()

    def add(d, carry):
        for rank in range(CAP):
            pos = spot_ref[rank, d]
            row = jnp.where(pos < 0, hblocks, pos)
            block = got_ref[d, rank * chans : (rank + 1) * chans, :]
            sum_ref[rank, row] = sum_ref[rank, row] + block.astype(F32)
        return carry

    lax.fori_loop(0, devices, add, 0, unroll=16)

    def total_of(r):
        return sum_ref[0, r] + sum_ref[1, r]

    corners = jnp.zeros((up_ref.shape[0] - cols, lanes), F32)
    corner_row = lax.broadcasted_iota(jnp.int32, corners.shape, 0)
    for ref, g in ((up_ref, 0), (down_ref, pairs - 1)):
        ref[0:cols, :] = jnp.concatenate([total_of(2 * g), total_of(2 * g + 1)], axis=0).T.astype(BF16)
        rest = corners
        for n in range(4):
            rest = jnp.where(corner_row == n, side_ref[n, g : g + 1, :], rest)
        ref[cols:, :] = rest.astype(BF16)

    def finish(r, carry):
        field_ref[r] = total_of(r).astype(BF16)
        return carry

    lax.fori_loop(0, hblocks, finish, 0, unroll=4)


def sum_field(got, hblocks):
    devices, depth, cols = got.shape
    chans = (depth - META) // CAP
    pairs = hblocks // 2
    message = jax.ShapeDtypeStruct((cols + 16, 2 * chans), BF16)
    return pl.pallas_call(
        sum_kernel,
        out_shape=(
            jax.ShapeDtypeStruct((hblocks, chans, cols), BF16),
            message,
            message,
            jax.ShapeDtypeStruct((4, pairs, 2 * chans), F32),
            jax.ShapeDtypeStruct((8, devices), jnp.int32),
        ),
        in_specs=[vmem()],
        out_specs=(vmem(),) * 5,
        scratch_shapes=[
            pltpu.VMEM((devices * META, cols), F32),
            pltpu.VMEM((CAP, hblocks + 1, chans, cols), F32),
            pltpu.SMEM((8, devices), jnp.int32),
            pltpu.SemaphoreType.DMA,
        ],
        compiler_params=params(),
    )(got)


def gelu(x):
    return 0.5 * x * (1.0 + jnp.tanh(0.7978845608028654 * (x + 0.044715 * (x * x * x))))


def taps(x, weights_ref, d):
    lanes = x.shape[1] // 2
    return jnp.dot(x, weights_ref[:, d * lanes : (d + 1) * lanes], preferred_element_type=F32)


def row_pair_conv(upper, lower, weights_ref, bias, before, after):
    cols, lanes = upper.shape
    rows = jnp.concatenate([upper, lower], axis=1)
    product = jnp.dot(rows, weights_ref[...], preferred_element_type=F32)
    ahead = pltpu.roll(product[:, 0:lanes], 1, axis=0)
    behind = pltpu.roll(product[:, 2 * lanes :], cols - 1, axis=0)
    edge = lax.broadcasted_iota(jnp.int32, (8, lanes), 0)
    first = jnp.where(edge == 0, before, ahead[0:8, :])
    last = jnp.where(edge == 7, after, behind[cols - 8 :, :])
    ahead = jnp.concatenate([first, ahead[8:, :]], axis=0)
    behind = jnp.concatenate([behind[: cols - 8, :], last], axis=0)
    return product[:, lanes : 2 * lanes] + ahead + behind + bias


def twice(bias_ref):
    return jnp.concatenate([bias_ref[...], bias_ref[...]], axis=1)


def inner_kernel(field_ref, side_ref, k1_ref, b1_ref, turned_ref, hid_ref, halo_ref):
    hblocks, chans, cols = field_ref.shape
    pairs = hblocks // 2

    def turn(g, carry):
        turned_ref[g] = field_ref[pl.ds(2 * g, 2)].reshape(2 * chans, cols).T
        return carry

    lax.fori_loop(0, pairs, turn, 0, unroll=True)
    b1 = twice(b1_ref)
    for n, (k, d) in enumerate(((1, 0), (2, 2))):
        both = jnp.concatenate([side_ref[k, 0 : pairs - 1, :], side_ref[k, 1:pairs, :]], axis=1)
        halo_ref[n, 1:pairs, :] = taps(both.astype(BF16), k1_ref, d)

    def first(g, carry):
        out = row_pair_conv(
            turned_ref[g - 1],
            turned_ref[g],
            k1_ref,
            b1,
            halo_ref[0, pl.ds(g, 1), :],
            halo_ref[1, pl.ds(g, 1), :],
        )
        hid_ref[g] = gelu(out).astype(BF16)
        return carry

    lax.fori_loop(1, pairs, first, 0, unroll=True)


def inner_hidden(field, sides, k1, b1):
    hblocks, chans, cols = field.shape
    pairs = hblocks // 2
    shape = jax.ShapeDtypeStruct((pairs, cols, 2 * chans), BF16)
    return pl.pallas_call(
        inner_kernel,
        out_shape=(shape, shape),
        in_specs=[vmem()] * 4,
        out_specs=(vmem(), vmem()),
        scratch_shapes=[pltpu.VMEM((2, pairs + 8, 2 * chans), F32)],
        compiler_params=params(),
        cost_estimate=pl.CostEstimate(
            flops=2 * 8192 * 9 * 64 * 64, bytes_accessed=4 << 20, transcendentals=1 << 19
        ),
    )(field, sides, k1, b1)


def outer_kernel(
    pos_hbm,
    place_ref,
    field_ref,
    hid_ref,
    sides_ref,
    above_ref,
    below_ref,
    k1_ref,
    b1_ref,
    k2_ref,
    b2_ref,
    send_ref,
    side_ref,
    halo_ref,
    state_ref,
    pos_ref,
    pos_sem,
):
    pos_copy = pltpu.make_async_copy(pos_hbm, pos_ref, pos_sem)
    pos_copy.start()
    pairs, cols, lanes = field_ref.shape
    chans = lanes // 2
    devices = pos_ref.shape[1]
    groups = pairs + 1
    above = above_ref[cols:, :].astype(F32)
    below = below_ref[cols:, :].astype(F32)
    for n, k in enumerate((0, 1, 4, 5)):
        side_ref[k, 0:1, :] = above[n : n + 1, :]
        side_ref[k, 1 : pairs + 1, :] = sides_ref[n]
        side_ref[k, pairs + 1 : pairs + 2, :] = below[n : n + 1, :]

    def ends(block):
        return (
            block[0:16, :].astype(F32)[0:1, :],
            block[cols - 16 : cols, :].astype(F32)[15:16, :],
        )

    for k, (high, low) in enumerate(zip(ends(above_ref[0:cols, :]), ends(below_ref[0:cols, :]))):
        side_ref[2 + k, 0:1, :] = high
        side_ref[2 + k, pairs + 1 : pairs + 2, :] = low

    def inner_side(g, carry):
        for k, end in enumerate(ends(field_ref[g])):
            side_ref[2 + k, pl.ds(g + 1, 1), :] = end
        return carry

    lax.fori_loop(0, pairs, inner_side, 0, unroll=4)

    def paired(k):
        return jnp.concatenate(
            [side_ref[k, 0:groups, :], side_ref[k, 1 : groups + 1, :]], axis=1
        ).astype(BF16)

    b1 = twice(b1_ref)
    b2 = twice(b2_ref)
    c = [paired(k) for k in range(6)]
    left = taps(c[1], k1_ref, 0)
    right = taps(c[4], k1_ref, 2)
    before = taps(c[0], k1_ref, 0) + taps(c[1], k1_ref, 1) + taps(c[2], k1_ref, 2) + b1
    after = taps(c[3], k1_ref, 0) + taps(c[4], k1_ref, 1) + taps(c[5], k1_ref, 2) + b1
    before = jnp.where(place_ref[0:1, :] > 0, gelu(before), 0.0)
    after = jnp.where(place_ref[1:2, :] > 0, gelu(after), 0.0)
    for n, (column, d) in enumerate(((before, 0), (after, 2))):
        side_ref[n, 0:groups, :] = column
        both = jnp.concatenate([side_ref[n, 0:pairs, :], side_ref[n, 1 : pairs + 1, :]], axis=1)
        halo_ref[n, 0:pairs, :] = taps(both.astype(BF16), k2_ref, d)

    def hidden(upper, lower, g):
        out = row_pair_conv(upper, lower, k1_ref, b1, left[g : g + 1, :], right[g : g + 1, :])
        return gelu(out).astype(BF16)

    def second(g, upper, lower):
        out = row_pair_conv(
            upper, lower, k2_ref, b2, halo_ref[0, pl.ds(g, 1), :], halo_ref[1, pl.ds(g, 1), :]
        )
        state = out + field_ref[g].astype(F32)
        state_ref[pl.ds(2 * g, 2)] = state.T.astype(BF16).reshape(2, chans, cols)

    second(0, hidden(above_ref[0:cols, :], field_ref[0], 0), hid_ref[1])
    second(pairs - 1, hid_ref[pairs - 1], hidden(field_ref[pairs - 1], below_ref[0:cols, :], pairs))

    def inner(g, carry):
        second(g, hid_ref[g], hid_ref[g + 1])
        return carry

    lax.fori_loop(1, pairs - 1, inner, 0, unroll=True)
    pos_copy.wait()

    def pick(d, carry):
        for rank in range(CAP):
            pos = jnp.maximum(pos_ref[rank, d], 0)
            send_ref[d, rank * chans : (rank + 1) * chans, :] = state_ref[pos]
        return carry

    lax.fori_loop(0, devices, pick, 0, unroll=16)


def outer_state(positions, place, field, hidden, sides, above, below, k1, b1, k2, b2):
    pairs, cols, lanes = field.shape
    chans = lanes // 2
    devices = positions.shape[1]
    return pl.pallas_call(
        outer_kernel,
        out_shape=jax.ShapeDtypeStruct((devices, CAP * chans, cols), BF16),
        in_specs=[vmem()] * 11,
        out_specs=vmem(),
        scratch_shapes=[
            pltpu.VMEM((6, pairs + 8, lanes), F32),
            pltpu.VMEM((2, pairs + 8, lanes), F32),
            pltpu.VMEM((2 * pairs, chans, cols), BF16),
            pltpu.SMEM(positions.shape, jnp.int32),
            pltpu.SemaphoreType.DMA,
        ],
        compiler_params=params(),
    )(positions, place, field, hidden, sides, above, below, k1, b1, k2, b2)


def backward_kernel(
    return_hbm,
    got_ref,
    table_ref,
    out_hbm,
    return_ref,
    rows_ref,
    out_ref,
    return_sem,
    out_sem,
):
    blocks, width = out_hbm.shape
    tables, seg, _ = table_ref.shape
    chans = width // seg
    parts = out_sem.shape[0]
    part = blocks // parts
    return_copy = pltpu.make_async_copy(return_hbm, return_ref, return_sem)
    return_copy.start()
    return_copy.wait()
    step = rows_ref.shape[1] // chans
    out_copies = []

    def finish(q):
        piece = pl.ds(q * part, part)
        for c in range(chans):
            out_ref[piece, c * seg : (c + 1) * seg] = rows_ref[
                q, c * step : c * step + part, :
            ].astype(BF16)
        out_copies.append(
            pltpu.make_async_copy(out_ref.at[piece], out_hbm.at[piece], out_sem.at[q])
        )
        out_copies[-1].start()

    for q in range(parts):
        if q > 0:
            finish(q - 1)
        for n in range(part):
            states, weights = [], []
            for t in range(2):
                code = return_ref[t, q * part + n]
                slot = code >> log2(tables)
                at = pl.multiple_of((slot & 1) * chans, chans)
                states.append(got_ref[slot >> 1, pl.ds(at, chans), :])
                weights.append(table_ref[code & (tables - 1)])
            rows_ref[q, pl.ds(n, chans, stride=step), :] = lax.dot_general(
                jnp.concatenate(states, axis=1),
                jnp.concatenate(weights, axis=1),
                NT,
                preferred_element_type=F32,
            )
    finish(parts - 1)
    for copy in out_copies:
        copy.wait()


def backward_remap(returns, got, back_table):
    blocks = returns.shape[1]
    chans = got.shape[1] // CAP
    seg = got.shape[2]
    parts = 4
    return pl.pallas_call(
        backward_kernel,
        out_shape=jax.ShapeDtypeStruct((blocks, chans * seg), BF16),
        in_specs=[hbm(), vmem(), vmem()],
        out_specs=hbm(),
        scratch_shapes=[
            pltpu.SMEM(returns.shape, jnp.int32),
            pltpu.VMEM((parts, chans * (blocks // parts + PAD), seg), F32),
            pltpu.VMEM((blocks, chans * seg), BF16),
            pltpu.SemaphoreType.DMA,
            pltpu.SemaphoreType.DMA((parts,)),
        ],
        compiler_params=params(),
    )(returns, got, back_table)


def exchange(buffer):
    return lax.all_to_all(buffer, AXES, split_axis=0, concat_axis=0, tiled=True)


def local(
    ll_blocks,
    dest_dev,
    dest_pos,
    fwd_id,
    back_id,
    fwd_table,
    back_table,
    kernel_one,
    bias_one,
    kernel_two,
    bias_two,
):
    n_fx = lax.axis_size("fx")
    n_fy = lax.axis_size("fy")
    hblocks = 64
    j = lax.axis_index("fy")
    place = jnp.stack([j > 0, j < n_fy - 1]).astype(jnp.int32)[:, None]
    place = jnp.broadcast_to(place, (2, 128))
    send, returns, w1, w2 = forward_remap(
        dest_dev,
        dest_pos,
        fwd_id,
        back_id,
        ll_blocks,
        fwd_table,
        kernel_one,
        kernel_two,
        n_fx * n_fy,
        n_fy,
    )
    send, place = lax.optimization_barrier((send, place))
    b1, b2 = bias_one[None], bias_two[None]
    field, up, down, sides, positions = sum_field(exchange(send), hblocks)
    above = lax.ppermute(down, "fx", [(i, (i + 1) % n_fx) for i in range(n_fx)])
    below = lax.ppermute(up, "fx", [((i + 1) % n_fx, i) for i in range(n_fx)])
    turned, hidden = inner_hidden(field, sides, w1, b1)
    send_back = outer_state(
        positions, place, turned, hidden, sides, above, below, w1, b1, w2, b2
    )
    return backward_remap(returns, exchange(send_back), back_table)


def solution(mesh):
    blocked = P(AXES, None)
    in_specs = (blocked,) * 5 + (P(),) * 6
    return jax.shard_map(
        local, mesh=mesh, in_specs=in_specs, out_specs=P(AXES, None), check_vma=False
    )
```

```python
import functools

import jax
import jax.numpy as jnp
from jax import lax
from jax.experimental import pallas as pl
from jax.experimental.pallas import tpu as pltpu
from jax.sharding import PartitionSpec as P

CAP = 2
PAD = 8
META = 8
AXES = ("fx", "fy")
F32 = jnp.float32
BF16 = jnp.bfloat16
VMEM_LIMIT = 40 * 1024 * 1024
NT = (((1,), (1,)), ((), ()))


def smem():
    return pl.BlockSpec(memory_space=pltpu.SMEM)


def vmem():
    return pl.BlockSpec(memory_space=pltpu.VMEM)


def hbm():
    return pl.BlockSpec(memory_space=pl.ANY)


def params():
    return pltpu.CompilerParams(vmem_limit_bytes=VMEM_LIMIT)


def in_hbm(x):
    return pltpu.with_memory_space_constraint(x, pltpu.HBM)


def log2(count):
    assert count & (count - 1) == 0
    return count.bit_length() - 1


def lane_iota(shape):
    return lax.broadcasted_iota(jnp.int32, shape, len(shape) - 1)


def row_pair_weights(taps_ref, weights_ref):
    _, columns, chans, _ = taps_ref.shape
    none = jnp.zeros((chans, chans), BF16)
    for q in range(4):
        for d in range(columns):
            upper = taps_ref[q, d] if q < 3 else none
            lower = taps_ref[q - 1, d] if q > 0 else none
            weights_ref[q * chans : (q + 1) * chans, 2 * d * chans : 2 * (d + 1) * chans] = (
                jnp.concatenate([upper, lower], axis=1)
            )


def forward_kernel(
    n_fy,
    dev_hbm,
    pos_hbm,
    fwd_hbm,
    back_hbm,
    x_hbm,
    table_hbm,
    k1_hbm,
    k2_hbm,
    send_ref,
    return_hbm,
    w1_ref,
    w2_ref,
    dev_ref,
    pos_ref,
    fwd_ref,
    back_ref,
    return_ref,
    x_ref,
    table_ref,
    taps_ref,
    rows_ref,
    edge_ref,
    meta_ref,
    count_ref,
    code_sem,
    x_sem,
    table_sem,
    taps_sem,
    return_sem,
):
    blocks, width = x_ref.shape
    tables, seg, _ = table_ref.shape
    chans = width // seg
    devices = count_ref.shape[0]
    assert n_fy == 1 << log2(n_fy)
    parts = x_sem.shape[0]
    wide = width // parts
    step = rows_ref.shape[0] // chans
    pieces = table_sem.shape[0]
    deep = tables // pieces
    x_copies = [
        pltpu.make_async_copy(
            x_hbm.at[:, pl.ds(q * wide, wide)], x_ref.at[:, pl.ds(q * wide, wide)], x_sem.at[q]
        )
        for q in range(parts)
    ]
    table_copies = [
        pltpu.make_async_copy(
            table_hbm.at[pl.ds(q * deep, deep)], table_ref.at[pl.ds(q * deep, deep)], table_sem.at[q]
        )
        for q in range(pieces)
    ]
    code_copies = [
        pltpu.make_async_copy(source, target, code_sem.at[n])
        for n, (source, target) in enumerate(
            ((dev_hbm, dev_ref), (pos_hbm, pos_ref), (fwd_hbm, fwd_ref), (back_hbm, back_ref))
        )
    ]
    taps_copies = [
        pltpu.make_async_copy(source, taps_ref.at[n], taps_sem.at[n])
        for n, source in enumerate((k1_hbm, k2_hbm))
    ]
    for copy in code_copies + x_copies + taps_copies + table_copies:
        copy.start()

    def clear(d, carry):
        count_ref[d] = 0
        return carry

    lax.fori_loop(0, devices, clear, 0, unroll=8)
    meta_ref[...] = jnp.zeros_like(meta_ref)
    for copy in code_copies:
        copy.wait()

    def plan(b, carry):
        for t in range(2):
            dev = dev_ref[t, b]
            rank = count_ref[dev]
            count_ref[dev] = rank + 1
            return_ref[t, b] = ((dev * CAP + rank) << log2(tables)) + back_ref[t, b]
            pos = (pos_ref[t, b] + 1).astype(F32)
            meta_ref[pl.ds(dev * META + 4 + rank, 1), :] = jnp.full((1, seg), pos, F32)
        return carry

    lax.fori_loop(0, blocks, plan, 0, unroll=8)
    return_copy = pltpu.make_async_copy(return_ref, return_hbm, return_sem)
    return_copy.start()
    both = jnp.where(
        lane_iota((devices, seg)) < chans,
        meta_ref[pl.ds(4, devices, stride=META), :],
        meta_ref[pl.ds(5, devices, stride=META), :],
    )
    col = lax.broadcasted_iota(jnp.int32, both.shape, 0) & (n_fy - 1)
    meta_ref[pl.ds(6, devices, stride=META), :] = jnp.where(
        col > 0, pltpu.roll(both, 1, axis=0), 0.0
    )
    meta_ref[pl.ds(7, devices, stride=META), :] = jnp.where(
        col < n_fy - 1, pltpu.roll(both, devices - 1, axis=0), 0.0
    )
    for q, copy in enumerate(x_copies):
        copy.wait()
        for c in range(q * wide // seg, (q + 1) * wide // seg):
            rows_ref[c * step : c * step + blocks, :] = x_ref[:, c * seg : (c + 1) * seg].astype(F32)
    for n, (copy, weights_ref) in enumerate(zip(taps_copies, (w1_ref, w2_ref))):
        copy.wait()
        row_pair_weights(taps_ref.at[n], weights_ref)
    for q, copy in enumerate(table_copies):
        copy.wait()

        def edges(n, carry):
            edge_ref[n, 0:2, :] = table_ref[n, seg - 16 : seg, :].astype(F32)[14:16, :]
            edge_ref[n, 2:4, :] = table_ref[n, 0:16, :].astype(F32)[0:2, :]
            return carry

        lax.fori_loop(q * deep, (q + 1) * deep, edges, 0, unroll=4)
    lane = lane_iota((1, seg))

    def one_block(b, carry):
        tables_of = [fwd_ref[t, b] for t in range(2)]
        x = rows_ref[pl.ds(b, chans, stride=step), :].astype(BF16)
        weights = jnp.concatenate([table_ref[n] for n in tables_of], axis=0)
        product = lax.dot_general(x, weights, NT, preferred_element_type=F32)
        tips = jnp.concatenate([edge_ref[n] for n in tables_of], axis=0).astype(BF16)
        ends = lax.dot_general(tips, x, NT, preferred_element_type=F32)
        ends = jnp.concatenate([ends, ends], axis=1)
        for t in range(2):
            slot = return_ref[t, b] >> log2(tables)
            dev, rank = slot >> 1, slot & 1
            at = pl.multiple_of(rank * chans, chans)
            send_ref[dev, pl.ds(at, chans), :] = product[:, t * seg : (t + 1) * seg].astype(BF16)
            col = dev & (n_fy - 1)
            for side in range(2):
                inside = (col < n_fy - 1) if side == 0 else (col > 0)
                near = jnp.where(inside, dev + 1 - 2 * side, devices)
                first = t * 4 + side * 2
                meta_ref[pl.ds(near * META + 2 * side + rank, 1), :] = jnp.where(
                    lane < chans, ends[first : first + 1, :], ends[first + 1 : first + 2, :]
                )
        return carry

    lax.fori_loop(0, blocks, one_block, 0, unroll=True)
    send_ref[:, CAP * chans :, :] = (
        meta_ref[0 : devices * META, :].astype(BF16).reshape(devices, META, seg)
    )
    return_copy.wait()


def forward_remap(
    dest_dev, dest_pos, fwd_id, back_id, ll_blocks, fwd_table, k1, k2, devices, n_fy
):
    blocks, width = ll_blocks.shape
    tables, seg, _ = fwd_table.shape
    chans = width // seg
    return pl.pallas_call(
        functools.partial(forward_kernel, n_fy),
        out_shape=(
            jax.ShapeDtypeStruct((devices, CAP * chans + META, seg), BF16),
            jax.ShapeDtypeStruct((2, blocks), jnp.int32),
            jax.ShapeDtypeStruct((4 * chans, 6 * chans), BF16),
            jax.ShapeDtypeStruct((4 * chans, 6 * chans), BF16),
        ),
        in_specs=[hbm()] * 8,
        out_specs=(vmem(), hbm(), vmem(), vmem()),
        scratch_shapes=[
            pltpu.SMEM((2, blocks), jnp.int32),
            pltpu.SMEM((2, blocks), jnp.int32),
            pltpu.SMEM((2, blocks), jnp.int32),
            pltpu.SMEM((2, blocks), jnp.int32),
            pltpu.SMEM((2, blocks), jnp.int32),
            pltpu.VMEM((blocks, width), BF16),
            pltpu.VMEM((tables, seg, seg), BF16),
            pltpu.VMEM((2,) + k1.shape, BF16),
            pltpu.VMEM((chans * (blocks + PAD), seg), F32),
            pltpu.VMEM((tables, 4, seg), F32),
            pltpu.VMEM(((devices + 1) * META, seg), F32),
            pltpu.SMEM((devices,), jnp.int32),
            pltpu.SemaphoreType.DMA((4,)),
            pltpu.SemaphoreType.DMA((4,)),
            pltpu.SemaphoreType.DMA((8,)),
            pltpu.SemaphoreType.DMA((2,)),
            pltpu.SemaphoreType.DMA,
        ],
        compiler_params=params(),
    )(
        *(in_hbm(route.T) for route in (dest_dev, dest_pos, fwd_id, back_id)),
        *(in_hbm(x) for x in (ll_blocks, fwd_table, k1, k2)),
    )


def sum_kernel(
    got_ref,
    field_ref,
    up_ref,
    down_ref,
    side_ref,
    pos_ref,
    rows_ref,
    sum0_ref,
    sum1_ref,
    spot_ref,
    spot_sem,
):
    devices, _, cols = got_ref.shape
    hblocks, chans, _ = field_ref.shape
    pairs = hblocks // 2
    lanes = 2 * chans
    rows_ref[...] = got_ref[:, CAP * chans :, :].reshape(devices * META, lanes).astype(F32)

    def meta_row(n):
        return rows_ref[pl.ds(n, devices, stride=META), :]

    lane = lane_iota((devices, lanes))
    table = jnp.where(lane % 2 == 0, meta_row(4), meta_row(5))
    beside = [meta_row(6), meta_row(7)]
    for side in range(2):
        turned_half = pltpu.roll(beside[side], chans, axis=1)
        for rank in range(CAP):
            here = lane == 2 + 2 * side + rank
            table = jnp.where(here, beside[side] if rank == 0 else turned_half, table)
    spots = table.T[0:8, :].astype(jnp.int32) - 1
    pos_ref[...] = spots
    spot_copy = pltpu.make_async_copy(pos_ref, spot_ref, spot_sem)
    spot_copy.start()

    def clear(r, carry):
        for rank in range(CAP):
            (sum0_ref, sum1_ref)[rank][r] = jnp.zeros((chans, cols), F32)
        return carry

    lax.fori_loop(0, hblocks, clear, 0, unroll=4)
    block = lax.broadcasted_iota(jnp.int32, (pairs, devices), 0)
    low = lane_iota((pairs, lanes)) < chans
    for side in range(2):
        sums = []
        for parity in range(2):
            total = jnp.zeros((pairs, lanes), F32)
            for rank in range(CAP):
                n = 2 + 2 * side + rank
                hit = (spots[n : n + 1, :] == 2 * block + parity).astype(F32).astype(BF16)
                total += jnp.dot(
                    hit, meta_row(2 * side + rank).astype(BF16), preferred_element_type=F32
                )
            sums.append(total)
        even, odd = sums
        side_ref[2 * side] = jnp.where(low, even, pltpu.roll(odd, chans, axis=1))
        side_ref[2 * side + 1] = jnp.where(low, pltpu.roll(even, chans, axis=1), odd)
    spot_copy.wait()

    def add(d, carry):
        rows, sums = [], []
        for rank, sum_ref in enumerate((sum0_ref, sum1_ref)):
            pos = spot_ref[rank, d]
            rows.append(jnp.where(pos < 0, hblocks, pos))
            block = got_ref[d, rank * chans : (rank + 1) * chans, :]
            sums.append(sum_ref[rows[-1]] + block.astype(F32))
        sum0_ref[rows[0]] = sums[0]
        sum1_ref[rows[1]] = sums[1]
        return carry

    lax.fori_loop(0, devices, add, 0, unroll=16)

    def total_of(r):
        return sum0_ref[r] + sum1_ref[r]

    corners = jnp.zeros((up_ref.shape[0] - cols, lanes), F32)
    corner_row = lax.broadcasted_iota(jnp.int32, corners.shape, 0)
    for ref, g in ((up_ref, 0), (down_ref, pairs - 1)):
        ref[0:cols, :] = jnp.concatenate([total_of(2 * g), total_of(2 * g + 1)], axis=0).T.astype(BF16)
        rest = corners
        for n in range(4):
            rest = jnp.where(corner_row == n, side_ref[n, g : g + 1, :], rest)
        ref[cols:, :] = rest.astype(BF16)

    def finish(r, carry):
        field_ref[r] = total_of(r).astype(BF16)
        return carry

    lax.fori_loop(0, hblocks, finish, 0, unroll=4)


def sum_field(got, hblocks):
    devices, depth, cols = got.shape
    chans = (depth - META) // CAP
    pairs = hblocks // 2
    message = jax.ShapeDtypeStruct((cols + 16, 2 * chans), BF16)
    return pl.pallas_call(
        sum_kernel,
        out_shape=(
            jax.ShapeDtypeStruct((hblocks, chans, cols), BF16),
            message,
            message,
            jax.ShapeDtypeStruct((4, pairs, 2 * chans), F32),
            jax.ShapeDtypeStruct((8, devices), jnp.int32),
        ),
        in_specs=[vmem()],
        out_specs=(vmem(),) * 5,
        scratch_shapes=[
            pltpu.VMEM((devices * META, cols), F32),
            pltpu.VMEM((hblocks + 1, chans, cols), F32),
            pltpu.VMEM((hblocks + 1, chans, cols), F32),
            pltpu.SMEM((8, devices), jnp.int32),
            pltpu.SemaphoreType.DMA,
        ],
        compiler_params=params(),
    )(got)


def gelu(x):
    return 0.5 * x * (1.0 + jnp.tanh(0.7978845608028654 * (x + 0.044715 * (x * x * x))))


def taps(x, weights_ref, d):
    lanes = x.shape[1] // 2
    return jnp.dot(x, weights_ref[:, d * lanes : (d + 1) * lanes], preferred_element_type=F32)


def row_pair_conv(upper, lower, weights_ref, bias, before, after):
    cols, lanes = upper.shape
    rows = jnp.concatenate([upper, lower], axis=1)
    product = jnp.dot(rows, weights_ref[...], preferred_element_type=F32)
    ahead = pltpu.roll(product[:, 0:lanes], 1, axis=0)
    behind = pltpu.roll(product[:, 2 * lanes :], cols - 1, axis=0)
    edge = lax.broadcasted_iota(jnp.int32, (8, lanes), 0)
    first = jnp.where(edge == 0, before, ahead[0:8, :])
    last = jnp.where(edge == 7, after, behind[cols - 8 :, :])
    ahead = jnp.concatenate([first, ahead[8:, :]], axis=0)
    behind = jnp.concatenate([behind[: cols - 8, :], last], axis=0)
    return product[:, lanes : 2 * lanes] + ahead + behind + bias


def twice(bias_ref):
    return jnp.concatenate([bias_ref[...], bias_ref[...]], axis=1)


def inner_kernel(field_ref, side_ref, k1_ref, b1_ref, turned_ref, hid_ref, halo_ref):
    hblocks, chans, cols = field_ref.shape
    pairs = hblocks // 2

    def turn(g, carry):
        turned_ref[g] = field_ref[pl.ds(2 * g, 2)].reshape(2 * chans, cols).T
        return carry

    lax.fori_loop(0, pairs, turn, 0, unroll=True)
    b1 = twice(b1_ref)
    for n, (k, d) in enumerate(((1, 0), (2, 2))):
        both = jnp.concatenate([side_ref[k, 0 : pairs - 1, :], side_ref[k, 1:pairs, :]], axis=1)
        halo_ref[n, 1:pairs, :] = taps(both.astype(BF16), k1_ref, d)

    def first(g, carry):
        out = row_pair_conv(
            turned_ref[g - 1],
            turned_ref[g],
            k1_ref,
            b1,
            halo_ref[0, pl.ds(g, 1), :],
            halo_ref[1, pl.ds(g, 1), :],
        )
        hid_ref[g] = gelu(out).astype(BF16)
        return carry

    lax.fori_loop(1, pairs, first, 0, unroll=True)


def inner_hidden(field, sides, k1, b1):
    hblocks, chans, cols = field.shape
    pairs = hblocks // 2
    shape = jax.ShapeDtypeStruct((pairs, cols, 2 * chans), BF16)
    return pl.pallas_call(
        inner_kernel,
        out_shape=(shape, shape),
        in_specs=[vmem()] * 4,
        out_specs=(vmem(), vmem()),
        scratch_shapes=[pltpu.VMEM((2, pairs + 8, 2 * chans), F32)],
        compiler_params=params(),
        cost_estimate=pl.CostEstimate(
            flops=2 * 8192 * 9 * 64 * 64, bytes_accessed=4 << 20, transcendentals=1 << 19
        ),
    )(field, sides, k1, b1)


def outer_kernel(
    pos_hbm,
    place_ref,
    field_ref,
    hid_ref,
    sides_ref,
    above_ref,
    below_ref,
    k1_ref,
    b1_ref,
    k2_ref,
    b2_ref,
    send_ref,
    side_ref,
    halo_ref,
    state_ref,
    pos_ref,
    pos_sem,
):
    pos_copy = pltpu.make_async_copy(pos_hbm, pos_ref, pos_sem)
    pos_copy.start()
    pairs, cols, lanes = field_ref.shape
    chans = lanes // 2
    devices = pos_ref.shape[1]
    groups = pairs + 1
    above = above_ref[cols:, :].astype(F32)
    below = below_ref[cols:, :].astype(F32)
    for n, k in enumerate((0, 1, 4, 5)):
        side_ref[k, 0:1, :] = above[n : n + 1, :]
        side_ref[k, 1 : pairs + 1, :] = sides_ref[n]
        side_ref[k, pairs + 1 : pairs + 2, :] = below[n : n + 1, :]

    def ends(block):
        return (
            block[0:16, :].astype(F32)[0:1, :],
            block[cols - 16 : cols, :].astype(F32)[15:16, :],
        )

    for k, (high, low) in enumerate(zip(ends(above_ref[0:cols, :]), ends(below_ref[0:cols, :]))):
        side_ref[2 + k, 0:1, :] = high
        side_ref[2 + k, pairs + 1 : pairs + 2, :] = low

    def inner_side(g, carry):
        for k, end in enumerate(ends(field_ref[g])):
            side_ref[2 + k, pl.ds(g + 1, 1), :] = end
        return carry

    lax.fori_loop(0, pairs, inner_side, 0, unroll=4)

    def paired(k):
        return jnp.concatenate(
            [side_ref[k, 0:groups, :], side_ref[k, 1 : groups + 1, :]], axis=1
        ).astype(BF16)

    b1 = twice(b1_ref)
    b2 = twice(b2_ref)
    c = [paired(k) for k in range(6)]
    left = taps(c[1], k1_ref, 0)
    right = taps(c[4], k1_ref, 2)
    before = taps(c[0], k1_ref, 0) + taps(c[1], k1_ref, 1) + taps(c[2], k1_ref, 2) + b1
    after = taps(c[3], k1_ref, 0) + taps(c[4], k1_ref, 1) + taps(c[5], k1_ref, 2) + b1
    before = jnp.where(place_ref[0:1, :] > 0, gelu(before), 0.0)
    after = jnp.where(place_ref[1:2, :] > 0, gelu(after), 0.0)
    for n, (column, d) in enumerate(((before, 0), (after, 2))):
        side_ref[n, 0:groups, :] = column
        both = jnp.concatenate([side_ref[n, 0:pairs, :], side_ref[n, 1 : pairs + 1, :]], axis=1)
        halo_ref[n, 0:pairs, :] = taps(both.astype(BF16), k2_ref, d)

    def hidden(upper, lower, g):
        out = row_pair_conv(upper, lower, k1_ref, b1, left[g : g + 1, :], right[g : g + 1, :])
        return gelu(out).astype(BF16)

    def second(g, upper, lower):
        out = row_pair_conv(
            upper, lower, k2_ref, b2, halo_ref[0, pl.ds(g, 1), :], halo_ref[1, pl.ds(g, 1), :]
        )
        state = out + field_ref[g].astype(F32)
        state_ref[pl.ds(2 * g, 2)] = state.T.astype(BF16).reshape(2, chans, cols)

    second(0, hidden(above_ref[0:cols, :], field_ref[0], 0), hid_ref[1])
    second(pairs - 1, hid_ref[pairs - 1], hidden(field_ref[pairs - 1], below_ref[0:cols, :], pairs))

    def inner(g, carry):
        second(g, hid_ref[g], hid_ref[g + 1])
        return carry

    lax.fori_loop(1, pairs - 1, inner, 0, unroll=True)
    pos_copy.wait()

    def pick(d, carry):
        for rank in range(CAP):
            pos = jnp.maximum(pos_ref[rank, d], 0)
            send_ref[d, rank * chans : (rank + 1) * chans, :] = state_ref[pos]
        return carry

    lax.fori_loop(0, devices, pick, 0, unroll=16)


def outer_state(positions, place, field, hidden, sides, above, below, k1, b1, k2, b2):
    pairs, cols, lanes = field.shape
    chans = lanes // 2
    devices = positions.shape[1]
    return pl.pallas_call(
        outer_kernel,
        out_shape=jax.ShapeDtypeStruct((devices, CAP * chans, cols), BF16),
        in_specs=[vmem()] * 11,
        out_specs=vmem(),
        scratch_shapes=[
            pltpu.VMEM((6, pairs + 8, lanes), F32),
            pltpu.VMEM((2, pairs + 8, lanes), F32),
            pltpu.VMEM((2 * pairs, chans, cols), BF16),
            pltpu.SMEM(positions.shape, jnp.int32),
            pltpu.SemaphoreType.DMA,
        ],
        compiler_params=params(),
    )(positions, place, field, hidden, sides, above, below, k1, b1, k2, b2)


def backward_kernel(
    return_hbm,
    got_ref,
    table_ref,
    out_hbm,
    return_ref,
    rows_ref,
    out_ref,
    return_sem,
    out_sem,
):
    blocks, width = out_hbm.shape
    tables, seg, _ = table_ref.shape
    chans = width // seg
    parts = out_sem.shape[0]
    part = blocks // parts
    return_copy = pltpu.make_async_copy(return_hbm, return_ref, return_sem)
    return_copy.start()
    return_copy.wait()
    step = rows_ref.shape[1] // chans
    out_copies = []

    def finish(q):
        piece = pl.ds(q * part, part)
        for c in range(chans):
            out_ref[piece, c * seg : (c + 1) * seg] = rows_ref[
                q, c * step : c * step + part, :
            ].astype(BF16)
        out_copies.append(
            pltpu.make_async_copy(out_ref.at[piece], out_hbm.at[piece], out_sem.at[q])
        )
        out_copies[-1].start()

    for q in range(parts):
        if q > 0:
            finish(q - 1)
        for n in range(part):
            states, weights = [], []
            for t in range(2):
                code = return_ref[t, q * part + n]
                slot = code >> log2(tables)
                at = pl.multiple_of((slot & 1) * chans, chans)
                states.append(got_ref[slot >> 1, pl.ds(at, chans), :])
                weights.append(table_ref[code & (tables - 1)])
            rows_ref[q, pl.ds(n, chans, stride=step), :] = lax.dot_general(
                jnp.concatenate(states, axis=1),
                jnp.concatenate(weights, axis=1),
                NT,
                preferred_element_type=F32,
            )
    finish(parts - 1)
    for copy in out_copies:
        copy.wait()


def backward_remap(returns, got, back_table):
    blocks = returns.shape[1]
    chans = got.shape[1] // CAP
    seg = got.shape[2]
    parts = 4
    return pl.pallas_call(
        backward_kernel,
        out_shape=jax.ShapeDtypeStruct((blocks, chans * seg), BF16),
        in_specs=[hbm(), vmem(), vmem()],
        out_specs=hbm(),
        scratch_shapes=[
            pltpu.SMEM(returns.shape, jnp.int32),
            pltpu.VMEM((parts, chans * (blocks // parts + PAD), seg), F32),
            pltpu.VMEM((blocks, chans * seg), BF16),
            pltpu.SemaphoreType.DMA,
            pltpu.SemaphoreType.DMA((parts,)),
        ],
        compiler_params=params(),
    )(returns, got, back_table)


def exchange(buffer):
    return lax.all_to_all(buffer, AXES, split_axis=0, concat_axis=0, tiled=True)


def local(
    ll_blocks,
    dest_dev,
    dest_pos,
    fwd_id,
    back_id,
    fwd_table,
    back_table,
    kernel_one,
    bias_one,
    kernel_two,
    bias_two,
):
    n_fx = lax.axis_size("fx")
    n_fy = lax.axis_size("fy")
    hblocks = 64
    j = lax.axis_index("fy")
    place = jnp.stack([j > 0, j < n_fy - 1]).astype(jnp.int32)[:, None]
    place = jnp.broadcast_to(place, (2, 128))
    send, returns, w1, w2 = forward_remap(
        dest_dev,
        dest_pos,
        fwd_id,
        back_id,
        ll_blocks,
        fwd_table,
        kernel_one,
        kernel_two,
        n_fx * n_fy,
        n_fy,
    )
    send, place = lax.optimization_barrier((send, place))
    b1, b2 = bias_one[None], bias_two[None]
    field, up, down, sides, positions = sum_field(exchange(send), hblocks)
    above = lax.ppermute(down, "fx", [(i, (i + 1) % n_fx) for i in range(n_fx)])
    below = lax.ppermute(up, "fx", [((i + 1) % n_fx, i) for i in range(n_fx)])
    turned, hidden = inner_hidden(field, sides, w1, b1)
    send_back = outer_state(
        positions, place, turned, hidden, sides, above, below, w1, b1, w2, b2
    )
    return backward_remap(returns, exchange(send_back), back_table)


def solution(mesh):
    blocked = P(AXES, None)
    in_specs = (blocked,) * 5 + (P(),) * 6
    return jax.shard_map(
        local, mesh=mesh, in_specs=in_specs, out_specs=P(AXES, None), check_vma=False
    )
```

```python
import functools

import jax
import jax.numpy as jnp
from jax import lax
from jax.experimental import pallas as pl
from jax.experimental.pallas import tpu as pltpu
from jax.sharding import PartitionSpec as P

CAP = 2
PAD = 8
META = 8
AXES = ("fx", "fy")
F32 = jnp.float32
BF16 = jnp.bfloat16
VMEM_LIMIT = 40 * 1024 * 1024
NT = (((1,), (1,)), ((), ()))


def smem():
    return pl.BlockSpec(memory_space=pltpu.SMEM)


def vmem():
    return pl.BlockSpec(memory_space=pltpu.VMEM)


def hbm():
    return pl.BlockSpec(memory_space=pl.ANY)


def params():
    return pltpu.CompilerParams(vmem_limit_bytes=VMEM_LIMIT)


def in_hbm(x):
    return pltpu.with_memory_space_constraint(x, pltpu.HBM)


def log2(count):
    assert count & (count - 1) == 0
    return count.bit_length() - 1


def lane_iota(shape):
    return lax.broadcasted_iota(jnp.int32, shape, len(shape) - 1)


def row_pair_weights(taps_ref, weights_ref):
    _, columns, chans, _ = taps_ref.shape
    none = jnp.zeros((chans, chans), BF16)
    for q in range(4):
        for d in range(columns):
            upper = taps_ref[q, d] if q < 3 else none
            lower = taps_ref[q - 1, d] if q > 0 else none
            weights_ref[q * chans : (q + 1) * chans, 2 * d * chans : 2 * (d + 1) * chans] = (
                jnp.concatenate([upper, lower], axis=1)
            )


def forward_kernel(
    n_fy,
    dev_hbm,
    pos_hbm,
    fwd_hbm,
    back_hbm,
    x_hbm,
    table_hbm,
    k1_hbm,
    k2_hbm,
    send_ref,
    return_hbm,
    w1_ref,
    w2_ref,
    dev_ref,
    pos_ref,
    fwd_ref,
    back_ref,
    return_ref,
    x_ref,
    table_ref,
    taps_ref,
    rows_ref,
    edge_ref,
    meta_ref,
    count_ref,
    code_sem,
    x_sem,
    table_sem,
    taps_sem,
    return_sem,
):
    blocks, width = x_ref.shape
    tables, seg, _ = table_ref.shape
    chans = width // seg
    devices = count_ref.shape[0]
    assert n_fy == 1 << log2(n_fy)
    parts = x_sem.shape[0]
    wide = width // parts
    step = rows_ref.shape[0] // chans
    pieces = table_sem.shape[0]
    deep = tables // pieces
    x_copies = [
        pltpu.make_async_copy(
            x_hbm.at[:, pl.ds(q * wide, wide)], x_ref.at[:, pl.ds(q * wide, wide)], x_sem.at[q]
        )
        for q in range(parts)
    ]
    table_copies = [
        pltpu.make_async_copy(
            table_hbm.at[pl.ds(q * deep, deep)], table_ref.at[pl.ds(q * deep, deep)], table_sem.at[q]
        )
        for q in range(pieces)
    ]
    code_copies = [
        pltpu.make_async_copy(source, target, code_sem.at[n])
        for n, (source, target) in enumerate(
            ((dev_hbm, dev_ref), (pos_hbm, pos_ref), (fwd_hbm, fwd_ref), (back_hbm, back_ref))
        )
    ]
    taps_copies = [
        pltpu.make_async_copy(source, taps_ref.at[n], taps_sem.at[n])
        for n, source in enumerate((k1_hbm, k2_hbm))
    ]
    for copy in code_copies + x_copies + taps_copies + table_copies:
        copy.start()

    def clear(d, carry):
        count_ref[d] = 0
        return carry

    lax.fori_loop(0, devices, clear, 0, unroll=8)
    meta_ref[...] = jnp.zeros_like(meta_ref)
    for copy in code_copies:
        copy.wait()

    def plan(b, carry):
        for t in range(2):
            dev = dev_ref[t, b]
            rank = count_ref[dev]
            count_ref[dev] = rank + 1
            return_ref[t, b] = ((dev * CAP + rank) << log2(tables)) + back_ref[t, b]
            pos = (pos_ref[t, b] + 1).astype(F32)
            meta_ref[pl.ds(dev * META + 4 + rank, 1), :] = jnp.full((1, seg), pos, F32)
        return carry

    lax.fori_loop(0, blocks, plan, 0, unroll=8)
    return_copy = pltpu.make_async_copy(return_ref, return_hbm, return_sem)
    return_copy.start()
    both = jnp.where(
        lane_iota((devices, seg)) < chans,
        meta_ref[pl.ds(4, devices, stride=META), :],
        meta_ref[pl.ds(5, devices, stride=META), :],
    )
    col = lax.broadcasted_iota(jnp.int32, both.shape, 0) & (n_fy - 1)
    meta_ref[pl.ds(6, devices, stride=META), :] = jnp.where(
        col > 0, pltpu.roll(both, 1, axis=0), 0.0
    )
    meta_ref[pl.ds(7, devices, stride=META), :] = jnp.where(
        col < n_fy - 1, pltpu.roll(both, devices - 1, axis=0), 0.0
    )
    for q, copy in enumerate(x_copies):
        copy.wait()
        for c in range(q * wide // seg, (q + 1) * wide // seg):
            rows_ref[c * step : c * step + blocks, :] = x_ref[:, c * seg : (c + 1) * seg].astype(F32)
    for n, (copy, weights_ref) in enumerate(zip(taps_copies, (w1_ref, w2_ref))):
        copy.wait()
        row_pair_weights(taps_ref.at[n], weights_ref)
    for q, copy in enumerate(table_copies):
        copy.wait()

        def edges(n, carry):
            edge_ref[n, 0:2, :] = table_ref[n, seg - 16 : seg, :].astype(F32)[14:16, :]
            edge_ref[n, 2:4, :] = table_ref[n, 0:16, :].astype(F32)[0:2, :]
            return carry

        lax.fori_loop(q * deep, (q + 1) * deep, edges, 0, unroll=4)
    lane = lane_iota((1, seg))

    def one_block(b, carry):
        tables_of = [fwd_ref[t, b] for t in range(2)]
        x = rows_ref[pl.ds(b, chans, stride=step), :].astype(BF16)
        weights = jnp.concatenate([table_ref[n] for n in tables_of], axis=0)
        product = lax.dot_general(x, weights, NT, preferred_element_type=F32)
        tips = jnp.concatenate([edge_ref[n] for n in tables_of], axis=0).astype(BF16)
        ends = lax.dot_general(tips, x, NT, preferred_element_type=F32)
        ends = jnp.concatenate([ends, ends], axis=1)
        for t in range(2):
            slot = return_ref[t, b] >> log2(tables)
            dev, rank = slot >> 1, slot & 1
            at = pl.multiple_of(rank * chans, chans)
            send_ref[dev, pl.ds(at, chans), :] = product[:, t * seg : (t + 1) * seg].astype(BF16)
            col = dev & (n_fy - 1)
            for side in range(2):
                inside = (col < n_fy - 1) if side == 0 else (col > 0)
                near = jnp.where(inside, dev + 1 - 2 * side, devices)
                first = t * 4 + side * 2
                meta_ref[pl.ds(near * META + 2 * side + rank, 1), :] = jnp.where(
                    lane < chans, ends[first : first + 1, :], ends[first + 1 : first + 2, :]
                )
        return carry

    lax.fori_loop(0, blocks, one_block, 0, unroll=True)
    send_ref[:, CAP * chans :, :] = (
        meta_ref[0 : devices * META, :].astype(BF16).reshape(devices, META, seg)
    )
    return_copy.wait()


def forward_remap(
    dest_dev, dest_pos, fwd_id, back_id, ll_blocks, fwd_table, k1, k2, devices, n_fy
):
    blocks, width = ll_blocks.shape
    tables, seg, _ = fwd_table.shape
    chans = width // seg
    return pl.pallas_call(
        functools.partial(forward_kernel, n_fy),
        out_shape=(
            jax.ShapeDtypeStruct((devices, CAP * chans + META, seg), BF16),
            jax.ShapeDtypeStruct((2, blocks), jnp.int32),
            jax.ShapeDtypeStruct((4 * chans, 6 * chans), BF16),
            jax.ShapeDtypeStruct((4 * chans, 6 * chans), BF16),
        ),
        in_specs=[hbm()] * 8,
        out_specs=(vmem(), hbm(), vmem(), vmem()),
        scratch_shapes=[
            pltpu.SMEM((2, blocks), jnp.int32),
            pltpu.SMEM((2, blocks), jnp.int32),
            pltpu.SMEM((2, blocks), jnp.int32),
            pltpu.SMEM((2, blocks), jnp.int32),
            pltpu.SMEM((2, blocks), jnp.int32),
            pltpu.VMEM((blocks, width), BF16),
            pltpu.VMEM((tables, seg, seg), BF16),
            pltpu.VMEM((2,) + k1.shape, BF16),
            pltpu.VMEM((chans * (blocks + PAD), seg), F32),
            pltpu.VMEM((tables, 4, seg), F32),
            pltpu.VMEM(((devices + 1) * META, seg), F32),
            pltpu.SMEM((devices,), jnp.int32),
            pltpu.SemaphoreType.DMA((4,)),
            pltpu.SemaphoreType.DMA((4,)),
            pltpu.SemaphoreType.DMA((8,)),
            pltpu.SemaphoreType.DMA((2,)),
            pltpu.SemaphoreType.DMA,
        ],
        compiler_params=params(),
    )(
        *(in_hbm(route.T) for route in (dest_dev, dest_pos, fwd_id, back_id)),
        *(in_hbm(x) for x in (ll_blocks, fwd_table, k1, k2)),
    )


def sum_kernel(
    got_ref,
    field_ref,
    up_ref,
    down_ref,
    side_ref,
    pos_ref,
    rows_ref,
    sum0_ref,
    sum1_ref,
    spot_ref,
    spot_sem,
):
    devices, _, cols = got_ref.shape
    hblocks, chans, _ = field_ref.shape
    pairs = hblocks // 2
    lanes = 2 * chans
    rows_ref[...] = got_ref[:, CAP * chans :, :].reshape(devices * META, lanes).astype(F32)

    def meta_row(n):
        return rows_ref[pl.ds(n, devices, stride=META), :]

    lane = lane_iota((devices, lanes))
    table = jnp.where(lane % 2 == 0, meta_row(4), meta_row(5))
    beside = [meta_row(6), meta_row(7)]
    for side in range(2):
        turned_half = pltpu.roll(beside[side], chans, axis=1)
        for rank in range(CAP):
            here = lane == 2 + 2 * side + rank
            table = jnp.where(here, beside[side] if rank == 0 else turned_half, table)
    spots = table.T[0:8, :].astype(jnp.int32) - 1
    pos_ref[...] = spots
    spot_copy = pltpu.make_async_copy(pos_ref, spot_ref, spot_sem)
    spot_copy.start()

    def clear(r, carry):
        for rank in range(CAP):
            (sum0_ref, sum1_ref)[rank][r] = jnp.zeros((chans, cols), F32)
        return carry

    lax.fori_loop(0, hblocks, clear, 0, unroll=4)
    block = lax.broadcasted_iota(jnp.int32, (pairs, devices), 0)
    low = lane_iota((pairs, lanes)) < chans
    for side in range(2):
        sums = []
        for parity in range(2):
            total = jnp.zeros((pairs, lanes), F32)
            for rank in range(CAP):
                n = 2 + 2 * side + rank
                hit = (spots[n : n + 1, :] == 2 * block + parity).astype(F32).astype(BF16)
                total += jnp.dot(
                    hit, meta_row(2 * side + rank).astype(BF16), preferred_element_type=F32
                )
            sums.append(total)
        even, odd = sums
        side_ref[2 * side] = jnp.where(low, even, pltpu.roll(odd, chans, axis=1))
        side_ref[2 * side + 1] = jnp.where(low, pltpu.roll(even, chans, axis=1), odd)
    spot_copy.wait()

    def add(d, carry):
        rows, sums = [], []
        for rank, sum_ref in enumerate((sum0_ref, sum1_ref)):
            pos = spot_ref[rank, d]
            rows.append(jnp.where(pos < 0, hblocks, pos))
            block = got_ref[d, rank * chans : (rank + 1) * chans, :]
            sums.append(sum_ref[rows[-1]] + block.astype(F32))
        sum0_ref[rows[0]] = sums[0]
        sum1_ref[rows[1]] = sums[1]
        return carry

    lax.fori_loop(0, devices, add, 0, unroll=16)

    def total_of(r):
        return sum0_ref[r] + sum1_ref[r]

    corners = jnp.zeros((up_ref.shape[0] - cols, lanes), F32)
    corner_row = lax.broadcasted_iota(jnp.int32, corners.shape, 0)
    for ref, g in ((up_ref, 0), (down_ref, pairs - 1)):
        ref[0:cols, :] = jnp.concatenate([total_of(2 * g), total_of(2 * g + 1)], axis=0).T.astype(BF16)
        rest = corners
        for n in range(4):
            rest = jnp.where(corner_row == n, side_ref[n, g : g + 1, :], rest)
        ref[cols:, :] = rest.astype(BF16)

    def finish(r, carry):
        field_ref[r] = total_of(r).astype(BF16)
        return carry

    lax.fori_loop(0, hblocks, finish, 0, unroll=4)


def sum_field(got, hblocks):
    devices, depth, cols = got.shape
    chans = (depth - META) // CAP
    pairs = hblocks // 2
    message = jax.ShapeDtypeStruct((cols + 16, 2 * chans), BF16)
    return pl.pallas_call(
        sum_kernel,
        out_shape=(
            jax.ShapeDtypeStruct((hblocks, chans, cols), BF16),
            message,
            message,
            jax.ShapeDtypeStruct((4, pairs, 2 * chans), F32),
            jax.ShapeDtypeStruct((8, devices), jnp.int32),
        ),
        in_specs=[vmem()],
        out_specs=(vmem(),) * 5,
        scratch_shapes=[
            pltpu.VMEM((devices * META, cols), F32),
            pltpu.VMEM((hblocks + 1, chans, cols), F32),
            pltpu.VMEM((hblocks + 1, chans, cols), F32),
            pltpu.SMEM((8, devices), jnp.int32),
            pltpu.SemaphoreType.DMA,
        ],
        compiler_params=params(),
    )(got)


def gelu(x):
    return 0.5 * x * (1.0 + jnp.tanh(0.7978845608028654 * (x + 0.044715 * (x * x * x))))


def taps(x, weights_ref, d):
    lanes = x.shape[1] // 2
    return jnp.dot(x, weights_ref[:, d * lanes : (d + 1) * lanes], preferred_element_type=F32)


def row_pair_conv(upper, lower, weights_ref, bias, before, after):
    cols, lanes = upper.shape
    rows = jnp.concatenate([upper, lower], axis=1)
    product = jnp.dot(rows, weights_ref[...], preferred_element_type=F32)
    ahead = pltpu.roll(product[:, 0:lanes], 1, axis=0)
    behind = pltpu.roll(product[:, 2 * lanes :], cols - 1, axis=0)
    edge = lax.broadcasted_iota(jnp.int32, (8, lanes), 0)
    first = jnp.where(edge == 0, before, ahead[0:8, :])
    last = jnp.where(edge == 7, after, behind[cols - 8 :, :])
    ahead = jnp.concatenate([first, ahead[8:, :]], axis=0)
    behind = jnp.concatenate([behind[: cols - 8, :], last], axis=0)
    return product[:, lanes : 2 * lanes] + ahead + behind + bias


def twice(bias_ref):
    return jnp.concatenate([bias_ref[...], bias_ref[...]], axis=1)


def inner_kernel(field_ref, side_ref, k1_ref, b1_ref, turned_ref, hid_ref, halo_ref):
    hblocks, chans, cols = field_ref.shape
    pairs = hblocks // 2

    def turn(g, carry):
        turned_ref[g] = field_ref[pl.ds(2 * g, 2)].reshape(2 * chans, cols).T
        return carry

    lax.fori_loop(0, pairs, turn, 0, unroll=True)
    b1 = twice(b1_ref)
    for n, (k, d) in enumerate(((1, 0), (2, 2))):
        both = jnp.concatenate([side_ref[k, 0 : pairs - 1, :], side_ref[k, 1:pairs, :]], axis=1)
        halo_ref[n, 1:pairs, :] = taps(both.astype(BF16), k1_ref, d)

    def first(g, carry):
        out = row_pair_conv(
            turned_ref[g - 1],
            turned_ref[g],
            k1_ref,
            b1,
            halo_ref[0, pl.ds(g, 1), :],
            halo_ref[1, pl.ds(g, 1), :],
        )
        hid_ref[g] = gelu(out).astype(BF16)
        return carry

    lax.fori_loop(1, pairs, first, 0, unroll=True)


def inner_hidden(field, sides, k1, b1):
    hblocks, chans, cols = field.shape
    pairs = hblocks // 2
    shape = jax.ShapeDtypeStruct((pairs, cols, 2 * chans), BF16)
    return pl.pallas_call(
        inner_kernel,
        out_shape=(shape, shape),
        in_specs=[vmem()] * 4,
        out_specs=(vmem(), vmem()),
        scratch_shapes=[pltpu.VMEM((2, pairs + 8, 2 * chans), F32)],
        compiler_params=params(),
        cost_estimate=pl.CostEstimate(
            flops=2 * 8192 * 9 * 64 * 64, bytes_accessed=4 << 20, transcendentals=1 << 19
        ),
    )(field, sides, k1, b1)


def outer_kernel(
    pos_hbm,
    place_ref,
    field_ref,
    hid_ref,
    sides_ref,
    below_ref,
    above_ref,
    k1_ref,
    b1_ref,
    k2_ref,
    b2_ref,
    send_ref,
    side_ref,
    halo_ref,
    state_ref,
    pos_ref,
    pos_sem,
):
    pos_copy = pltpu.make_async_copy(pos_hbm, pos_ref, pos_sem)
    pos_copy.start()
    pairs, cols, lanes = field_ref.shape
    chans = lanes // 2
    devices = pos_ref.shape[1]
    groups = pairs + 1
    above = above_ref[cols:, :].astype(F32)
    below = below_ref[cols:, :].astype(F32)
    for n, k in enumerate((0, 1, 4, 5)):
        side_ref[k, 0:1, :] = above[n : n + 1, :]
        side_ref[k, 1 : pairs + 1, :] = sides_ref[n]
        side_ref[k, pairs + 1 : pairs + 2, :] = below[n : n + 1, :]

    def ends(block):
        return (
            block[0:16, :].astype(F32)[0:1, :],
            block[cols - 16 : cols, :].astype(F32)[15:16, :],
        )

    for k, (high, low) in enumerate(zip(ends(above_ref[0:cols, :]), ends(below_ref[0:cols, :]))):
        side_ref[2 + k, 0:1, :] = high
        side_ref[2 + k, pairs + 1 : pairs + 2, :] = low

    def inner_side(g, carry):
        for k, end in enumerate(ends(field_ref[g])):
            side_ref[2 + k, pl.ds(g + 1, 1), :] = end
        return carry

    lax.fori_loop(0, pairs, inner_side, 0, unroll=4)

    def paired(k):
        return jnp.concatenate(
            [side_ref[k, 0:groups, :], side_ref[k, 1 : groups + 1, :]], axis=1
        ).astype(BF16)

    b1 = twice(b1_ref)
    b2 = twice(b2_ref)
    c = [paired(k) for k in range(6)]
    left = taps(c[1], k1_ref, 0)
    right = taps(c[4], k1_ref, 2)
    before = taps(c[0], k1_ref, 0) + taps(c[1], k1_ref, 1) + taps(c[2], k1_ref, 2) + b1
    after = taps(c[3], k1_ref, 0) + taps(c[4], k1_ref, 1) + taps(c[5], k1_ref, 2) + b1
    before = jnp.where(place_ref[0:1, :] > 0, gelu(before), 0.0)
    after = jnp.where(place_ref[1:2, :] > 0, gelu(after), 0.0)
    for n, (column, d) in enumerate(((before, 0), (after, 2))):
        side_ref[n, 0:groups, :] = column
        both = jnp.concatenate([side_ref[n, 0:pairs, :], side_ref[n, 1 : pairs + 1, :]], axis=1)
        halo_ref[n, 0:pairs, :] = taps(both.astype(BF16), k2_ref, d)

    def hidden(upper, lower, g):
        out = row_pair_conv(upper, lower, k1_ref, b1, left[g : g + 1, :], right[g : g + 1, :])
        return gelu(out).astype(BF16)

    def second(g, upper, lower):
        out = row_pair_conv(
            upper, lower, k2_ref, b2, halo_ref[0, pl.ds(g, 1), :], halo_ref[1, pl.ds(g, 1), :]
        )
        state = out + field_ref[g].astype(F32)
        state_ref[pl.ds(2 * g, 2)] = state.T.astype(BF16).reshape(2, chans, cols)

    second(0, hidden(above_ref[0:cols, :], field_ref[0], 0), hid_ref[1])
    second(pairs - 1, hid_ref[pairs - 1], hidden(field_ref[pairs - 1], below_ref[0:cols, :], pairs))

    def inner(g, carry):
        second(g, hid_ref[g], hid_ref[g + 1])
        return carry

    lax.fori_loop(1, pairs - 1, inner, 0, unroll=True)
    pos_copy.wait()

    def pick(d, carry):
        for rank in range(CAP):
            pos = jnp.maximum(pos_ref[rank, d], 0)
            send_ref[d, rank * chans : (rank + 1) * chans, :] = state_ref[pos]
        return carry

    lax.fori_loop(0, devices, pick, 0, unroll=16)


def outer_state(positions, place, field, hidden, sides, below, above, k1, b1, k2, b2):
    pairs, cols, lanes = field.shape
    chans = lanes // 2
    devices = positions.shape[1]
    return pl.pallas_call(
        outer_kernel,
        out_shape=jax.ShapeDtypeStruct((devices, CAP * chans, cols), BF16),
        in_specs=[vmem()] * 11,
        out_specs=vmem(),
        scratch_shapes=[
            pltpu.VMEM((6, pairs + 8, lanes), F32),
            pltpu.VMEM((2, pairs + 8, lanes), F32),
            pltpu.VMEM((2 * pairs, chans, cols), BF16),
            pltpu.SMEM(positions.shape, jnp.int32),
            pltpu.SemaphoreType.DMA,
        ],
        compiler_params=params(),
    )(positions, place, field, hidden, sides, below, above, k1, b1, k2, b2)


def backward_kernel(
    return_hbm,
    got_ref,
    table_ref,
    out_hbm,
    return_ref,
    rows_ref,
    out_ref,
    return_sem,
    out_sem,
):
    blocks, width = out_hbm.shape
    tables, seg, _ = table_ref.shape
    chans = width // seg
    parts = out_sem.shape[0]
    part = blocks // parts
    return_copy = pltpu.make_async_copy(return_hbm, return_ref, return_sem)
    return_copy.start()
    return_copy.wait()
    step = rows_ref.shape[1] // chans
    out_copies = []

    def finish(q):
        piece = pl.ds(q * part, part)
        for c in range(chans):
            out_ref[piece, c * seg : (c + 1) * seg] = rows_ref[
                q, c * step : c * step + part, :
            ].astype(BF16)
        out_copies.append(
            pltpu.make_async_copy(out_ref.at[piece], out_hbm.at[piece], out_sem.at[q])
        )
        out_copies[-1].start()

    for q in range(parts):
        if q > 0:
            finish(q - 1)
        for n in range(part):
            states, weights = [], []
            for t in range(2):
                code = return_ref[t, q * part + n]
                slot = code >> log2(tables)
                at = pl.multiple_of((slot & 1) * chans, chans)
                states.append(got_ref[slot >> 1, pl.ds(at, chans), :])
                weights.append(table_ref[code & (tables - 1)])
            rows_ref[q, pl.ds(n, chans, stride=step), :] = lax.dot_general(
                jnp.concatenate(states, axis=1),
                jnp.concatenate(weights, axis=1),
                NT,
                preferred_element_type=F32,
            )
    finish(parts - 1)
    for copy in out_copies:
        copy.wait()


def backward_remap(returns, got, back_table):
    blocks = returns.shape[1]
    chans = got.shape[1] // CAP
    seg = got.shape[2]
    parts = 4
    return pl.pallas_call(
        backward_kernel,
        out_shape=jax.ShapeDtypeStruct((blocks, chans * seg), BF16),
        in_specs=[hbm(), vmem(), vmem()],
        out_specs=hbm(),
        scratch_shapes=[
            pltpu.SMEM(returns.shape, jnp.int32),
            pltpu.VMEM((parts, chans * (blocks // parts + PAD), seg), F32),
            pltpu.VMEM((blocks, chans * seg), BF16),
            pltpu.SemaphoreType.DMA,
            pltpu.SemaphoreType.DMA((parts,)),
        ],
        compiler_params=params(),
    )(returns, got, back_table)


def exchange(buffer):
    return lax.all_to_all(buffer, AXES, split_axis=0, concat_axis=0, tiled=True)


def local(
    ll_blocks,
    dest_dev,
    dest_pos,
    fwd_id,
    back_id,
    fwd_table,
    back_table,
    kernel_one,
    bias_one,
    kernel_two,
    bias_two,
):
    n_fx = lax.axis_size("fx")
    n_fy = lax.axis_size("fy")
    hblocks = 64
    j = lax.axis_index("fy")
    place = jnp.stack([j > 0, j < n_fy - 1]).astype(jnp.int32)[:, None]
    place = jnp.broadcast_to(place, (2, 128))
    send, returns, w1, w2 = forward_remap(
        dest_dev,
        dest_pos,
        fwd_id,
        back_id,
        ll_blocks,
        fwd_table,
        kernel_one,
        kernel_two,
        n_fx * n_fy,
        n_fy,
    )
    send, place = lax.optimization_barrier((send, place))
    b1, b2 = bias_one[None], bias_two[None]
    field, up, down, sides, positions = sum_field(exchange(send), hblocks)
    below = lax.ppermute(up, "fx", [((i + 1) % n_fx, i) for i in range(n_fx)])
    above = lax.ppermute(down, "fx", [(i, (i + 1) % n_fx) for i in range(n_fx)])
    turned, hidden = inner_hidden(field, sides, w1, b1)
    send_back = outer_state(
        positions, place, turned, hidden, sides, below, above, w1, b1, w2, b2
    )
    return backward_remap(returns, exchange(send_back), back_table)


def solution(mesh):
    blocked = P(AXES, None)
    in_specs = (blocked,) * 5 + (P(),) * 6
    return jax.shard_map(
        local, mesh=mesh, in_specs=in_specs, out_specs=P(AXES, None), check_vma=False
    )
```

```python
import functools

import jax
import jax.numpy as jnp
from jax import lax
from jax.experimental import pallas as pl
from jax.experimental.pallas import tpu as pltpu
from jax.sharding import PartitionSpec as P

CAP = 2
PAD = 8
META = 8
AXES = ("fx", "fy")
F32 = jnp.float32
BF16 = jnp.bfloat16
VMEM_LIMIT = 40 * 1024 * 1024
NT = (((1,), (1,)), ((), ()))


def smem():
    return pl.BlockSpec(memory_space=pltpu.SMEM)


def vmem():
    return pl.BlockSpec(memory_space=pltpu.VMEM)


def hbm():
    return pl.BlockSpec(memory_space=pl.ANY)


def params():
    return pltpu.CompilerParams(vmem_limit_bytes=VMEM_LIMIT)


def in_hbm(x):
    return pltpu.with_memory_space_constraint(x, pltpu.HBM)


def log2(count):
    assert count & (count - 1) == 0
    return count.bit_length() - 1


def lane_iota(shape):
    return lax.broadcasted_iota(jnp.int32, shape, len(shape) - 1)


def row_pair_weights(taps_ref, weights_ref):
    _, columns, chans, _ = taps_ref.shape
    none = jnp.zeros((chans, chans), BF16)
    for q in range(4):
        for d in range(columns):
            upper = taps_ref[q, d] if q < 3 else none
            lower = taps_ref[q - 1, d] if q > 0 else none
            weights_ref[q * chans : (q + 1) * chans, 2 * d * chans : 2 * (d + 1) * chans] = (
                jnp.concatenate([upper, lower], axis=1)
            )


def forward_kernel(
    n_fy,
    dev_hbm,
    pos_hbm,
    fwd_hbm,
    back_hbm,
    x_hbm,
    table_hbm,
    k1_hbm,
    k2_hbm,
    send_ref,
    return_hbm,
    w1_ref,
    w2_ref,
    dev_ref,
    pos_ref,
    fwd_ref,
    back_ref,
    return_ref,
    x_ref,
    table_ref,
    taps_ref,
    rows_ref,
    edge_ref,
    meta_ref,
    count_ref,
    code_sem,
    x_sem,
    table_sem,
    taps_sem,
    return_sem,
):
    blocks, width = x_ref.shape
    tables, seg, _ = table_ref.shape
    chans = width // seg
    devices = count_ref.shape[0]
    assert n_fy == 1 << log2(n_fy)
    parts = x_sem.shape[0]
    wide = width // parts
    step = rows_ref.shape[0] // chans
    pieces = table_sem.shape[0]
    deep = tables // pieces
    x_copies = [
        pltpu.make_async_copy(
            x_hbm.at[:, pl.ds(q * wide, wide)], x_ref.at[:, pl.ds(q * wide, wide)], x_sem.at[q]
        )
        for q in range(parts)
    ]
    table_copies = [
        pltpu.make_async_copy(
            table_hbm.at[pl.ds(q * deep, deep)], table_ref.at[pl.ds(q * deep, deep)], table_sem.at[q]
        )
        for q in range(pieces)
    ]
    code_copies = [
        pltpu.make_async_copy(source, target, code_sem.at[n])
        for n, (source, target) in enumerate(
            ((dev_hbm, dev_ref), (pos_hbm, pos_ref), (fwd_hbm, fwd_ref), (back_hbm, back_ref))
        )
    ]
    taps_copies = [
        pltpu.make_async_copy(source, taps_ref.at[n], taps_sem.at[n])
        for n, source in enumerate((k1_hbm, k2_hbm))
    ]
    for copy in code_copies + x_copies + taps_copies + table_copies:
        copy.start()

    def clear(d, carry):
        count_ref[d] = 0
        return carry

    lax.fori_loop(0, devices, clear, 0, unroll=8)
    meta_ref[...] = jnp.zeros_like(meta_ref)
    for copy in code_copies:
        copy.wait()

    def plan(b, carry):
        for t in range(2):
            dev = dev_ref[t, b]
            rank = count_ref[dev]
            count_ref[dev] = rank + 1
            return_ref[t, b] = ((dev * CAP + rank) << log2(tables)) + back_ref[t, b]
            pos = (pos_ref[t, b] + 1).astype(F32)
            meta_ref[pl.ds(dev * META + 4 + rank, 1), :] = jnp.full((1, seg), pos, F32)
        return carry

    lax.fori_loop(0, blocks, plan, 0, unroll=8)
    return_copy = pltpu.make_async_copy(return_ref, return_hbm, return_sem)
    return_copy.start()
    both = jnp.where(
        lane_iota((devices, seg)) < chans,
        meta_ref[pl.ds(4, devices, stride=META), :],
        meta_ref[pl.ds(5, devices, stride=META), :],
    )
    col = lax.broadcasted_iota(jnp.int32, both.shape, 0) & (n_fy - 1)
    meta_ref[pl.ds(6, devices, stride=META), :] = jnp.where(
        col > 0, pltpu.roll(both, 1, axis=0), 0.0
    )
    meta_ref[pl.ds(7, devices, stride=META), :] = jnp.where(
        col < n_fy - 1, pltpu.roll(both, devices - 1, axis=0), 0.0
    )
    for q, copy in enumerate(x_copies):
        copy.wait()
        for c in range(q * wide // seg, (q + 1) * wide // seg):
            rows_ref[c * step : c * step + blocks, :] = x_ref[:, c * seg : (c + 1) * seg].astype(F32)
    for n, (copy, weights_ref) in enumerate(zip(taps_copies, (w1_ref, w2_ref))):
        copy.wait()
        row_pair_weights(taps_ref.at[n], weights_ref)
    for q, copy in enumerate(table_copies):
        copy.wait()

        def edges(n, carry):
            edge_ref[n, 0:2, :] = table_ref[n, seg - 16 : seg, :].astype(F32)[14:16, :]
            edge_ref[n, 2:4, :] = table_ref[n, 0:16, :].astype(F32)[0:2, :]
            return carry

        lax.fori_loop(q * deep, (q + 1) * deep, edges, 0, unroll=4)
    lane = lane_iota((1, seg))

    def one_block(b, carry):
        tables_of = [fwd_ref[t, b] for t in range(2)]
        x = rows_ref[pl.ds(b, chans, stride=step), :].astype(BF16)
        weights = jnp.concatenate([table_ref[n] for n in tables_of], axis=0)
        product = lax.dot_general(x, weights, NT, preferred_element_type=F32)
        tips = jnp.concatenate([edge_ref[n] for n in tables_of], axis=0).astype(BF16)
        ends = lax.dot_general(tips, x, NT, preferred_element_type=F32)
        ends = jnp.concatenate([ends, ends], axis=1)
        for t in range(2):
            slot = return_ref[t, b] >> log2(tables)
            dev, rank = slot >> 1, slot & 1
            at = pl.multiple_of(rank * chans, chans)
            send_ref[dev, pl.ds(at, chans), :] = product[:, t * seg : (t + 1) * seg].astype(BF16)
            col = dev & (n_fy - 1)
            for side in range(2):
                inside = (col < n_fy - 1) if side == 0 else (col > 0)
                near = jnp.where(inside, dev + 1 - 2 * side, devices)
                first = t * 4 + side * 2
                meta_ref[pl.ds(near * META + 2 * side + rank, 1), :] = jnp.where(
                    lane < chans, ends[first : first + 1, :], ends[first + 1 : first + 2, :]
                )
        return carry

    lax.fori_loop(0, blocks, one_block, 0, unroll=True)
    send_ref[:, CAP * chans :, :] = (
        meta_ref[0 : devices * META, :].astype(BF16).reshape(devices, META, seg)
    )
    return_copy.wait()


def forward_remap(
    dest_dev, dest_pos, fwd_id, back_id, ll_blocks, fwd_table, k1, k2, devices, n_fy
):
    blocks, width = ll_blocks.shape
    tables, seg, _ = fwd_table.shape
    chans = width // seg
    return pl.pallas_call(
        functools.partial(forward_kernel, n_fy),
        out_shape=(
            jax.ShapeDtypeStruct((devices, CAP * chans + META, seg), BF16),
            jax.ShapeDtypeStruct((2, blocks), jnp.int32),
            jax.ShapeDtypeStruct((4 * chans, 6 * chans), BF16),
            jax.ShapeDtypeStruct((4 * chans, 6 * chans), BF16),
        ),
        in_specs=[hbm()] * 8,
        out_specs=(vmem(), hbm(), vmem(), vmem()),
        scratch_shapes=[
            pltpu.SMEM((2, blocks), jnp.int32),
            pltpu.SMEM((2, blocks), jnp.int32),
            pltpu.SMEM((2, blocks), jnp.int32),
            pltpu.SMEM((2, blocks), jnp.int32),
            pltpu.SMEM((2, blocks), jnp.int32),
            pltpu.VMEM((blocks, width), BF16),
            pltpu.VMEM((tables, seg, seg), BF16),
            pltpu.VMEM((2,) + k1.shape, BF16),
            pltpu.VMEM((chans * (blocks + PAD), seg), F32),
            pltpu.VMEM((tables, 4, seg), F32),
            pltpu.VMEM(((devices + 1) * META, seg), F32),
            pltpu.SMEM((devices,), jnp.int32),
            pltpu.SemaphoreType.DMA((4,)),
            pltpu.SemaphoreType.DMA((4,)),
            pltpu.SemaphoreType.DMA((8,)),
            pltpu.SemaphoreType.DMA((2,)),
            pltpu.SemaphoreType.DMA,
        ],
        compiler_params=params(),
    )(
        *(in_hbm(route.T) for route in (dest_dev, dest_pos, fwd_id, back_id)),
        *(in_hbm(x) for x in (ll_blocks, fwd_table, k1, k2)),
    )


def sum_kernel(
    got_ref,
    field_ref,
    up_ref,
    down_ref,
    side_ref,
    pos_ref,
    rows_ref,
    sum0_ref,
    sum1_ref,
    spot_ref,
    spot_sem,
):
    devices, _, cols = got_ref.shape
    hblocks, chans, _ = field_ref.shape
    pairs = hblocks // 2
    lanes = 2 * chans
    rows_ref[...] = got_ref[:, CAP * chans :, :].reshape(devices * META, lanes).astype(F32)

    def meta_row(n):
        return rows_ref[pl.ds(n, devices, stride=META), :]

    lane = lane_iota((devices, lanes))
    table = jnp.where(lane % 2 == 0, meta_row(4), meta_row(5))
    beside = [meta_row(6), meta_row(7)]
    for side in range(2):
        turned_half = pltpu.roll(beside[side], chans, axis=1)
        for rank in range(CAP):
            here = lane == 2 + 2 * side + rank
            table = jnp.where(here, beside[side] if rank == 0 else turned_half, table)
    spots = table.T[0:8, :].astype(jnp.int32) - 1
    pos_ref[...] = spots
    spot_copy = pltpu.make_async_copy(pos_ref, spot_ref, spot_sem)
    spot_copy.start()

    def clear(r, carry):
        for rank in range(CAP):
            (sum0_ref, sum1_ref)[rank][r] = jnp.zeros((chans, cols), F32)
        return carry

    lax.fori_loop(0, hblocks, clear, 0, unroll=4)
    block = lax.broadcasted_iota(jnp.int32, (pairs, devices), 0)
    low = lane_iota((pairs, lanes)) < chans
    for side in range(2):
        sums = []
        for parity in range(2):
            total = jnp.zeros((pairs, lanes), F32)
            for rank in range(CAP):
                n = 2 + 2 * side + rank
                hit = (spots[n : n + 1, :] == 2 * block + parity).astype(F32).astype(BF16)
                total += jnp.dot(
                    hit, meta_row(2 * side + rank).astype(BF16), preferred_element_type=F32
                )
            sums.append(total)
        even, odd = sums
        side_ref[2 * side] = jnp.where(low, even, pltpu.roll(odd, chans, axis=1))
        side_ref[2 * side + 1] = jnp.where(low, pltpu.roll(even, chans, axis=1), odd)
    spot_copy.wait()

    def add(d, carry):
        rows, sums = [], []
        for rank, sum_ref in enumerate((sum0_ref, sum1_ref)):
            pos = spot_ref[rank, d]
            rows.append(jnp.where(pos < 0, hblocks, pos))
            block = got_ref[d, rank * chans : (rank + 1) * chans, :]
            sums.append(sum_ref[rows[-1]] + block.astype(F32))
        sum0_ref[rows[0]] = sums[0]
        sum1_ref[rows[1]] = sums[1]
        return carry

    lax.fori_loop(0, devices, add, 0, unroll=16)

    def total_of(r):
        return sum0_ref[r] + sum1_ref[r]

    corners = jnp.zeros((up_ref.shape[0] - cols, lanes), F32)
    corner_row = lax.broadcasted_iota(jnp.int32, corners.shape, 0)
    for ref, g in ((up_ref, 0), (down_ref, pairs - 1)):
        ref[0:cols, :] = jnp.concatenate([total_of(2 * g), total_of(2 * g + 1)], axis=0).T.astype(BF16)
        rest = corners
        for n in range(4):
            rest = jnp.where(corner_row == n, side_ref[n, g : g + 1, :], rest)
        ref[cols:, :] = rest.astype(BF16)

    def finish(r, carry):
        field_ref[r] = total_of(r).astype(BF16)
        return carry

    lax.fori_loop(0, hblocks, finish, 0, unroll=4)


def sum_field(got, hblocks):
    devices, depth, cols = got.shape
    chans = (depth - META) // CAP
    pairs = hblocks // 2
    message = jax.ShapeDtypeStruct((cols + 16, 2 * chans), BF16)
    return pl.pallas_call(
        sum_kernel,
        out_shape=(
            jax.ShapeDtypeStruct((hblocks, chans, cols), BF16),
            message,
            message,
            jax.ShapeDtypeStruct((4, pairs, 2 * chans), F32),
            jax.ShapeDtypeStruct((8, devices), jnp.int32),
        ),
        in_specs=[vmem()],
        out_specs=(vmem(),) * 5,
        scratch_shapes=[
            pltpu.VMEM((devices * META, cols), F32),
            pltpu.VMEM((hblocks + 1, chans, cols), F32),
            pltpu.VMEM((hblocks + 1, chans, cols), F32),
            pltpu.SMEM((8, devices), jnp.int32),
            pltpu.SemaphoreType.DMA,
        ],
        compiler_params=params(),
    )(got)


def gelu(x):
    return 0.5 * x * (1.0 + jnp.tanh(0.7978845608028654 * (x + 0.044715 * (x * x * x))))


def taps(x, weights_ref, d):
    lanes = x.shape[1] // 2
    return jnp.dot(x, weights_ref[:, d * lanes : (d + 1) * lanes], preferred_element_type=F32)


def row_pair_conv(upper, lower, weights_ref, bias, before, after):
    cols, lanes = upper.shape
    rows = jnp.concatenate([upper, lower], axis=1)
    product = jnp.dot(rows, weights_ref[...], preferred_element_type=F32)
    ahead = pltpu.roll(product[:, 0:lanes], 1, axis=0)
    behind = pltpu.roll(product[:, 2 * lanes :], cols - 1, axis=0)
    edge = lax.broadcasted_iota(jnp.int32, (8, lanes), 0)
    first = jnp.where(edge == 0, before, ahead[0:8, :])
    last = jnp.where(edge == 7, after, behind[cols - 8 :, :])
    ahead = jnp.concatenate([first, ahead[8:, :]], axis=0)
    behind = jnp.concatenate([behind[: cols - 8, :], last], axis=0)
    return product[:, lanes : 2 * lanes] + ahead + behind + bias


def twice(bias_ref):
    return jnp.concatenate([bias_ref[...], bias_ref[...]], axis=1)


def column_ends(block):
    cols = block.shape[0]
    return (
        block[0:16, :].astype(F32)[0:1, :],
        block[cols - 16 : cols, :].astype(F32)[15:16, :],
    )


def side_columns(columns, weights_ref, bias, place_ref):
    c = columns
    left = taps(c[1], weights_ref, 0)
    right = taps(c[4], weights_ref, 2)
    before = taps(c[0], weights_ref, 0) + taps(c[1], weights_ref, 1) + taps(c[2], weights_ref, 2)
    after = taps(c[3], weights_ref, 0) + taps(c[4], weights_ref, 1) + taps(c[5], weights_ref, 2)
    before = jnp.where(place_ref[0:1, :] > 0, gelu(before + bias), 0.0)
    after = jnp.where(place_ref[1:2, :] > 0, gelu(after + bias), 0.0)
    return left, right, before, after


def put_state(state_ref, g, out, field):
    _, chans, cols = state_ref.shape
    state = out + field.astype(F32)
    state_ref[pl.ds(2 * g, 2)] = state.T.astype(BF16).reshape(2, chans, cols)


def inner_kernel(
    field_ref,
    side_ref,
    place_ref,
    k1_ref,
    b1_ref,
    k2_ref,
    b2_ref,
    ends_ref,
    hids_ref,
    cols_ref,
    state_ref,
    turned_ref,
    hid_ref,
    column_ref,
    halo_ref,
):
    hblocks, chans, cols = field_ref.shape
    pairs = hblocks // 2

    def turn(g, carry):
        turned_ref[g] = field_ref[pl.ds(2 * g, 2)].reshape(2 * chans, cols).T
        return carry

    lax.fori_loop(0, pairs, turn, 0, unroll=True)
    for n, k in enumerate((0, 1, 4, 5)):
        column_ref[k, 0:pairs, :] = side_ref[n]

    def inner_side(g, carry):
        for k, end in enumerate(column_ends(turned_ref[g])):
            column_ref[2 + k, pl.ds(g, 1), :] = end
        return carry

    lax.fori_loop(0, pairs, inner_side, 0, unroll=4)
    b1 = twice(b1_ref)
    b2 = twice(b2_ref)
    columns = [
        jnp.concatenate([column_ref[k, 0 : pairs - 1, :], column_ref[k, 1:pairs, :]], axis=1).astype(
            BF16
        )
        for k in range(6)
    ]
    left, right, before, after = side_columns(columns, k1_ref, b1, place_ref)
    halo_ref[0, 1:pairs, :] = left
    halo_ref[1, 1:pairs, :] = right
    cols_ref[...] = jnp.zeros_like(cols_ref)
    for n, (column, d) in enumerate(((before, 0), (after, 2))):
        cols_ref[n : n + 1, :] = column[0:1, :]
        cols_ref[2 + n : 3 + n, :] = column[pairs - 2 : pairs - 1, :]
        column_ref[n, 1:pairs, :] = column
        both = jnp.concatenate(
            [column_ref[n, 1 : pairs - 1, :], column_ref[n, 2:pairs, :]], axis=1
        )
        halo_ref[2 + n, 1 : pairs - 1, :] = taps(both.astype(BF16), k2_ref, d)

    def halos(h, g):
        return halo_ref[h, pl.ds(g, 1), :], halo_ref[h + 1, pl.ds(g, 1), :]

    def first(g, carry):
        out = row_pair_conv(turned_ref[g - 1], turned_ref[g], k1_ref, b1, *halos(0, g))
        hid_ref[g] = gelu(out).astype(BF16)
        return carry

    lax.fori_loop(1, pairs, first, 0, unroll=True)

    def second(g, carry):
        out = row_pair_conv(hid_ref[g], hid_ref[g + 1], k2_ref, b2, *halos(2, g))
        put_state(state_ref, g, out, turned_ref[g])
        return carry

    lax.fori_loop(1, pairs - 1, second, 0, unroll=True)
    for n, g in enumerate((0, pairs - 1)):
        ends_ref[n] = turned_ref[g]
    for n, g in enumerate((1, pairs - 1)):
        hids_ref[n] = hid_ref[g]


def inner_state(field, sides, place, k1, b1, k2, b2):
    hblocks, chans, cols = field.shape
    pairs = hblocks // 2
    lanes = 2 * chans
    two = jax.ShapeDtypeStruct((2, cols, lanes), BF16)
    return pl.pallas_call(
        inner_kernel,
        out_shape=(
            two,
            two,
            jax.ShapeDtypeStruct((8, lanes), F32),
            jax.ShapeDtypeStruct((hblocks, chans, cols), BF16),
        ),
        in_specs=[vmem()] * 7,
        out_specs=(vmem(),) * 4,
        scratch_shapes=[
            pltpu.VMEM((pairs, cols, lanes), BF16),
            pltpu.VMEM((pairs, cols, lanes), BF16),
            pltpu.VMEM((6, pairs + 8, lanes), F32),
            pltpu.VMEM((4, pairs + 8, lanes), F32),
        ],
        compiler_params=params(),
        cost_estimate=pl.CostEstimate(
            flops=4 * 8192 * 9 * 64 * 64, bytes_accessed=4 << 20, transcendentals=1 << 19
        ),
    )(field, sides, place, k1, b1, k2, b2)


def outer_kernel(
    pos_hbm,
    place_ref,
    ends_ref,
    hids_ref,
    cols_ref,
    inner_ref,
    sides_ref,
    below_ref,
    above_ref,
    k1_ref,
    b1_ref,
    k2_ref,
    b2_ref,
    send_ref,
    column_ref,
    state_ref,
    pos_ref,
    pos_sem,
):
    pos_copy = pltpu.make_async_copy(pos_hbm, pos_ref, pos_sem)
    pos_copy.start()
    hblocks, chans, cols = inner_ref.shape
    pairs = hblocks // 2
    devices = pos_ref.shape[1]
    state_ref[pl.ds(2, hblocks - 4)] = inner_ref[pl.ds(2, hblocks - 4)]
    column_ref[...] = jnp.zeros_like(column_ref)
    above = above_ref[cols:, :].astype(F32)
    below = below_ref[cols:, :].astype(F32)
    for n, k in enumerate((0, 1, 4, 5)):
        column_ref[k, 0, 0:1, :] = above[n : n + 1, :]
        column_ref[k, 0, 1:2, :] = sides_ref[n, pairs - 1 : pairs, :]
        column_ref[k, 1, 0:1, :] = sides_ref[n, 0:1, :]
        column_ref[k, 1, 1:2, :] = below[n : n + 1, :]
    for part, row, block in (
        (0, 0, above_ref[0:cols, :]),
        (0, 1, ends_ref[1]),
        (1, 0, ends_ref[0]),
        (1, 1, below_ref[0:cols, :]),
    ):
        for k, end in enumerate(column_ends(block)):
            column_ref[2 + k, part, row : row + 1, :] = end
    b1 = twice(b1_ref)
    b2 = twice(b2_ref)
    columns = [
        jnp.concatenate([column_ref[k, 0], column_ref[k, 1]], axis=1).astype(BF16) for k in range(6)
    ]
    left, right, before, after = side_columns(columns, k1_ref, b1, place_ref)
    top = lax.broadcasted_iota(jnp.int32, before.shape, 0) == 0
    halos = []
    for n, (column, d) in enumerate(((before, 0), (after, 2))):
        upper = jnp.where(top, column, cols_ref[2 + n : 3 + n, :])
        lower = jnp.where(top, cols_ref[n : n + 1, :], column)
        both = jnp.concatenate([upper, lower], axis=1).astype(BF16)
        halos.append(taps(both, k2_ref, d))

    def hidden(upper, lower, row):
        sides = left[row : row + 1, :], right[row : row + 1, :]
        return gelu(row_pair_conv(upper, lower, k1_ref, b1, *sides)).astype(BF16)

    def second(g, upper, lower, row):
        sides = (halo[row : row + 1, :] for halo in halos)
        out = row_pair_conv(upper, lower, k2_ref, b2, *sides)
        put_state(state_ref, g, out, ends_ref[row])

    second(0, hidden(above_ref[0:cols, :], ends_ref[0], 0), hids_ref[0], 0)
    second(pairs - 1, hids_ref[1], hidden(ends_ref[1], below_ref[0:cols, :], 1), 1)
    pos_copy.wait()

    def pick(d, carry):
        for rank in range(CAP):
            pos = jnp.maximum(pos_ref[rank, d], 0)
            send_ref[d, rank * chans : (rank + 1) * chans, :] = state_ref[pos]
        return carry

    lax.fori_loop(0, devices, pick, 0, unroll=16)


def outer_state(positions, place, ends, hids, columns, inner, sides, below, above, k1, b1, k2, b2):
    hblocks, chans, cols = inner.shape
    devices = positions.shape[1]
    return pl.pallas_call(
        outer_kernel,
        out_shape=jax.ShapeDtypeStruct((devices, CAP * chans, cols), BF16),
        in_specs=[vmem()] * 13,
        out_specs=vmem(),
        scratch_shapes=[
            pltpu.VMEM((6, 2, 8, 2 * chans), F32),
            pltpu.VMEM((hblocks, chans, cols), BF16),
            pltpu.SMEM(positions.shape, jnp.int32),
            pltpu.SemaphoreType.DMA,
        ],
        compiler_params=params(),
    )(positions, place, ends, hids, columns, inner, sides, below, above, k1, b1, k2, b2)


def backward_kernel(
    return_hbm,
    got_ref,
    table_ref,
    out_hbm,
    return_ref,
    rows_ref,
    out_ref,
    return_sem,
    out_sem,
):
    blocks, width = out_hbm.shape
    tables, seg, _ = table_ref.shape
    chans = width // seg
    parts = out_sem.shape[0]
    part = blocks // parts
    return_copy = pltpu.make_async_copy(return_hbm, return_ref, return_sem)
    return_copy.start()
    return_copy.wait()
    step = rows_ref.shape[1] // chans
    out_copies = []

    def finish(q):
        piece = pl.ds(q * part, part)
        for c in range(chans):
            out_ref[piece, c * seg : (c + 1) * seg] = rows_ref[
                q, c * step : c * step + part, :
            ].astype(BF16)
        out_copies.append(
            pltpu.make_async_copy(out_ref.at[piece], out_hbm.at[piece], out_sem.at[q])
        )
        out_copies[-1].start()

    for q in range(parts):
        if q > 0:
            finish(q - 1)
        for n in range(part):
            states, weights = [], []
            for t in range(2):
                code = return_ref[t, q * part + n]
                slot = code >> log2(tables)
                at = pl.multiple_of((slot & 1) * chans, chans)
                states.append(got_ref[slot >> 1, pl.ds(at, chans), :])
                weights.append(table_ref[code & (tables - 1)])
            rows_ref[q, pl.ds(n, chans, stride=step), :] = lax.dot_general(
                jnp.concatenate(states, axis=1),
                jnp.concatenate(weights, axis=1),
                NT,
                preferred_element_type=F32,
            )
    finish(parts - 1)
    for copy in out_copies:
        copy.wait()


def backward_remap(returns, got, back_table):
    blocks = returns.shape[1]
    chans = got.shape[1] // CAP
    seg = got.shape[2]
    parts = 4
    return pl.pallas_call(
        backward_kernel,
        out_shape=jax.ShapeDtypeStruct((blocks, chans * seg), BF16),
        in_specs=[hbm(), vmem(), vmem()],
        out_specs=hbm(),
        scratch_shapes=[
            pltpu.SMEM(returns.shape, jnp.int32),
            pltpu.VMEM((parts, chans * (blocks // parts + PAD), seg), F32),
            pltpu.VMEM((blocks, chans * seg), BF16),
            pltpu.SemaphoreType.DMA,
            pltpu.SemaphoreType.DMA((parts,)),
        ],
        compiler_params=params(),
    )(returns, got, back_table)


def exchange(buffer):
    return lax.all_to_all(buffer, AXES, split_axis=0, concat_axis=0, tiled=True)


def local(
    ll_blocks,
    dest_dev,
    dest_pos,
    fwd_id,
    back_id,
    fwd_table,
    back_table,
    kernel_one,
    bias_one,
    kernel_two,
    bias_two,
):
    n_fx = lax.axis_size("fx")
    n_fy = lax.axis_size("fy")
    hblocks = 64
    j = lax.axis_index("fy")
    place = jnp.stack([j > 0, j < n_fy - 1]).astype(jnp.int32)[:, None]
    place = jnp.broadcast_to(place, (2, 128))
    send, returns, w1, w2 = forward_remap(
        dest_dev,
        dest_pos,
        fwd_id,
        back_id,
        ll_blocks,
        fwd_table,
        kernel_one,
        kernel_two,
        n_fx * n_fy,
        n_fy,
    )
    send, place = lax.optimization_barrier((send, place))
    b1, b2 = bias_one[None], bias_two[None]
    field, up, down, sides, positions = sum_field(exchange(send), hblocks)
    below = lax.ppermute(up, "fx", [((i + 1) % n_fx, i) for i in range(n_fx)])
    above = lax.ppermute(down, "fx", [(i, (i + 1) % n_fx) for i in range(n_fx)])
    ends, hids, columns, inner = inner_state(field, sides, place, w1, b1, w2, b2)
    send_back = outer_state(
        positions, place, ends, hids, columns, inner, sides, below, above, w1, b1, w2, b2
    )
    return backward_remap(returns, exchange(send_back), back_table)


def solution(mesh):
    blocked = P(AXES, None)
    in_specs = (blocked,) * 5 + (P(),) * 6
    return jax.shard_map(
        local, mesh=mesh, in_specs=in_specs, out_specs=P(AXES, None), check_vma=False
    )
```

```python
import functools

import jax
import jax.numpy as jnp
from jax import lax
from jax.experimental import pallas as pl
from jax.experimental.pallas import tpu as pltpu
from jax.sharding import PartitionSpec as P

CAP = 2
PAD = 8
META = 8
AXES = ("fx", "fy")
F32 = jnp.float32
BF16 = jnp.bfloat16
VMEM_LIMIT = 40 * 1024 * 1024
NT = (((1,), (1,)), ((), ()))


def smem():
    return pl.BlockSpec(memory_space=pltpu.SMEM)


def vmem():
    return pl.BlockSpec(memory_space=pltpu.VMEM)


def hbm():
    return pl.BlockSpec(memory_space=pl.ANY)


def params():
    return pltpu.CompilerParams(vmem_limit_bytes=VMEM_LIMIT)


def in_hbm(x):
    return pltpu.with_memory_space_constraint(x, pltpu.HBM)


def log2(count):
    assert count & (count - 1) == 0
    return count.bit_length() - 1


def lane_iota(shape):
    return lax.broadcasted_iota(jnp.int32, shape, len(shape) - 1)


def row_pair_weights(taps_ref, weights_ref):
    _, columns, chans, _ = taps_ref.shape
    none = jnp.zeros((chans, chans), BF16)
    for q in range(4):
        for d in range(columns):
            upper = taps_ref[q, d] if q < 3 else none
            lower = taps_ref[q - 1, d] if q > 0 else none
            weights_ref[q * chans : (q + 1) * chans, 2 * d * chans : 2 * (d + 1) * chans] = (
                jnp.concatenate([upper, lower], axis=1)
            )


def forward_kernel(
    n_fy,
    dev_hbm,
    pos_hbm,
    fwd_hbm,
    back_hbm,
    x_hbm,
    table_hbm,
    k1_hbm,
    k2_hbm,
    send_ref,
    return_hbm,
    w1_ref,
    w2_ref,
    dev_ref,
    pos_ref,
    fwd_ref,
    back_ref,
    return_ref,
    x_ref,
    table_ref,
    taps_ref,
    rows_ref,
    edge_ref,
    meta_ref,
    count_ref,
    code_sem,
    x_sem,
    table_sem,
    taps_sem,
    return_sem,
):
    blocks, width = x_ref.shape
    tables, seg, _ = table_ref.shape
    chans = width // seg
    devices = count_ref.shape[0]
    assert n_fy == 1 << log2(n_fy)
    parts = x_sem.shape[0]
    wide = width // parts
    step = rows_ref.shape[0] // chans
    pieces = table_sem.shape[0]
    deep = tables // pieces
    x_copies = [
        pltpu.make_async_copy(
            x_hbm.at[:, pl.ds(q * wide, wide)], x_ref.at[:, pl.ds(q * wide, wide)], x_sem.at[q]
        )
        for q in range(parts)
    ]
    table_copies = [
        pltpu.make_async_copy(
            table_hbm.at[pl.ds(q * deep, deep)], table_ref.at[pl.ds(q * deep, deep)], table_sem.at[q]
        )
        for q in range(pieces)
    ]
    code_copies = [
        pltpu.make_async_copy(source, target, code_sem.at[n])
        for n, (source, target) in enumerate(
            ((dev_hbm, dev_ref), (pos_hbm, pos_ref), (fwd_hbm, fwd_ref), (back_hbm, back_ref))
        )
    ]
    taps_copies = [
        pltpu.make_async_copy(source, taps_ref.at[n], taps_sem.at[n])
        for n, source in enumerate((k1_hbm, k2_hbm))
    ]
    for copy in code_copies + x_copies + taps_copies + table_copies:
        copy.start()

    def clear(d, carry):
        count_ref[d] = 0
        return carry

    lax.fori_loop(0, devices, clear, 0, unroll=8)
    meta_ref[...] = jnp.zeros_like(meta_ref)
    for copy in code_copies:
        copy.wait()

    def plan(b, carry):
        for t in range(2):
            dev = dev_ref[t, b]
            rank = count_ref[dev]
            count_ref[dev] = rank + 1
            return_ref[t, b] = ((dev * CAP + rank) << log2(tables)) + back_ref[t, b]
            pos = (pos_ref[t, b] + 1).astype(F32)
            meta_ref[pl.ds(dev * META + 4 + rank, 1), :] = jnp.full((1, seg), pos, F32)
        return carry

    lax.fori_loop(0, blocks, plan, 0, unroll=8)
    return_copy = pltpu.make_async_copy(return_ref, return_hbm, return_sem)
    return_copy.start()
    both = jnp.where(
        lane_iota((devices, seg)) < chans,
        meta_ref[pl.ds(4, devices, stride=META), :],
        meta_ref[pl.ds(5, devices, stride=META), :],
    )
    col = lax.broadcasted_iota(jnp.int32, both.shape, 0) & (n_fy - 1)
    meta_ref[pl.ds(6, devices, stride=META), :] = jnp.where(
        col > 0, pltpu.roll(both, 1, axis=0), 0.0
    )
    meta_ref[pl.ds(7, devices, stride=META), :] = jnp.where(
        col < n_fy - 1, pltpu.roll(both, devices - 1, axis=0), 0.0
    )
    for q, copy in enumerate(x_copies):
        copy.wait()
        for c in range(q * wide // seg, (q + 1) * wide // seg):
            rows_ref[c * step : c * step + blocks, :] = x_ref[:, c * seg : (c + 1) * seg].astype(F32)
    for n, (copy, weights_ref) in enumerate(zip(taps_copies, (w1_ref, w2_ref))):
        copy.wait()
        row_pair_weights(taps_ref.at[n], weights_ref)
    for q, copy in enumerate(table_copies):
        copy.wait()

        def edges(n, carry):
            edge_ref[n, 0:2, :] = table_ref[n, seg - 16 : seg, :].astype(F32)[14:16, :]
            edge_ref[n, 2:4, :] = table_ref[n, 0:16, :].astype(F32)[0:2, :]
            return carry

        lax.fori_loop(q * deep, (q + 1) * deep, edges, 0, unroll=4)
    lane = lane_iota((1, seg))

    def one_block(b, carry):
        tables_of = [fwd_ref[t, b] for t in range(2)]
        x = rows_ref[pl.ds(b, chans, stride=step), :].astype(BF16)
        weights = jnp.concatenate([table_ref[n] for n in tables_of], axis=0)
        product = lax.dot_general(x, weights, NT, preferred_element_type=F32)
        tips = jnp.concatenate([edge_ref[n] for n in tables_of], axis=0).astype(BF16)
        ends = lax.dot_general(tips, x, NT, preferred_element_type=F32)
        ends = jnp.concatenate([ends, ends], axis=1)
        for t in range(2):
            slot = return_ref[t, b] >> log2(tables)
            dev, rank = slot >> 1, slot & 1
            at = pl.multiple_of(rank * chans, chans)
            send_ref[dev, pl.ds(at, chans), :] = product[:, t * seg : (t + 1) * seg].astype(BF16)
            col = dev & (n_fy - 1)
            for side in range(2):
                inside = (col < n_fy - 1) if side == 0 else (col > 0)
                near = jnp.where(inside, dev + 1 - 2 * side, devices)
                first = t * 4 + side * 2
                meta_ref[pl.ds(near * META + 2 * side + rank, 1), :] = jnp.where(
                    lane < chans, ends[first : first + 1, :], ends[first + 1 : first + 2, :]
                )
        return carry

    lax.fori_loop(0, blocks, one_block, 0, unroll=True)
    send_ref[:, CAP * chans :, :] = (
        meta_ref[0 : devices * META, :].astype(BF16).reshape(devices, META, seg)
    )
    return_copy.wait()


def forward_remap(
    dest_dev, dest_pos, fwd_id, back_id, ll_blocks, fwd_table, k1, k2, devices, n_fy
):
    blocks, width = ll_blocks.shape
    tables, seg, _ = fwd_table.shape
    chans = width // seg
    return pl.pallas_call(
        functools.partial(forward_kernel, n_fy),
        out_shape=(
            jax.ShapeDtypeStruct((devices, CAP * chans + META, seg), BF16),
            jax.ShapeDtypeStruct((2, blocks), jnp.int32),
            jax.ShapeDtypeStruct((4 * chans, 6 * chans), BF16),
            jax.ShapeDtypeStruct((4 * chans, 6 * chans), BF16),
        ),
        in_specs=[hbm()] * 8,
        out_specs=(vmem(), hbm(), vmem(), vmem()),
        scratch_shapes=[
            pltpu.SMEM((2, blocks), jnp.int32),
            pltpu.SMEM((2, blocks), jnp.int32),
            pltpu.SMEM((2, blocks), jnp.int32),
            pltpu.SMEM((2, blocks), jnp.int32),
            pltpu.SMEM((2, blocks), jnp.int32),
            pltpu.VMEM((blocks, width), BF16),
            pltpu.VMEM((tables, seg, seg), BF16),
            pltpu.VMEM((2,) + k1.shape, BF16),
            pltpu.VMEM((chans * (blocks + PAD), seg), F32),
            pltpu.VMEM((tables, 4, seg), F32),
            pltpu.VMEM(((devices + 1) * META, seg), F32),
            pltpu.SMEM((devices,), jnp.int32),
            pltpu.SemaphoreType.DMA((4,)),
            pltpu.SemaphoreType.DMA((4,)),
            pltpu.SemaphoreType.DMA((8,)),
            pltpu.SemaphoreType.DMA((2,)),
            pltpu.SemaphoreType.DMA,
        ],
        compiler_params=params(),
    )(
        *(in_hbm(route.T) for route in (dest_dev, dest_pos, fwd_id, back_id)),
        *(in_hbm(x) for x in (ll_blocks, fwd_table, k1, k2)),
    )


def sum_kernel(
    got_ref,
    sum0_ref,
    sum1_ref,
    up_ref,
    down_ref,
    side_ref,
    pos_ref,
    rows_ref,
    spot_ref,
    spot_sem,
):
    devices, _, cols = got_ref.shape
    hblocks, chans, _ = sum0_ref.shape
    hblocks -= 1
    pairs = hblocks // 2
    lanes = 2 * chans
    rows_ref[...] = got_ref[:, CAP * chans :, :].reshape(devices * META, lanes).astype(F32)

    def meta_row(n):
        return rows_ref[pl.ds(n, devices, stride=META), :]

    lane = lane_iota((devices, lanes))
    table = jnp.where(lane % 2 == 0, meta_row(4), meta_row(5))
    beside = [meta_row(6), meta_row(7)]
    for side in range(2):
        turned_half = pltpu.roll(beside[side], chans, axis=1)
        for rank in range(CAP):
            here = lane == 2 + 2 * side + rank
            table = jnp.where(here, beside[side] if rank == 0 else turned_half, table)
    spots = table.T[0:8, :].astype(jnp.int32) - 1
    pos_ref[...] = spots
    spot_copy = pltpu.make_async_copy(pos_ref, spot_ref, spot_sem)
    spot_copy.start()

    def clear(r, carry):
        for rank in range(CAP):
            (sum0_ref, sum1_ref)[rank][r] = jnp.zeros((chans, cols), F32)
        return carry

    lax.fori_loop(0, hblocks, clear, 0, unroll=4)
    block = lax.broadcasted_iota(jnp.int32, (pairs, devices), 0)
    low = lane_iota((pairs, lanes)) < chans
    for side in range(2):
        sums = []
        for parity in range(2):
            total = jnp.zeros((pairs, lanes), F32)
            for rank in range(CAP):
                n = 2 + 2 * side + rank
                hit = (spots[n : n + 1, :] == 2 * block + parity).astype(F32).astype(BF16)
                total += jnp.dot(
                    hit, meta_row(2 * side + rank).astype(BF16), preferred_element_type=F32
                )
            sums.append(total)
        even, odd = sums
        side_ref[2 * side] = jnp.where(low, even, pltpu.roll(odd, chans, axis=1))
        side_ref[2 * side + 1] = jnp.where(low, pltpu.roll(even, chans, axis=1), odd)
    spot_copy.wait()

    def add(d, carry):
        rows, sums = [], []
        for rank, sum_ref in enumerate((sum0_ref, sum1_ref)):
            pos = spot_ref[rank, d]
            rows.append(jnp.where(pos < 0, hblocks, pos))
            block = got_ref[d, rank * chans : (rank + 1) * chans, :]
            sums.append(sum_ref[rows[-1]] + block.astype(F32))
        sum0_ref[rows[0]] = sums[0]
        sum1_ref[rows[1]] = sums[1]
        return carry

    lax.fori_loop(0, devices, add, 0, unroll=16)

    def total_of(r):
        return sum0_ref[r] + sum1_ref[r]

    corners = jnp.zeros((up_ref.shape[0] - cols, lanes), F32)
    corner_row = lax.broadcasted_iota(jnp.int32, corners.shape, 0)
    for ref, g in ((up_ref, 0), (down_ref, pairs - 1)):
        ref[0:cols, :] = jnp.concatenate([total_of(2 * g), total_of(2 * g + 1)], axis=0).T.astype(BF16)
        rest = corners
        for n in range(4):
            rest = jnp.where(corner_row == n, side_ref[n, g : g + 1, :], rest)
        ref[cols:, :] = rest.astype(BF16)


def sum_field(got, hblocks):
    devices, depth, cols = got.shape
    chans = (depth - META) // CAP
    pairs = hblocks // 2
    message = jax.ShapeDtypeStruct((cols + 16, 2 * chans), BF16)
    sums = jax.ShapeDtypeStruct((hblocks + 1, chans, cols), F32)
    return pl.pallas_call(
        sum_kernel,
        out_shape=(
            sums,
            sums,
            message,
            message,
            jax.ShapeDtypeStruct((4, pairs, 2 * chans), F32),
            jax.ShapeDtypeStruct((8, devices), jnp.int32),
        ),
        in_specs=[vmem()],
        out_specs=(vmem(),) * 6,
        scratch_shapes=[
            pltpu.VMEM((devices * META, cols), F32),
            pltpu.SMEM((8, devices), jnp.int32),
            pltpu.SemaphoreType.DMA,
        ],
        compiler_params=params(),
    )(got)


def gelu(x):
    return 0.5 * x * (1.0 + jnp.tanh(0.7978845608028654 * (x + 0.044715 * (x * x * x))))


def taps(x, weights_ref, d):
    lanes = x.shape[1] // 2
    return jnp.dot(x, weights_ref[:, d * lanes : (d + 1) * lanes], preferred_element_type=F32)


def row_pair_conv(upper, lower, weights_ref, bias, before, after):
    cols, lanes = upper.shape
    rows = jnp.concatenate([upper, lower], axis=1)
    product = jnp.dot(rows, weights_ref[...], preferred_element_type=F32)
    ahead = pltpu.roll(product[:, 0:lanes], 1, axis=0)
    behind = pltpu.roll(product[:, 2 * lanes :], cols - 1, axis=0)
    edge = lax.broadcasted_iota(jnp.int32, (8, lanes), 0)
    first = jnp.where(edge == 0, before, ahead[0:8, :])
    last = jnp.where(edge == 7, after, behind[cols - 8 :, :])
    ahead = jnp.concatenate([first, ahead[8:, :]], axis=0)
    behind = jnp.concatenate([behind[: cols - 8, :], last], axis=0)
    return product[:, lanes : 2 * lanes] + ahead + behind + bias


def twice(bias_ref):
    return jnp.concatenate([bias_ref[...], bias_ref[...]], axis=1)


def column_ends(block):
    cols = block.shape[0]
    return (
        block[0:16, :].astype(F32)[0:1, :],
        block[cols - 16 : cols, :].astype(F32)[15:16, :],
    )


def side_columns(columns, weights_ref, bias, place_ref):
    c = columns
    left = taps(c[1], weights_ref, 0)
    right = taps(c[4], weights_ref, 2)
    before = taps(c[0], weights_ref, 0) + taps(c[1], weights_ref, 1) + taps(c[2], weights_ref, 2)
    after = taps(c[3], weights_ref, 0) + taps(c[4], weights_ref, 1) + taps(c[5], weights_ref, 2)
    before = jnp.where(place_ref[0:1, :] > 0, gelu(before + bias), 0.0)
    after = jnp.where(place_ref[1:2, :] > 0, gelu(after + bias), 0.0)
    return left, right, before, after


def put_state(state_ref, g, out, field):
    _, chans, cols = state_ref.shape
    state = out + field.astype(F32)
    state_ref[pl.ds(2 * g, 2)] = state.T.astype(BF16).reshape(2, chans, cols)


def inner_kernel(
    sum0_ref,
    sum1_ref,
    side_ref,
    place_ref,
    k1_ref,
    b1_ref,
    k2_ref,
    b2_ref,
    ends_ref,
    hids_ref,
    cols_ref,
    state_ref,
    turned_ref,
    hid_ref,
    column_ref,
    halo_ref,
):
    hblocks, chans, cols = state_ref.shape
    pairs = hblocks // 2

    def turn(g, carry):
        both = (sum0_ref[pl.ds(2 * g, 2)] + sum1_ref[pl.ds(2 * g, 2)]).astype(BF16)
        turned_ref[g] = both.reshape(2 * chans, cols).T
        return carry

    lax.fori_loop(0, pairs, turn, 0, unroll=True)
    for n, k in enumerate((0, 1, 4, 5)):
        column_ref[k, 0:pairs, :] = side_ref[n]

    def inner_side(g, carry):
        for k, end in enumerate(column_ends(turned_ref[g])):
            column_ref[2 + k, pl.ds(g, 1), :] = end
        return carry

    lax.fori_loop(0, pairs, inner_side, 0, unroll=4)
    b1 = twice(b1_ref)
    b2 = twice(b2_ref)
    columns = [
        jnp.concatenate([column_ref[k, 0 : pairs - 1, :], column_ref[k, 1:pairs, :]], axis=1).astype(
            BF16
        )
        for k in range(6)
    ]
    left, right, before, after = side_columns(columns, k1_ref, b1, place_ref)
    halo_ref[0, 1:pairs, :] = left
    halo_ref[1, 1:pairs, :] = right
    cols_ref[...] = jnp.zeros_like(cols_ref)
    for n, (column, d) in enumerate(((before, 0), (after, 2))):
        cols_ref[n : n + 1, :] = column[0:1, :]
        cols_ref[2 + n : 3 + n, :] = column[pairs - 2 : pairs - 1, :]
        column_ref[n, 1:pairs, :] = column
        both = jnp.concatenate(
            [column_ref[n, 1 : pairs - 1, :], column_ref[n, 2:pairs, :]], axis=1
        )
        halo_ref[2 + n, 1 : pairs - 1, :] = taps(both.astype(BF16), k2_ref, d)

    def halos(h, g):
        return halo_ref[h, pl.ds(g, 1), :], halo_ref[h + 1, pl.ds(g, 1), :]

    def first(g, carry):
        out = row_pair_conv(turned_ref[g - 1], turned_ref[g], k1_ref, b1, *halos(0, g))
        hid_ref[g] = gelu(out).astype(BF16)
        return carry

    lax.fori_loop(1, pairs, first, 0, unroll=True)

    def second(g, carry):
        out = row_pair_conv(hid_ref[g], hid_ref[g + 1], k2_ref, b2, *halos(2, g))
        put_state(state_ref, g, out, turned_ref[g])
        return carry

    lax.fori_loop(1, pairs - 1, second, 0, unroll=True)
    for n, g in enumerate((0, pairs - 1)):
        ends_ref[n] = turned_ref[g]
    for n, g in enumerate((1, pairs - 1)):
        hids_ref[n] = hid_ref[g]


def inner_state(sum0, sum1, sides, place, k1, b1, k2, b2):
    hblocks, chans, cols = sum0.shape
    hblocks -= 1
    pairs = hblocks // 2
    lanes = 2 * chans
    two = jax.ShapeDtypeStruct((2, cols, lanes), BF16)
    return pl.pallas_call(
        inner_kernel,
        out_shape=(
            two,
            two,
            jax.ShapeDtypeStruct((8, lanes), F32),
            jax.ShapeDtypeStruct((hblocks, chans, cols), BF16),
        ),
        in_specs=[vmem()] * 8,
        out_specs=(vmem(),) * 4,
        scratch_shapes=[
            pltpu.VMEM((pairs, cols, lanes), BF16),
            pltpu.VMEM((pairs, cols, lanes), BF16),
            pltpu.VMEM((6, pairs + 8, lanes), F32),
            pltpu.VMEM((4, pairs + 8, lanes), F32),
        ],
        compiler_params=params(),
        cost_estimate=pl.CostEstimate(
            flops=4 * 8192 * 9 * 64 * 64, bytes_accessed=4 << 20, transcendentals=1 << 19
        ),
    )(sum0, sum1, sides, place, k1, b1, k2, b2)


def outer_kernel(
    pos_hbm,
    place_ref,
    ends_ref,
    hids_ref,
    cols_ref,
    inner_ref,
    sides_ref,
    below_ref,
    above_ref,
    k1_ref,
    b1_ref,
    k2_ref,
    b2_ref,
    send_ref,
    column_ref,
    state_ref,
    pos_ref,
    pos_sem,
):
    pos_copy = pltpu.make_async_copy(pos_hbm, pos_ref, pos_sem)
    pos_copy.start()
    hblocks, chans, cols = inner_ref.shape
    pairs = hblocks // 2
    devices = pos_ref.shape[1]
    state_ref[pl.ds(2, hblocks - 4)] = inner_ref[pl.ds(2, hblocks - 4)]
    column_ref[...] = jnp.zeros_like(column_ref)
    above = above_ref[cols:, :].astype(F32)
    below = below_ref[cols:, :].astype(F32)
    for n, k in enumerate((0, 1, 4, 5)):
        column_ref[k, 0, 0:1, :] = above[n : n + 1, :]
        column_ref[k, 0, 1:2, :] = sides_ref[n, pairs - 1 : pairs, :]
        column_ref[k, 1, 0:1, :] = sides_ref[n, 0:1, :]
        column_ref[k, 1, 1:2, :] = below[n : n + 1, :]
    for part, row, block in (
        (0, 0, above_ref[0:cols, :]),
        (0, 1, ends_ref[1]),
        (1, 0, ends_ref[0]),
        (1, 1, below_ref[0:cols, :]),
    ):
        for k, end in enumerate(column_ends(block)):
            column_ref[2 + k, part, row : row + 1, :] = end
    b1 = twice(b1_ref)
    b2 = twice(b2_ref)
    columns = [
        jnp.concatenate([column_ref[k, 0], column_ref[k, 1]], axis=1).astype(BF16) for k in range(6)
    ]
    left, right, before, after = side_columns(columns, k1_ref, b1, place_ref)
    top = lax.broadcasted_iota(jnp.int32, before.shape, 0) == 0
    halos = []
    for n, (column, d) in enumerate(((before, 0), (after, 2))):
        upper = jnp.where(top, column, cols_ref[2 + n : 3 + n, :])
        lower = jnp.where(top, cols_ref[n : n + 1, :], column)
        both = jnp.concatenate([upper, lower], axis=1).astype(BF16)
        halos.append(taps(both, k2_ref, d))

    def hidden(upper, lower, row):
        sides = left[row : row + 1, :], right[row : row + 1, :]
        return gelu(row_pair_conv(upper, lower, k1_ref, b1, *sides)).astype(BF16)

    def second(g, upper, lower, row):
        sides = (halo[row : row + 1, :] for halo in halos)
        out = row_pair_conv(upper, lower, k2_ref, b2, *sides)
        put_state(state_ref, g, out, ends_ref[row])

    second(0, hidden(above_ref[0:cols, :], ends_ref[0], 0), hids_ref[0], 0)
    second(pairs - 1, hids_ref[1], hidden(ends_ref[1], below_ref[0:cols, :], 1), 1)
    pos_copy.wait()

    def pick(d, carry):
        for rank in range(CAP):
            pos = jnp.maximum(pos_ref[rank, d], 0)
            send_ref[d, rank * chans : (rank + 1) * chans, :] = state_ref[pos]
        return carry

    lax.fori_loop(0, devices, pick, 0, unroll=16)


def outer_state(positions, place, ends, hids, columns, inner, sides, below, above, k1, b1, k2, b2):
    hblocks, chans, cols = inner.shape
    devices = positions.shape[1]
    return pl.pallas_call(
        outer_kernel,
        out_shape=jax.ShapeDtypeStruct((devices, CAP * chans, cols), BF16),
        in_specs=[vmem()] * 13,
        out_specs=vmem(),
        scratch_shapes=[
            pltpu.VMEM((6, 2, 8, 2 * chans), F32),
            pltpu.VMEM((hblocks, chans, cols), BF16),
            pltpu.SMEM(positions.shape, jnp.int32),
            pltpu.SemaphoreType.DMA,
        ],
        compiler_params=params(),
    )(positions, place, ends, hids, columns, inner, sides, below, above, k1, b1, k2, b2)


def backward_kernel(
    return_hbm,
    got_ref,
    table_ref,
    out_hbm,
    return_ref,
    rows_ref,
    out_ref,
    return_sem,
    out_sem,
):
    blocks, width = out_hbm.shape
    tables, seg, _ = table_ref.shape
    chans = width // seg
    parts = out_sem.shape[0]
    part = blocks // parts
    return_copy = pltpu.make_async_copy(return_hbm, return_ref, return_sem)
    return_copy.start()
    return_copy.wait()
    step = rows_ref.shape[1] // chans
    out_copies = []

    def finish(q):
        piece = pl.ds(q * part, part)
        for c in range(chans):
            out_ref[piece, c * seg : (c + 1) * seg] = rows_ref[
                q, c * step : c * step + part, :
            ].astype(BF16)
        out_copies.append(
            pltpu.make_async_copy(out_ref.at[piece], out_hbm.at[piece], out_sem.at[q])
        )
        out_copies[-1].start()

    for q in range(parts):
        if q > 0:
            finish(q - 1)
        for n in range(part):
            states, weights = [], []
            for t in range(2):
                code = return_ref[t, q * part + n]
                slot = code >> log2(tables)
                at = pl.multiple_of((slot & 1) * chans, chans)
                states.append(got_ref[slot >> 1, pl.ds(at, chans), :])
                weights.append(table_ref[code & (tables - 1)])
            rows_ref[q, pl.ds(n, chans, stride=step), :] = lax.dot_general(
                jnp.concatenate(states, axis=1),
                jnp.concatenate(weights, axis=1),
                NT,
                preferred_element_type=F32,
            )
    finish(parts - 1)
    for copy in out_copies:
        copy.wait()


def backward_remap(returns, got, back_table):
    blocks = returns.shape[1]
    chans = got.shape[1] // CAP
    seg = got.shape[2]
    parts = 4
    return pl.pallas_call(
        backward_kernel,
        out_shape=jax.ShapeDtypeStruct((blocks, chans * seg), BF16),
        in_specs=[hbm(), vmem(), vmem()],
        out_specs=hbm(),
        scratch_shapes=[
            pltpu.SMEM(returns.shape, jnp.int32),
            pltpu.VMEM((parts, chans * (blocks // parts + PAD), seg), F32),
            pltpu.VMEM((blocks, chans * seg), BF16),
            pltpu.SemaphoreType.DMA,
            pltpu.SemaphoreType.DMA((parts,)),
        ],
        compiler_params=params(),
    )(returns, got, back_table)


def exchange(buffer):
    return lax.all_to_all(buffer, AXES, split_axis=0, concat_axis=0, tiled=True)


def local(
    ll_blocks,
    dest_dev,
    dest_pos,
    fwd_id,
    back_id,
    fwd_table,
    back_table,
    kernel_one,
    bias_one,
    kernel_two,
    bias_two,
):
    n_fx = lax.axis_size("fx")
    n_fy = lax.axis_size("fy")
    hblocks = 64
    j = lax.axis_index("fy")
    place = jnp.stack([j > 0, j < n_fy - 1]).astype(jnp.int32)[:, None]
    place = jnp.broadcast_to(place, (2, 128))
    send, returns, w1, w2 = forward_remap(
        dest_dev,
        dest_pos,
        fwd_id,
        back_id,
        ll_blocks,
        fwd_table,
        kernel_one,
        kernel_two,
        n_fx * n_fy,
        n_fy,
    )
    send, place = lax.optimization_barrier((send, place))
    b1, b2 = bias_one[None], bias_two[None]
    sum0, sum1, up, down, sides, positions = sum_field(exchange(send), hblocks)
    below = lax.ppermute(up, "fx", [((i + 1) % n_fx, i) for i in range(n_fx)])
    above = lax.ppermute(down, "fx", [(i, (i + 1) % n_fx) for i in range(n_fx)])
    ends, hids, columns, inner = inner_state(sum0, sum1, sides, place, w1, b1, w2, b2)
    send_back = outer_state(
        positions, place, ends, hids, columns, inner, sides, below, above, w1, b1, w2, b2
    )
    return backward_remap(returns, exchange(send_back), back_table)


def solution(mesh):
    blocked = P(AXES, None)
    in_specs = (blocked,) * 5 + (P(),) * 6
    return jax.shard_map(
        local, mesh=mesh, in_specs=in_specs, out_specs=P(AXES, None), check_vma=False
    )
```

```python
import functools

import jax
import jax.numpy as jnp
from jax import lax
from jax.experimental import pallas as pl
from jax.experimental.pallas import tpu as pltpu
from jax.sharding import PartitionSpec as P

CAP = 2
PAD = 24
META = 8
AXES = ("fx", "fy")
F32 = jnp.float32
BF16 = jnp.bfloat16
VMEM_LIMIT = 40 * 1024 * 1024
NT = (((1,), (1,)), ((), ()))


def smem():
    return pl.BlockSpec(memory_space=pltpu.SMEM)


def vmem():
    return pl.BlockSpec(memory_space=pltpu.VMEM)


def hbm():
    return pl.BlockSpec(memory_space=pl.ANY)


def params():
    return pltpu.CompilerParams(vmem_limit_bytes=VMEM_LIMIT)


def in_hbm(x):
    return pltpu.with_memory_space_constraint(x, pltpu.HBM)


def log2(count):
    assert count & (count - 1) == 0
    return count.bit_length() - 1


def lane_iota(shape):
    return lax.broadcasted_iota(jnp.int32, shape, len(shape) - 1)


def row_pair_weights(taps_ref, weights_ref):
    _, columns, chans, _ = taps_ref.shape
    none = jnp.zeros((chans, chans), BF16)
    for q in range(4):
        for d in range(columns):
            upper = taps_ref[q, d] if q < 3 else none
            lower = taps_ref[q - 1, d] if q > 0 else none
            weights_ref[q * chans : (q + 1) * chans, 2 * d * chans : 2 * (d + 1) * chans] = (
                jnp.concatenate([upper, lower], axis=1)
            )


def forward_kernel(
    n_fy,
    dev_hbm,
    pos_hbm,
    fwd_hbm,
    back_hbm,
    x_hbm,
    table_hbm,
    k1_hbm,
    k2_hbm,
    send_ref,
    return_hbm,
    w1_ref,
    w2_ref,
    dev_ref,
    pos_ref,
    fwd_ref,
    back_ref,
    return_ref,
    x_ref,
    table_ref,
    taps_ref,
    rows_ref,
    edge_ref,
    meta_ref,
    count_ref,
    code_sem,
    x_sem,
    table_sem,
    taps_sem,
    return_sem,
):
    blocks, width = x_ref.shape
    tables, seg, _ = table_ref.shape
    chans = width // seg
    devices = count_ref.shape[0]
    assert n_fy == 1 << log2(n_fy)
    parts = x_sem.shape[0]
    wide = width // parts
    step = rows_ref.shape[0] // chans
    pieces = table_sem.shape[0]
    deep = tables // pieces
    x_copies = [
        pltpu.make_async_copy(
            x_hbm.at[:, pl.ds(q * wide, wide)], x_ref.at[:, pl.ds(q * wide, wide)], x_sem.at[q]
        )
        for q in range(parts)
    ]
    table_copies = [
        pltpu.make_async_copy(
            table_hbm.at[pl.ds(q * deep, deep)], table_ref.at[pl.ds(q * deep, deep)], table_sem.at[q]
        )
        for q in range(pieces)
    ]
    code_copies = [
        pltpu.make_async_copy(source, target, code_sem.at[n])
        for n, (source, target) in enumerate(
            ((dev_hbm, dev_ref), (pos_hbm, pos_ref), (fwd_hbm, fwd_ref), (back_hbm, back_ref))
        )
    ]
    taps_copies = [
        pltpu.make_async_copy(source, taps_ref.at[n], taps_sem.at[n])
        for n, source in enumerate((k1_hbm, k2_hbm))
    ]
    for copy in code_copies + x_copies + taps_copies + table_copies:
        copy.start()

    def clear(d, carry):
        count_ref[d] = 0
        return carry

    lax.fori_loop(0, devices, clear, 0, unroll=8)
    meta_ref[...] = jnp.zeros_like(meta_ref)
    for copy in code_copies:
        copy.wait()

    def plan(b, carry):
        for t in range(2):
            dev = dev_ref[t, b]
            rank = count_ref[dev]
            count_ref[dev] = rank + 1
            return_ref[t, b] = ((dev * CAP + rank) << log2(tables)) + back_ref[t, b]
            pos = (pos_ref[t, b] + 1).astype(F32)
            meta_ref[pl.ds(dev * META + 4 + rank, 1), :] = jnp.full((1, seg), pos, F32)
        return carry

    lax.fori_loop(0, blocks, plan, 0, unroll=8)
    return_copy = pltpu.make_async_copy(return_ref, return_hbm, return_sem)
    return_copy.start()
    both = jnp.where(
        lane_iota((devices, seg)) < chans,
        meta_ref[pl.ds(4, devices, stride=META), :],
        meta_ref[pl.ds(5, devices, stride=META), :],
    )
    col = lax.broadcasted_iota(jnp.int32, both.shape, 0) & (n_fy - 1)
    meta_ref[pl.ds(6, devices, stride=META), :] = jnp.where(
        col > 0, pltpu.roll(both, 1, axis=0), 0.0
    )
    meta_ref[pl.ds(7, devices, stride=META), :] = jnp.where(
        col < n_fy - 1, pltpu.roll(both, devices - 1, axis=0), 0.0
    )
    for q, copy in enumerate(x_copies):
        copy.wait()
        for c in range(q * wide // seg, (q + 1) * wide // seg):
            rows_ref[c * step : c * step + blocks, :] = x_ref[:, c * seg : (c + 1) * seg].astype(F32)
    for n, (copy, weights_ref) in enumerate(zip(taps_copies, (w1_ref, w2_ref))):
        copy.wait()
        row_pair_weights(taps_ref.at[n], weights_ref)
    for q, copy in enumerate(table_copies):
        copy.wait()

        def edges(n, carry):
            edge_ref[n, 0:2, :] = table_ref[n, seg - 16 : seg, :].astype(F32)[14:16, :]
            edge_ref[n, 2:4, :] = table_ref[n, 0:16, :].astype(F32)[0:2, :]
            return carry

        lax.fori_loop(q * deep, (q + 1) * deep, edges, 0, unroll=4)
    lane = lane_iota((1, seg))

    def one_block(b, carry):
        tables_of = [fwd_ref[t, b] for t in range(2)]
        x = rows_ref[pl.ds(b, chans, stride=step), :].astype(BF16)
        weights = jnp.concatenate([table_ref[n] for n in tables_of], axis=0)
        product = lax.dot_general(x, weights, NT, preferred_element_type=F32)
        tips = jnp.concatenate([edge_ref[n] for n in tables_of], axis=0).astype(BF16)
        ends = lax.dot_general(tips, x, NT, preferred_element_type=F32)
        ends = jnp.concatenate([ends, ends], axis=1)
        for t in range(2):
            slot = return_ref[t, b] >> log2(tables)
            dev, rank = slot >> 1, slot & 1
            at = pl.multiple_of(rank * chans, chans)
            send_ref[dev, pl.ds(at, chans), :] = product[:, t * seg : (t + 1) * seg].astype(BF16)
            col = dev & (n_fy - 1)
            for side in range(2):
                inside = (col < n_fy - 1) if side == 0 else (col > 0)
                near = jnp.where(inside, dev + 1 - 2 * side, devices)
                first = t * 4 + side * 2
                meta_ref[pl.ds(near * META + 2 * side + rank, 1), :] = jnp.where(
                    lane < chans, ends[first : first + 1, :], ends[first + 1 : first + 2, :]
                )
        return carry

    lax.fori_loop(0, blocks, one_block, 0, unroll=True)
    send_ref[:, CAP * chans :, :] = (
        meta_ref[0 : devices * META, :].astype(BF16).reshape(devices, META, seg)
    )
    return_copy.wait()


def forward_remap(
    dest_dev, dest_pos, fwd_id, back_id, ll_blocks, fwd_table, k1, k2, devices, n_fy
):
    blocks, width = ll_blocks.shape
    tables, seg, _ = fwd_table.shape
    chans = width // seg
    return pl.pallas_call(
        functools.partial(forward_kernel, n_fy),
        out_shape=(
            jax.ShapeDtypeStruct((devices, CAP * chans + META, seg), BF16),
            jax.ShapeDtypeStruct((2, blocks), jnp.int32),
            jax.ShapeDtypeStruct((4 * chans, 6 * chans), BF16),
            jax.ShapeDtypeStruct((4 * chans, 6 * chans), BF16),
        ),
        in_specs=[hbm()] * 8,
        out_specs=(vmem(), hbm(), vmem(), vmem()),
        scratch_shapes=[
            pltpu.SMEM((2, blocks), jnp.int32),
            pltpu.SMEM((2, blocks), jnp.int32),
            pltpu.SMEM((2, blocks), jnp.int32),
            pltpu.SMEM((2, blocks), jnp.int32),
            pltpu.SMEM((2, blocks), jnp.int32),
            pltpu.VMEM((blocks, width), BF16),
            pltpu.VMEM((tables, seg, seg), BF16),
            pltpu.VMEM((2,) + k1.shape, BF16),
            pltpu.VMEM((chans * (blocks + PAD), seg), F32),
            pltpu.VMEM((tables, 4, seg), F32),
            pltpu.VMEM(((devices + 1) * META, seg), F32),
            pltpu.SMEM((devices,), jnp.int32),
            pltpu.SemaphoreType.DMA((4,)),
            pltpu.SemaphoreType.DMA((4,)),
            pltpu.SemaphoreType.DMA((8,)),
            pltpu.SemaphoreType.DMA((2,)),
            pltpu.SemaphoreType.DMA,
        ],
        compiler_params=params(),
    )(
        *(in_hbm(route.T) for route in (dest_dev, dest_pos, fwd_id, back_id)),
        *(in_hbm(x) for x in (ll_blocks, fwd_table, k1, k2)),
    )


def sum_kernel(
    got_ref,
    sum0_ref,
    sum1_ref,
    up_ref,
    down_ref,
    side_ref,
    pos_ref,
    rows_ref,
    spot_ref,
    spot_sem,
):
    devices, _, cols = got_ref.shape
    hblocks, chans, _ = sum0_ref.shape
    hblocks -= 1
    pairs = hblocks // 2
    lanes = 2 * chans
    rows_ref[...] = got_ref[:, CAP * chans :, :].reshape(devices * META, lanes).astype(F32)

    def meta_row(n):
        return rows_ref[pl.ds(n, devices, stride=META), :]

    lane = lane_iota((devices, lanes))
    table = jnp.where(lane % 2 == 0, meta_row(4), meta_row(5))
    beside = [meta_row(6), meta_row(7)]
    for side in range(2):
        turned_half = pltpu.roll(beside[side], chans, axis=1)
        for rank in range(CAP):
            here = lane == 2 + 2 * side + rank
            table = jnp.where(here, beside[side] if rank == 0 else turned_half, table)
    spots = table.T[0:8, :].astype(jnp.int32) - 1
    pos_ref[...] = spots
    spot_copy = pltpu.make_async_copy(pos_ref, spot_ref, spot_sem)
    spot_copy.start()

    def clear(r, carry):
        for rank in range(CAP):
            (sum0_ref, sum1_ref)[rank][r] = jnp.zeros((chans, cols), F32)
        return carry

    lax.fori_loop(0, hblocks, clear, 0, unroll=4)
    block = lax.broadcasted_iota(jnp.int32, (pairs, devices), 0)
    low = lane_iota((pairs, lanes)) < chans
    for side in range(2):
        sums = []
        for parity in range(2):
            total = jnp.zeros((pairs, lanes), F32)
            for rank in range(CAP):
                n = 2 + 2 * side + rank
                hit = (spots[n : n + 1, :] == 2 * block + parity).astype(F32).astype(BF16)
                total += jnp.dot(
                    hit, meta_row(2 * side + rank).astype(BF16), preferred_element_type=F32
                )
            sums.append(total)
        even, odd = sums
        side_ref[2 * side] = jnp.where(low, even, pltpu.roll(odd, chans, axis=1))
        side_ref[2 * side + 1] = jnp.where(low, pltpu.roll(even, chans, axis=1), odd)
    spot_copy.wait()

    def add(d, carry):
        rows, sums = [], []
        for rank, sum_ref in enumerate((sum0_ref, sum1_ref)):
            pos = spot_ref[rank, d]
            rows.append(jnp.where(pos < 0, hblocks, pos))
            block = got_ref[d, rank * chans : (rank + 1) * chans, :]
            sums.append(sum_ref[rows[-1]] + block.astype(F32))
        sum0_ref[rows[0]] = sums[0]
        sum1_ref[rows[1]] = sums[1]
        return carry

    lax.fori_loop(0, devices, add, 0, unroll=16)

    def total_of(r):
        return sum0_ref[r] + sum1_ref[r]

    corners = jnp.zeros((up_ref.shape[0] - cols, lanes), F32)
    corner_row = lax.broadcasted_iota(jnp.int32, corners.shape, 0)
    for ref, g in ((up_ref, 0), (down_ref, pairs - 1)):
        ref[0:cols, :] = jnp.concatenate([total_of(2 * g), total_of(2 * g + 1)], axis=0).T.astype(BF16)
        rest = corners
        for n in range(4):
            rest = jnp.where(corner_row == n, side_ref[n, g : g + 1, :], rest)
        ref[cols:, :] = rest.astype(BF16)


def sum_field(got, hblocks):
    devices, depth, cols = got.shape
    chans = (depth - META) // CAP
    pairs = hblocks // 2
    message = jax.ShapeDtypeStruct((cols + 16, 2 * chans), BF16)
    sums = jax.ShapeDtypeStruct((hblocks + 1, chans, cols), F32)
    return pl.pallas_call(
        sum_kernel,
        out_shape=(
            sums,
            sums,
            message,
            message,
            jax.ShapeDtypeStruct((4, pairs, 2 * chans), F32),
            jax.ShapeDtypeStruct((8, devices), jnp.int32),
        ),
        in_specs=[vmem()],
        out_specs=(vmem(),) * 6,
        scratch_shapes=[
            pltpu.VMEM((devices * META, cols), F32),
            pltpu.SMEM((8, devices), jnp.int32),
            pltpu.SemaphoreType.DMA,
        ],
        compiler_params=params(),
    )(got)


def gelu(x):
    return 0.5 * x * (1.0 + jnp.tanh(0.7978845608028654 * (x + 0.044715 * (x * x * x))))


def taps(x, weights_ref, d):
    lanes = x.shape[1] // 2
    return jnp.dot(x, weights_ref[:, d * lanes : (d + 1) * lanes], preferred_element_type=F32)


def row_pair_conv(upper, lower, weights_ref, bias, before, after):
    cols, lanes = upper.shape
    rows = jnp.concatenate([upper, lower], axis=1)
    product = jnp.dot(rows, weights_ref[...], preferred_element_type=F32)
    ahead = pltpu.roll(product[:, 0:lanes], 1, axis=0)
    behind = pltpu.roll(product[:, 2 * lanes :], cols - 1, axis=0)
    edge = lax.broadcasted_iota(jnp.int32, (8, lanes), 0)
    first = jnp.where(edge == 0, before, ahead[0:8, :])
    last = jnp.where(edge == 7, after, behind[cols - 8 :, :])
    ahead = jnp.concatenate([first, ahead[8:, :]], axis=0)
    behind = jnp.concatenate([behind[: cols - 8, :], last], axis=0)
    return product[:, lanes : 2 * lanes] + ahead + behind + bias


def twice(bias_ref):
    return jnp.concatenate([bias_ref[...], bias_ref[...]], axis=1)


def column_ends(block):
    cols = block.shape[0]
    return (
        block[0:16, :].astype(F32)[0:1, :],
        block[cols - 16 : cols, :].astype(F32)[15:16, :],
    )


def side_columns(columns, weights_ref, bias, place_ref):
    c = columns
    left = taps(c[1], weights_ref, 0)
    right = taps(c[4], weights_ref, 2)
    before = taps(c[0], weights_ref, 0) + taps(c[1], weights_ref, 1) + taps(c[2], weights_ref, 2)
    after = taps(c[3], weights_ref, 0) + taps(c[4], weights_ref, 1) + taps(c[5], weights_ref, 2)
    before = jnp.where(place_ref[0:1, :] > 0, gelu(before + bias), 0.0)
    after = jnp.where(place_ref[1:2, :] > 0, gelu(after + bias), 0.0)
    return left, right, before, after


def put_state(state_ref, g, out, field):
    _, chans, cols = state_ref.shape
    state = out + field.astype(F32)
    state_ref[pl.ds(2 * g, 2)] = state.T.astype(BF16).reshape(2, chans, cols)


def inner_kernel(
    sum0_ref,
    sum1_ref,
    side_ref,
    place_ref,
    k1_ref,
    b1_ref,
    k2_ref,
    b2_ref,
    ends_ref,
    hids_ref,
    cols_ref,
    state_ref,
    turned_ref,
    hid_ref,
    column_ref,
    halo_ref,
):
    hblocks, chans, cols = state_ref.shape
    pairs = hblocks // 2

    def turn(g, carry):
        both = (sum0_ref[pl.ds(2 * g, 2)] + sum1_ref[pl.ds(2 * g, 2)]).astype(BF16)
        turned_ref[g] = both.reshape(2 * chans, cols).T
        return carry

    lax.fori_loop(0, pairs, turn, 0, unroll=True)
    for n, k in enumerate((0, 1, 4, 5)):
        column_ref[k, 0:pairs, :] = side_ref[n]

    def inner_side(g, carry):
        for k, end in enumerate(column_ends(turned_ref[g])):
            column_ref[2 + k, pl.ds(g, 1), :] = end
        return carry

    lax.fori_loop(0, pairs, inner_side, 0, unroll=4)
    b1 = twice(b1_ref)
    b2 = twice(b2_ref)
    columns = [
        jnp.concatenate([column_ref[k, 0 : pairs - 1, :], column_ref[k, 1:pairs, :]], axis=1).astype(
            BF16
        )
        for k in range(6)
    ]
    left, right, before, after = side_columns(columns, k1_ref, b1, place_ref)
    halo_ref[0, 1:pairs, :] = left
    halo_ref[1, 1:pairs, :] = right
    cols_ref[...] = jnp.zeros_like(cols_ref)
    for n, (column, d) in enumerate(((before, 0), (after, 2))):
        cols_ref[n : n + 1, :] = column[0:1, :]
        cols_ref[2 + n : 3 + n, :] = column[pairs - 2 : pairs - 1, :]
        column_ref[n, 1:pairs, :] = column
        both = jnp.concatenate(
            [column_ref[n, 1 : pairs - 1, :], column_ref[n, 2:pairs, :]], axis=1
        )
        halo_ref[2 + n, 1 : pairs - 1, :] = taps(both.astype(BF16), k2_ref, d)

    def halos(h, g):
        return halo_ref[h, pl.ds(g, 1), :], halo_ref[h + 1, pl.ds(g, 1), :]

    def first(g, carry):
        out = row_pair_conv(turned_ref[g - 1], turned_ref[g], k1_ref, b1, *halos(0, g))
        hid_ref[g] = gelu(out).astype(BF16)
        return carry

    lax.fori_loop(1, pairs, first, 0, unroll=True)

    def second(g, carry):
        out = row_pair_conv(hid_ref[g], hid_ref[g + 1], k2_ref, b2, *halos(2, g))
        put_state(state_ref, g, out, turned_ref[g])
        return carry

    lax.fori_loop(1, pairs - 1, second, 0, unroll=True)
    for n, g in enumerate((0, pairs - 1)):
        ends_ref[n] = turned_ref[g]
    for n, g in enumerate((1, pairs - 1)):
        hids_ref[n] = hid_ref[g]


def inner_state(sum0, sum1, sides, place, k1, b1, k2, b2):
    hblocks, chans, cols = sum0.shape
    hblocks -= 1
    pairs = hblocks // 2
    lanes = 2 * chans
    two = jax.ShapeDtypeStruct((2, cols, lanes), BF16)
    return pl.pallas_call(
        inner_kernel,
        out_shape=(
            two,
            two,
            jax.ShapeDtypeStruct((8, lanes), F32),
            jax.ShapeDtypeStruct((hblocks, chans, cols), BF16),
        ),
        in_specs=[vmem()] * 8,
        out_specs=(vmem(),) * 4,
        scratch_shapes=[
            pltpu.VMEM((pairs, cols, lanes), BF16),
            pltpu.VMEM((pairs, cols, lanes), BF16),
            pltpu.VMEM((6, pairs + 8, lanes), F32),
            pltpu.VMEM((4, pairs + 8, lanes), F32),
        ],
        compiler_params=params(),
        cost_estimate=pl.CostEstimate(
            flops=4 * 8192 * 9 * 64 * 64, bytes_accessed=4 << 20, transcendentals=1 << 19
        ),
    )(sum0, sum1, sides, place, k1, b1, k2, b2)


def outer_kernel(
    pos_hbm,
    place_ref,
    ends_ref,
    hids_ref,
    cols_ref,
    inner_ref,
    sides_ref,
    below_ref,
    above_ref,
    k1_ref,
    b1_ref,
    k2_ref,
    b2_ref,
    send_ref,
    column_ref,
    state_ref,
    pos_ref,
    pos_sem,
):
    pos_copy = pltpu.make_async_copy(pos_hbm, pos_ref, pos_sem)
    pos_copy.start()
    hblocks, chans, cols = inner_ref.shape
    pairs = hblocks // 2
    devices = pos_ref.shape[1]
    state_ref[pl.ds(2, hblocks - 4)] = inner_ref[pl.ds(2, hblocks - 4)]
    column_ref[...] = jnp.zeros_like(column_ref)
    above = above_ref[cols:, :].astype(F32)
    below = below_ref[cols:, :].astype(F32)
    for n, k in enumerate((0, 1, 4, 5)):
        column_ref[k, 0, 0:1, :] = above[n : n + 1, :]
        column_ref[k, 0, 1:2, :] = sides_ref[n, pairs - 1 : pairs, :]
        column_ref[k, 1, 0:1, :] = sides_ref[n, 0:1, :]
        column_ref[k, 1, 1:2, :] = below[n : n + 1, :]
    for part, row, block in (
        (0, 0, above_ref[0:cols, :]),
        (0, 1, ends_ref[1]),
        (1, 0, ends_ref[0]),
        (1, 1, below_ref[0:cols, :]),
    ):
        for k, end in enumerate(column_ends(block)):
            column_ref[2 + k, part, row : row + 1, :] = end
    b1 = twice(b1_ref)
    b2 = twice(b2_ref)
    columns = [
        jnp.concatenate([column_ref[k, 0], column_ref[k, 1]], axis=1).astype(BF16) for k in range(6)
    ]
    left, right, before, after = side_columns(columns, k1_ref, b1, place_ref)
    top = lax.broadcasted_iota(jnp.int32, before.shape, 0) == 0
    halos = []
    for n, (column, d) in enumerate(((before, 0), (after, 2))):
        upper = jnp.where(top, column, cols_ref[2 + n : 3 + n, :])
        lower = jnp.where(top, cols_ref[n : n + 1, :], column)
        both = jnp.concatenate([upper, lower], axis=1).astype(BF16)
        halos.append(taps(both, k2_ref, d))

    def hidden(upper, lower, row):
        sides = left[row : row + 1, :], right[row : row + 1, :]
        return gelu(row_pair_conv(upper, lower, k1_ref, b1, *sides)).astype(BF16)

    def second(g, upper, lower, row):
        sides = (halo[row : row + 1, :] for halo in halos)
        out = row_pair_conv(upper, lower, k2_ref, b2, *sides)
        put_state(state_ref, g, out, ends_ref[row])

    second(0, hidden(above_ref[0:cols, :], ends_ref[0], 0), hids_ref[0], 0)
    second(pairs - 1, hids_ref[1], hidden(ends_ref[1], below_ref[0:cols, :], 1), 1)
    pos_copy.wait()

    def pick(d, carry):
        for rank in range(CAP):
            pos = jnp.maximum(pos_ref[rank, d], 0)
            send_ref[d, rank * chans : (rank + 1) * chans, :] = state_ref[pos]
        return carry

    lax.fori_loop(0, devices, pick, 0, unroll=16)


def outer_state(positions, place, ends, hids, columns, inner, sides, below, above, k1, b1, k2, b2):
    hblocks, chans, cols = inner.shape
    devices = positions.shape[1]
    return pl.pallas_call(
        outer_kernel,
        out_shape=jax.ShapeDtypeStruct((devices, CAP * chans, cols), BF16),
        in_specs=[vmem()] * 13,
        out_specs=vmem(),
        scratch_shapes=[
            pltpu.VMEM((6, 2, 8, 2 * chans), F32),
            pltpu.VMEM((hblocks, chans, cols), BF16),
            pltpu.SMEM(positions.shape, jnp.int32),
            pltpu.SemaphoreType.DMA,
        ],
        compiler_params=params(),
    )(positions, place, ends, hids, columns, inner, sides, below, above, k1, b1, k2, b2)


def backward_kernel(
    return_hbm,
    got_ref,
    table_ref,
    out_hbm,
    return_ref,
    rows_ref,
    out_ref,
    return_sem,
    out_sem,
):
    blocks, width = out_hbm.shape
    tables, seg, _ = table_ref.shape
    chans = width // seg
    parts = out_sem.shape[0]
    part = blocks // parts
    return_copy = pltpu.make_async_copy(return_hbm, return_ref, return_sem)
    return_copy.start()
    return_copy.wait()
    step = rows_ref.shape[1] // chans
    out_copies = []

    def finish(q):
        piece = pl.ds(q * part, part)
        for c in range(chans):
            out_ref[piece, c * seg : (c + 1) * seg] = rows_ref[
                q, c * step : c * step + part, :
            ].astype(BF16)
        out_copies.append(
            pltpu.make_async_copy(out_ref.at[piece], out_hbm.at[piece], out_sem.at[q])
        )
        out_copies[-1].start()

    for q in range(parts):
        if q > 0:
            finish(q - 1)
        for n in range(part):
            states, weights = [], []
            for t in range(2):
                code = return_ref[t, q * part + n]
                slot = code >> log2(tables)
                at = pl.multiple_of((slot & 1) * chans, chans)
                states.append(got_ref[slot >> 1, pl.ds(at, chans), :])
                weights.append(table_ref[code & (tables - 1)])
            rows_ref[q, pl.ds(n, chans, stride=step), :] = lax.dot_general(
                jnp.concatenate(states, axis=1),
                jnp.concatenate(weights, axis=1),
                NT,
                preferred_element_type=F32,
            )
    finish(parts - 1)
    for copy in out_copies:
        copy.wait()


def backward_remap(returns, got, back_table):
    blocks = returns.shape[1]
    chans = got.shape[1] // CAP
    seg = got.shape[2]
    parts = 4
    return pl.pallas_call(
        backward_kernel,
        out_shape=jax.ShapeDtypeStruct((blocks, chans * seg), BF16),
        in_specs=[hbm(), vmem(), vmem()],
        out_specs=hbm(),
        scratch_shapes=[
            pltpu.SMEM(returns.shape, jnp.int32),
            pltpu.VMEM((parts, chans * (blocks // parts + PAD), seg), F32),
            pltpu.VMEM((blocks, chans * seg), BF16),
            pltpu.SemaphoreType.DMA,
            pltpu.SemaphoreType.DMA((parts,)),
        ],
        compiler_params=params(),
    )(returns, got, back_table)


def exchange(buffer):
    return lax.all_to_all(buffer, AXES, split_axis=0, concat_axis=0, tiled=True)


def local(
    ll_blocks,
    dest_dev,
    dest_pos,
    fwd_id,
    back_id,
    fwd_table,
    back_table,
    kernel_one,
    bias_one,
    kernel_two,
    bias_two,
):
    n_fx = lax.axis_size("fx")
    n_fy = lax.axis_size("fy")
    hblocks = 64
    j = lax.axis_index("fy")
    place = jnp.stack([j > 0, j < n_fy - 1]).astype(jnp.int32)[:, None]
    place = jnp.broadcast_to(place, (2, 128))
    send, returns, w1, w2 = forward_remap(
        dest_dev,
        dest_pos,
        fwd_id,
        back_id,
        ll_blocks,
        fwd_table,
        kernel_one,
        kernel_two,
        n_fx * n_fy,
        n_fy,
    )
    send, place = lax.optimization_barrier((send, place))
    b1, b2 = bias_one[None], bias_two[None]
    sum0, sum1, up, down, sides, positions = sum_field(exchange(send), hblocks)
    below = lax.ppermute(up, "fx", [((i + 1) % n_fx, i) for i in range(n_fx)])
    above = lax.ppermute(down, "fx", [(i, (i + 1) % n_fx) for i in range(n_fx)])
    ends, hids, columns, inner = inner_state(sum0, sum1, sides, place, w1, b1, w2, b2)
    send_back = outer_state(
        positions, place, ends, hids, columns, inner, sides, below, above, w1, b1, w2, b2
    )
    return backward_remap(returns, exchange(send_back), back_table)


def solution(mesh):
    blocked = P(AXES, None)
    in_specs = (blocked,) * 5 + (P(),) * 6
    return jax.shard_map(
        local, mesh=mesh, in_specs=in_specs, out_specs=P(AXES, None), check_vma=False
    )
```
